32 devices in a mesh: dp: 16 (over z, x, core), tp: 2 (over y).
Axes of the slice: x: 2, y: 2, z: 4, core: 2. Of those that a mesh axis runs over, the one named last changes fastest.
Arguments:
- tokens: bfloat16 [32768, 768], P(('dp', 'tp')), may hold values from -6 to 6
- masked_positions: int32 [64, 256], P(('dp', 'tp')), may hold values from -1 to 511, as said below
- cotangent: bfloat16 [32768, 768], P(('dp', 'tp')), may hold values from -6 to 6
- query_weight: bfloat16 [768, 768], replicated, may hold values from -0.3125 to 0.3125
- query_bias: float32 [768], replicated, may hold values from -3 to 3
- key_weight: bfloat16 [768, 768], replicated, may hold values from -0.3125 to 0.3125
- value_weight: bfloat16 [768, 768], replicated, may hold values from -0.21875 to 0.21875
- value_bias: float32 [768], replicated, may hold values from -3 to 3
- output_weight: bfloat16 [768, 768], replicated, may hold values from -0.875 to 0.875
- output_bias: float32 [768], replicated, may hold values from -2 to 2
- first_gain: float32 [768], replicated, may hold values from 0.1 to 1.9
- first_shift: float32 [768], replicated, may hold values from -2 to 2
- up_weight: bfloat16 [768, 3072], P(None, 'tp'), may hold values from -0.21875 to 0.21875
- up_bias: float32 [3072], P('tp'), may hold values from -3 to 3
- down_weight: bfloat16 [3072, 768], P('tp'), may hold values from -0.109375 to 0.109375
- lowering_offset: float32 [768], replicated, may hold values from -2 to 2
- second_gain: float32 [768], replicated, may hold values from 0.1 to 1.9
- second_shift: float32 [768], replicated, may hold values from -2 to 2
- channel_filter_scores: bfloat16 [12, 512, 512], P('tp'), may hold values from -6 to 6
- mask_noise: bfloat16 [12, 512, 512], P('tp'), may hold values from -6 to 6
Outputs:
- layer_output: bfloat16 [32768, 768], P(('dp', 'tp'))
- tokens_grad: bfloat16 [32768, 768], P(('dp', 'tp'))
- query_weight_grad: float32 [768, 768], P(None, 'tp')
- query_bias_grad: float32 [768], P('tp')
- key_weight_grad: float32 [768, 768], P(None, 'tp')
- value_weight_grad: float32 [768, 768], P(None, 'tp')
- value_bias_grad: float32 [768], P('tp')
- output_weight_grad: float32 [768, 768], P(None, 'tp')
- output_bias_grad: float32 [768], P('tp')
- first_gain_grad: float32 [768], P('tp')
- first_shift_grad: float32 [768], P('tp')
- up_weight_grad: float32 [768, 3072], P(None, 'tp')
- up_bias_grad: float32 [3072], P('tp')
- down_weight_grad: float32 [3072, 768], P('tp')
- down_bias_grad: float32 [768], P('tp')
- second_gain_grad: float32 [768], P('tp')
- second_shift_grad: float32 [768], P('tp')
- mask_logits_grad: float32 [12, 512, 512], P('tp')
The draws below stay inside these ranges and needn't reach their ends.
Inputs may be any that keep to these rules, and one draw needn't show every extreme that they name: `masked_positions`: each row lists distinct positions of its sequence in its first slots and -1 in the rest; a row holds 1 to 256 positions, most rows few, and some row exactly 256.
All inputs are finite; a program needn't handle non-finite values.
Results may differ from the reference program's by a relative error of at most 0.017.
The reference program's roundings to bfloat16 on the way count: a program that leaves them out, or rounds other values in their place, can miss the bound.
Values may be sent and summed in bfloat16 or wider, within the bound.
No kernel may reach another device: no remote copies, remote signals or barrier semaphores. Data moves between devices by JAX's collectives and lax.ppermute only.
A program may use at most 320 MiB of HBM per device.

```python
import math
import jax
import jax.numpy as jnp
from jax import lax

D = 768
HEADS = 12
HEAD_DIM = 64
FF = 3072
L = 512
MAXP = 256
SEQS = 64
TOKENS = 32768


def draw_masked_positions(key, part):
    key = jax.random.fold_in(key, 11)
    key_one, key_two, key_three, key_four = jax.random.split(key, 4)
    first_draw = jax.random.randint(key_one, (SEQS,), 1, MAXP + 1)
    second_draw = jax.random.randint(key_two, (SEQS,), 1, MAXP + 1)
    counts = jnp.maximum(first_draw * second_draw // MAXP, 1)
    chosen = jax.random.randint(key_three, (), 0, SEQS)
    counts = jnp.where(jnp.arange(SEQS) == chosen, MAXP, counts)
    key_list = jax.random.split(key_four, SEQS)
    orders = jax.vmap(lambda single: jax.random.permutation(single, L))(key_list)[:, :MAXP]
    slot_index = jnp.arange(MAXP)[None, :]
    return jnp.where(slot_index < counts[:, None], orders, -1).astype(jnp.int32)


def level_of(own_key, dims, cuts, low, top_value):
    def one(axis_at, blocks):
        draws = jax.random.uniform(jax.random.fold_in(jax.random.fold_in(own_key, 6), axis_at), (blocks,), jnp.float32, low / len(cuts), top_value / len(cuts))
        return jnp.repeat(jnp.exp(draws), dims[axis_at] // blocks).reshape((-1,) + (1,) * (len(dims) - axis_at - 1))

    level = one(*cuts[0])
    for cut in cuts[1:]:
        level = level * one(*cut)
    return level


def scatter_about(own_key, extent, scale, limit, cuts=(), held_as=jnp.bfloat16):
    level = level_of(own_key, extent, cuts, -0.22, 0.18) if cuts else 1.0
    values = jax.random.normal(own_key, extent, jnp.float32) * scale * level
    return jnp.minimum(jnp.maximum(values, -limit), limit).astype(held_as)


def setup_inputs(seed: int = 0) -> dict:
    arg_keys = jax.random.split(jax.random.key(seed), 21)
    return {
        "tokens": scatter_about(arg_keys[0], (TOKENS, D), 1.0, 6.0, ((0, 32),)),
        "masked_positions": draw_masked_positions(jax.random.fold_in(arg_keys[20], 71), 0),
        "cotangent": scatter_about(arg_keys[2], (TOKENS, D), 1.0, 6.0, ((0, 32),)),
        "query_weight": scatter_about(arg_keys[3], (D, D), (D // 2) ** -0.5, 0.3125),
        "query_bias": scatter_about(arg_keys[4], (D,), 0.5, 3.0, (), jnp.float32),
        "key_weight": scatter_about(arg_keys[5], (D, D), (D // 2) ** -0.5, 0.3125),
        "value_weight": scatter_about(arg_keys[6], (D, D), D ** -0.5, 0.21875),
        "value_bias": scatter_about(arg_keys[7], (D,), 0.5, 3.0, (), jnp.float32),
        "output_weight": scatter_about(arg_keys[8], (D, D), (D // 16) ** -0.5, 0.875),
        "output_bias": scatter_about(arg_keys[9], (D,), 0.3, 2.0, (), jnp.float32),
        "first_gain": jnp.clip(1.0 + 0.18 * jax.random.normal(arg_keys[10], (D,), jnp.float32), 0.1, 1.9),
        "first_shift": scatter_about(arg_keys[11], (D,), 0.3, 2.0, (), jnp.float32),
        "up_weight": scatter_about(arg_keys[12], (D, FF), D ** -0.5, 0.21875, ((1, 2),)),
        "up_bias": scatter_about(arg_keys[13], (FF,), 0.5, 3.0, ((0, 2),), jnp.float32),
        "down_weight": scatter_about(arg_keys[14], (FF, D), FF ** -0.5, 0.109375, ((0, 2),)),
        "lowering_offset": scatter_about(arg_keys[15], (D,), 0.3, 2.0, (), jnp.float32),
        "second_gain": jnp.clip(1.0 + 0.18 * jax.random.normal(arg_keys[16], (D,), jnp.float32), 0.1, 1.9),
        "second_shift": scatter_about(arg_keys[17], (D,), 0.3, 2.0, (), jnp.float32),
        "channel_filter_scores": scatter_about(arg_keys[18], (HEADS, L, L), 1.5, 6.0, ((0, 2),)),
        "mask_noise": scatter_about(arg_keys[19], (HEADS, L, L), 1.0, 6.0, ((0, 2),)),
    }


relaxation_heat = 0.6
epsilon = 1e-06
highest = lax.Precision.HIGHEST

@jax.custom_vjp
def low(v):
    return lax.optimization_barrier(v.astype(jnp.bfloat16)).astype(jnp.float32)

@jax.custom_vjp
def low_back(v):
    return v

def low_keep(v):
    return (low(v), None)

def low_pass(kept, grad):
    return (grad,)

def back_keep(v):
    return (v, None)

def back_low(kept, grad):
    return (low(grad),)
low.defvjp(low_keep, low_pass)
low_back.defvjp(back_keep, back_low)

def matmul_high(left, right):
    return jnp.dot(left, right, precision=highest, preferred_element_type=jnp.float32)

def norm_rows(hidden, gain, shift):
    centre = hidden - lax.optimization_barrier(jnp.mean(hidden, -1, keepdims=True))
    spread = lax.optimization_barrier(jnp.mean(centre * centre, -1, keepdims=True))
    return centre * lax.rsqrt(spread + epsilon) * gain + shift

def focus_tile_routine(switch_levels, block):
    queries, key_rows, value_rows = block
    scores = low_back(jnp.einsum('qhd,khd->hqk', queries, key_rows, precision=highest) * HEAD_DIM ** (-0.5))
    peak = lax.optimization_barrier(jnp.max(scores, -1, keepdims=True))
    expo = jnp.exp(scores - peak)
    probs = expo / lax.optimization_barrier(jnp.sum(expo, -1, keepdims=True))
    weights = low(probs * switch_levels)
    return jnp.einsum('hqk,khd->qhd', weights, value_rows, precision=highest)

def layer_forward(inputs, params, extreme_perturbation):
    query_weight, query_bias, key_weight, value_weight, value_bias, output_weight, output_bias, first_gain, first_shift, up_weight, up_bias, down_weight, lowering_offset, second_gain, second_shift, channel_filter_scores = params
    groups = inputs.shape[0] // L
    switch_levels = jax.nn.sigmoid((channel_filter_scores + extreme_perturbation) / relaxation_heat)
    queries = low(low_back(matmul_high(inputs, query_weight) + query_bias)).reshape(groups, L, HEADS, HEAD_DIM)
    key_rows = low(low_back(matmul_high(inputs, key_weight))).reshape(groups, L, HEADS, HEAD_DIM)
    value_rows = low(low_back(matmul_high(inputs, value_weight) + value_bias)).reshape(groups, L, HEADS, HEAD_DIM)
    context = lax.map(jax.checkpoint(lambda block: focus_tile_routine(switch_levels, block)), (queries, key_rows, value_rows))
    context = low(low_back(context.reshape(groups * L, D)))
    attention = low_back(matmul_high(context, output_weight)) + output_bias
    first_out = norm_rows(inputs + attention, first_gain, first_shift)
    hidden = low_back(matmul_high(low(first_out), up_weight) + up_bias)
    active = low(jax.nn.gelu(hidden, approximate=False))
    forward = low_back(matmul_high(active, down_weight)) + lowering_offset
    return norm_rows(first_out + forward, second_gain, second_shift)

def reference(tokens, masked_positions, cotangent, query_weight, query_bias, key_weight, value_weight, value_bias, output_weight, output_bias, first_gain, first_shift, up_weight, up_bias, down_weight, lowering_offset, second_gain, second_shift, channel_filter_scores, mask_noise):
    params = tuple((member.astype(jnp.float32) for member in (query_weight, query_bias, key_weight, value_weight, value_bias, output_weight, output_bias, first_gain, first_shift, up_weight, up_bias, down_weight, lowering_offset, second_gain, second_shift, channel_filter_scores)))
    extreme_perturbation = mask_noise.astype(jnp.float32)
    group = math.gcd(SEQS, max(1, 4096 // L))
    block_count = SEQS // group
    token_blocks = tokens.reshape(block_count, group * L, D)
    pick_blocks = masked_positions.reshape(block_count, group, MAXP)
    cot_blocks = cotangent.reshape(block_count, group * L, D)
    positions = jnp.arange(L, dtype=jnp.int32)

    def step(totals, block):
        token_block, pick_block, cot_block = block
        inputs = token_block.astype(jnp.float32)
        result, pullback = jax.vjp(lambda left, right: layer_forward(left, right, extreme_perturbation), inputs, params)
        chosen = jnp.any(pick_block[:, :, None] == positions[None, None, :], axis=1).reshape(group * L)
        grad_result = cot_block.astype(jnp.float32) * chosen[:, None].astype(jnp.float32)
        grad_inputs, grad_params = pullback(grad_result)
        totals = jax.tree.map(jnp.add, totals, grad_params)
        return (totals, (result.astype(jnp.bfloat16), grad_inputs.astype(jnp.bfloat16)))
    totals, (outputs, input_grads) = lax.scan(step, jax.tree.map(jnp.zeros_like, params), (token_blocks, pick_blocks, cot_blocks))
    return (outputs.reshape(TOKENS, D), input_grads.reshape(TOKENS, D), totals[0], totals[1], totals[2], totals[3], totals[4], totals[5], totals[6], totals[7], totals[8], totals[9], totals[10], totals[11], totals[12], totals[13], totals[14], totals[15])
```

```python
import functools

import jax
import jax.numpy as jnp
from jax import lax
from jax.experimental import pallas as pl
from jax.experimental.pallas import tpu as pltpu
from jax.sharding import PartitionSpec as P

heat = 0.6
epsilon = 1e-06
low = jnp.bfloat16
full = jnp.float32
MIB = 1 << 20


def dot(left, right, left_dim=1, right_dim=0):
    return lax.dot_general(
        left, right, (((left_dim,), (right_dim,)), ((), ())), preferred_element_type=full
    )


def shape(dims, kind):
    return jax.ShapeDtypeStruct(dims, kind)


def params(mib=40):
    return pltpu.CompilerParams(vmem_limit_bytes=mib * MIB)


def cost(flops, moved, special=0):
    return pl.CostEstimate(flops=int(flops), bytes_accessed=int(moved), transcendentals=int(special))


def head_lanes(width):
    lane = lax.broadcasted_iota(jnp.int32, (1, width), 1)
    first = lane < width // 2
    return first, (first.astype(full).astype(low), (1.0 - first.astype(full)).astype(low))


def attend_kernel(place, q_ref, k_ref, v_ref, *rest):
    gates, (context_ref, logsum_ref) = rest[:4], rest[-2:]
    rows = gates[0].shape[1]
    first, lanes = head_lanes(q_ref.shape[1])
    keys, values = k_ref[...], v_ref[...]
    for r, gate_ref in enumerate(gates):
        start = pl.multiple_of((place[1] ^ r) * rows, rows)
        tile = pl.ds(start, rows)
        queries = q_ref[tile, :]
        mixed, logs = [], []
        for h in range(2):
            scores = dot(queries * lanes[h], keys, 1, 1)
            peak = jnp.max(scores, -1, keepdims=True)
            expo = jnp.exp(scores - peak)
            total = jnp.sum(expo, -1, keepdims=True)
            weights = (expo * gate_ref[h].astype(full)).astype(low)
            mixed.append(dot(weights, values) * (1.0 / total))
            logs.append(peak + jnp.log(total))
        context_ref[tile, :] = jnp.where(first, mixed[0], mixed[1]).astype(low)
        logsum_ref[tile, :] = jnp.where(first, logs[0], logs[1])


def attend(place, queries, keys, values, gates, own, earlier, length):
    rows, width = queries.shape
    pairs, part = gates[0].shape[0] // 2, length // 4
    lanes = 128
    seqs = rows // length
    column = pl.BlockSpec((length, lanes), lambda hp, s, place: (s, place[0] + hp))
    if own:
        gate_specs = [
            pl.BlockSpec((2, part, length), lambda hp, s, place, r=r: (hp, place[1] ^ r, 0))
            for r in range(4)
        ]
    else:
        gate_specs = [
            pl.BlockSpec((2, part, length), lambda hp, s, place: (hp, 0, 0)) for r in range(4)
        ]
    return pl.pallas_call(
        attend_kernel,
        grid_spec=pltpu.PrefetchScalarGridSpec(
            num_scalar_prefetch=1,
            grid=(pairs, seqs),
            in_specs=[column] * 3
            + gate_specs
            + [pl.BlockSpec(memory_space=pl.ANY)] * len(earlier),
            out_specs=[column, column],
        ),
        out_shape=[shape((rows, width), low), shape((rows, width), full)],
        input_output_aliases={8 + i: i for i in range(len(earlier))},
        compiler_params=params(),
        cost_estimate=cost(
            8 * seqs * pairs * length * length * lanes,
            rows * width * 5,
            2 * seqs * pairs * length * length,
        ),
        name="attend",
    )(place, queries, keys, values, *gates, *earlier)


def attend_back_kernel(place, scale, q_ref, k_ref, v_ref, d_ref, logsum_ref, *rest):
    gates = rest[:4]
    grads_ref, mask_ref, sums_ref, mask_acc, weights_all, slopes_all = rest[4:]
    s, hp = pl.program_id(0), pl.program_id(1)
    rows = gates[0].shape[1]
    width = q_ref.shape[1]
    group = grads_ref.shape[1] // 3
    first, lanes = head_lanes(width)
    keys, values = k_ref[...], v_ref[...]
    grad_q = grad_k = grad_v = None
    for h in range(2):
        for r, gate_ref in enumerate(gates):
            start = pl.multiple_of((place[1] ^ r) * rows, rows)
            tile = pl.ds(start, rows)
            scores = dot(q_ref[tile, :] * lanes[h], keys, 1, 1)
            probs = jnp.exp(scores - logsum_ref[tile, h * (width // 2) : h * (width // 2) + 1])
            grad_weights = dot(d_ref[tile, :] * lanes[h], values, 1, 1)
            gate = gate_ref[h].astype(full)
            part = grad_weights * probs
            place_of = (hp * 2 + h, tile)

            @pl.when(s == 0)
            def _():
                mask_acc[place_of] = part

            @pl.when(s > 0)
            def _():
                mask_acc[place_of] += part

            gated = part * gate
            slopes = gated - probs * jnp.sum(gated, -1, keepdims=True)
            weights_all[tile, :] = (probs * gate).astype(low)
            slopes_all[tile, :] = slopes.astype(low)
        weights, slopes = weights_all[...], slopes_all[...]
        new_v = dot(weights, d_ref[...] * lanes[h], 0, 0)
        new_q = dot(slopes, keys * lanes[h])
        new_k = dot(slopes, q_ref[...] * lanes[h], 0, 0)
        if h == 0:
            grad_q, grad_k, grad_v = new_q, new_k, new_v
        else:
            grad_q, grad_k, grad_v = grad_q + new_q, grad_k + new_k, grad_v + new_v
    grad_q = (grad_q * scale).astype(low)
    grad_k, grad_v = grad_k.astype(low), grad_v.astype(low)
    for n, grad in enumerate((grad_q, grad_k, grad_v)):
        at = pl.multiple_of(n * group + hp * width, width)
        grads_ref[:, pl.ds(at, width)] = grad
    at = pl.ds(pl.multiple_of(hp * width, width), width)
    column = jnp.concatenate(
        [
            jnp.sum(grad_q.astype(full), 0, keepdims=True),
            jnp.sum(grad_v.astype(full), 0, keepdims=True),
            jnp.zeros((6, width), full),
        ],
        0,
    )

    @pl.when(s == 0)
    def _():
        sums_ref[:, at] = column

    @pl.when(s > 0)
    def _():
        sums_ref[:, at] += column

    @pl.when(s == pl.num_programs(0) - 1)
    def _():
        for h in range(2):
            mask_ref[h] = mask_acc[hp * 2 + h].astype(low)


def attend_back(place, queries, keys, values, grad_context, logsum, gates, own, length, scale):
    rows, width = queries.shape
    heads, part = gates[0].shape[0], length // 4
    pairs, lanes, seqs = heads // 2, 128, rows // length
    column = pl.BlockSpec((length, lanes), lambda s, hp, place: (s, place[0] + hp))
    if own:
        gate_specs = [
            pl.BlockSpec((2, part, length), lambda s, hp, place, r=r: (hp, place[1] ^ r, 0))
            for r in range(4)
        ]
    else:
        gate_specs = [
            pl.BlockSpec((2, part, length), lambda s, hp, place: (hp, 0, 0)) for r in range(4)
        ]
    group = pairs * lanes

    def kernel(place, *refs):
        attend_back_kernel(place, scale, *refs)

    return pl.pallas_call(
        kernel,
        grid_spec=pltpu.PrefetchScalarGridSpec(
            num_scalar_prefetch=1,
            grid=(seqs, pairs),
            in_specs=[column] * 5 + gate_specs,
            out_specs=[
                pl.BlockSpec((length, 3 * group), lambda s, hp, place: (s, 0)),
                pl.BlockSpec(
                    (2, length, length),
                    lambda s, hp, place: (jnp.where(s == seqs - 1, hp, 0), 0, 0),
                ),
                pl.BlockSpec((8, group), lambda s, hp, place: (0, 0)),
            ],
            scratch_shapes=[
                pltpu.VMEM((heads, length, length), full),
                pltpu.VMEM((length, length), low),
                pltpu.VMEM((length, length), low),
            ],
        ),
        out_shape=[
            shape((rows, 3 * group), low),
            shape((heads, length, length), low),
            shape((8, group), full),
        ],
        compiler_params=params(),
        cost_estimate=cost(
            20 * seqs * pairs * length * length * lanes,
            rows * width * 12,
            2 * seqs * pairs * length * length,
        ),
        name="attend_back",
    )(place, queries, keys, values, grad_context, logsum, *gates)


def norm_forward(hidden, gain, shift):
    centre = hidden - jnp.mean(hidden, -1, keepdims=True)
    spread = jnp.mean(centre * centre, -1, keepdims=True)
    inverse = lax.rsqrt(spread + epsilon)
    normed = centre * inverse
    return normed * gain + shift, normed, inverse


def norm_backward(incoming, normed, inverse, gain):
    scaled = incoming * gain
    return inverse * (
        scaled
        - jnp.mean(scaled, -1, keepdims=True)
        - normed * jnp.mean(scaled * normed, -1, keepdims=True)
    )


def add_rows(ref, rows):
    packed = jnp.concatenate(
        [jnp.sum(row, 0, keepdims=True) for row in rows]
        + [jnp.zeros((8 - len(rows), ref.shape[1]), full)],
        0,
    )

    @pl.when(pl.program_id(0) == 0)
    def _():
        ref[...] = packed

    @pl.when(pl.program_id(0) > 0)
    def _():
        ref[...] += packed


def first_norm_kernel(
    slots_ref, context_ref, tokens_ref, weight_ref, bias_ref, gain_ref, shift_ref,
    order_ref, picked_ref, compact_ref, low_ref, normed_ref, inverse_ref,
):
    length, slots = tokens_ref.shape[0], slots_ref.shape[-1]
    position = lax.broadcasted_iota(jnp.int32, (length, slots), 0)
    hit = (position == slots_ref[0]).astype(full)
    chosen = jnp.max(hit, -1, keepdims=True)
    row = lax.broadcasted_iota(jnp.int32, (length, length), 0)
    column = lax.broadcasted_iota(jnp.int32, (length, length), 1)
    lower = (column <= row).astype(full).astype(low)
    upto = dot(lower, jnp.broadcast_to(chosen, (length, 128)).astype(low))[:, :1]
    count = jnp.sum(chosen, 0, keepdims=True)
    at = lax.broadcasted_iota(jnp.int32, (length, 1), 0).astype(full)
    target = jnp.where(chosen > 0, upto - 1.0, count + at - upto)
    order = (column.astype(full) == target).astype(full)
    picked_ref[...] = (order * chosen)[:, :slots].astype(low)
    order = order.astype(low)
    order_ref[...] = order
    context = dot(order, context_ref[...], 0, 0).astype(low)
    tokens = dot(order, tokens_ref[...], 0, 0)
    compact_ref[...] = context[:slots]
    attention = dot(context, weight_ref[...]) + bias_ref[...]
    out, normed, inverse = norm_forward(tokens + attention, gain_ref[...], shift_ref[...])
    low_ref[...] = out.astype(low)
    normed_ref[...] = normed
    inverse_ref[...] = jnp.broadcast_to(inverse[:slots], (slots, 128))


def first_norm(positions, context, tokens, weight, bias, gain, shift, length):
    rows, width = tokens.shape
    seqs, slots = positions.shape
    by_seq = lambda n, w: pl.BlockSpec((n, w), lambda s: (s, 0))
    whole = lambda a: pl.BlockSpec(a.shape, lambda s: (0,) * a.ndim)
    return pl.pallas_call(
        first_norm_kernel,
        grid=(seqs,),
        in_specs=[
            pl.BlockSpec((1, 1, slots), lambda s: (s, 0, 0)),
            by_seq(length, width),
            by_seq(length, width),
            whole(weight),
            whole(bias),
            whole(gain),
            whole(shift),
        ],
        out_specs=[
            by_seq(length, length),
            by_seq(length, slots),
            by_seq(slots, width),
            by_seq(length, width),
            by_seq(length, width),
            by_seq(slots, 128),
        ],
        out_shape=[
            shape((rows, length), low),
            shape((rows, slots), low),
            shape((seqs * slots, width), low),
            shape((rows, width), low),
            shape((rows, width), full),
            shape((seqs * slots, 128), full),
        ],
        compiler_params=params(),
        cost_estimate=cost(2 * rows * width * (width + 2 * length), rows * width * 12),
        name="first_norm",
    )(positions[:, None, :], context, tokens, weight, bias, gain, shift)


def gelu_parts(hidden):
    size = jnp.abs(hidden)
    t = 1.0 / (1.0 + (0.3275911 * 0.7071067811865476) * size)
    poly = 1.061405429 * t - 1.453152027
    poly = poly * t + 1.421413741
    poly = poly * t - 0.284496736
    poly = poly * t + 0.254829592
    bell = jnp.exp(hidden * hidden * -0.5)
    tail = 0.5 * poly * t * bell
    below = jnp.where(hidden > 0, 1.0 - tail, tail)
    return below, bell


def forward_kernel(place, x_ref, *refs, chained, per_seq):
    weights, refs = refs[:6], refs[6:]
    if chained:
        start_ref, refs = refs[0], refs[1:]
    total_ref, active_refs, slope_refs = refs[0], refs[1:3], refs[3:5]
    x = x_ref[...]
    step = 256

    def body(keep):
        total = start_ref[...] if chained else None
        for r in range(2):
            up, down, bias = weights[3 * r : 3 * r + 3]
            for c in range(0, up.shape[1], step):
                hidden = dot(x, up[:, c : c + step]) + bias[:, c : c + step]
                below, bell = gelu_parts(hidden)
                active = (hidden * below).astype(low)
                if keep:
                    active_refs[r][:, c : c + step] = active
                    slope_refs[r][:, c : c + step] = below + hidden * bell * 0.3989422804014327
                term = dot(active, down[c : c + step, :])
                total = term if total is None else total + term
        total_ref[...] = total

    i = pl.program_id(0)

    @pl.when(lax.rem(i, per_seq) == 0)
    def _():
        body(True)

    @pl.when(lax.rem(i, per_seq) != 0)
    def _():
        body(False)


def weight_specs(width, half, sliced):
    specs = []
    for r in range(2):
        if sliced:
            specs += [
                pl.BlockSpec((width, half), lambda i, place, r=r: (0, place[2] ^ r)),
                pl.BlockSpec((half, width), lambda i, place, r=r: (place[2] ^ r, 0)),
                pl.BlockSpec((1, half), lambda i, place, r=r: (0, place[2] ^ r)),
            ]
        else:
            specs += [
                pl.BlockSpec((width, half), lambda i, place: (0, 0)),
                pl.BlockSpec((half, width), lambda i, place: (0, 0)),
                pl.BlockSpec((1, half), lambda i, place: (0, 0)),
            ]
    return specs


def forward(place, x, pieces, sliced, start, length, slots):
    rows, width = x.shape
    half = pieces[0].shape[1] // (2 if sliced else 1)
    per_seq = length // slots
    kept = rows // per_seq
    block = pl.BlockSpec((slots, width), lambda i, place: (i, 0))
    kept_block = pl.BlockSpec((slots, half), lambda i, place: (i // per_seq, 0))
    extra = [] if start is None else [start]
    return pl.pallas_call(
        functools.partial(forward_kernel, chained=bool(extra), per_seq=per_seq),
        grid_spec=pltpu.PrefetchScalarGridSpec(
            num_scalar_prefetch=1,
            grid=(rows // slots,),
            in_specs=[block] + weight_specs(width, half, sliced) + [block] * len(extra),
            out_specs=[block] + [kept_block] * 4,
        ),
        out_shape=[shape((rows, width), full)]
        + [shape((kept, half), low)] * 2
        + [shape((kept, half), full)] * 2,
        compiler_params=params(),
        cost_estimate=cost(
            8 * rows * width * half, rows * width * 16 + half * width * 8, 4 * rows * half
        ),
        name="forward",
    )(place, x, *pieces, *extra)


def second_norm_kernel(
    total_ref, normed_ref, cotangent_ref, order_ref, picked_ref,
    offset_ref, gain1_ref, shift1_ref, gain2_ref, shift2_ref,
    out_ref, grad_ref, low_ref, sums_ref,
):
    slots = picked_ref.shape[1]
    first_out = normed_ref[...] * gain1_ref[...] + shift1_ref[...]
    gain = gain2_ref[...]
    out, normed, inverse = norm_forward(
        first_out + (total_ref[...] + offset_ref[...]), gain, shift2_ref[...]
    )
    out_ref[...] = dot(order_ref[...], out.astype(low)).astype(low)
    grad_out = dot(picked_ref[...], cotangent_ref[...], 0, 0)
    normed, inverse = normed[:slots], inverse[:slots]
    grad = norm_backward(grad_out, normed, inverse, gain)
    grad_ref[...] = grad
    low_ref[...] = grad.astype(low)
    add_rows(sums_ref, (grad_out * normed, grad_out, grad))


def second_norm(total, normed, cotangent, order, picked, offset, gain1, shift1, gain2, shift2):
    rows, width = total.shape
    length, slots = order.shape[1], picked.shape[1]
    seqs = rows // length
    by_seq = lambda n, w: pl.BlockSpec((n, w), lambda s: (s, 0))
    vector = pl.BlockSpec((1, width), lambda s: (0, 0))
    return pl.pallas_call(
        second_norm_kernel,
        grid=(seqs,),
        in_specs=[
            by_seq(length, width),
            by_seq(length, width),
            by_seq(length, width),
            by_seq(length, length),
            by_seq(length, slots),
        ]
        + [vector] * 5,
        out_specs=[
            by_seq(length, width),
            by_seq(slots, width),
            by_seq(slots, width),
            pl.BlockSpec((8, width), lambda s: (0, 0)),
        ],
        out_shape=[
            shape((rows, width), low),
            shape((seqs * slots, width), full),
            shape((seqs * slots, width), low),
            shape((8, width), full),
        ],
        compiler_params=params(),
        cost_estimate=cost(2 * rows * width * (length + slots), rows * width * 16),
        name="second_norm",
    )(total, normed, cotangent, order, picked, offset, gain1, shift1, gain2, shift2)


def backward_kernel(place, grad_ref, *refs, chained):
    weights, refs = refs[:6], refs[6:]
    slope_refs, refs = refs[:2], refs[2:]
    if chained:
        start_ref, refs = refs[0], refs[1:]
    total_ref, hidden_refs, sums_ref = refs[0], refs[1:3], refs[3]
    grad = grad_ref[...]
    total = start_ref[...] if chained else None
    step = 256
    half = weights[0].shape[1]
    i = pl.program_id(0)

    @pl.when(i == 0)
    def _():
        sums_ref[...] = jnp.zeros_like(sums_ref)

    for r in range(2):
        up, down, _ = weights[3 * r : 3 * r + 3]
        for c in range(0, half, step):
            grad_active = dot(grad, down[c : c + step, :], 1, 1)
            grad_hidden = (grad_active * slope_refs[r][:, c : c + step]).astype(low)
            hidden_refs[r][:, c : c + step] = grad_hidden
            sums_ref[r : r + 1, c : c + step] += jnp.sum(grad_hidden.astype(full), 0, keepdims=True)
            term = dot(grad_hidden, up[:, c : c + step], 1, 1)
            total = term if total is None else total + term
    total_ref[...] = total


def backward(place, grad, pieces, sliced, slopes, start, block_rows):
    rows, width = grad.shape
    half = slopes[0].shape[1]
    block = pl.BlockSpec((block_rows, width), lambda i, place: (i, 0))
    wide = pl.BlockSpec((block_rows, half), lambda i, place: (i, 0))
    extra = [] if start is None else [start]
    return pl.pallas_call(
        functools.partial(backward_kernel, chained=bool(extra)),
        grid_spec=pltpu.PrefetchScalarGridSpec(
            num_scalar_prefetch=1,
            grid=(rows // block_rows,),
            in_specs=[block]
            + weight_specs(width, half, sliced)
            + [wide] * 2
            + [block] * len(extra),
            out_specs=[block, wide, wide, pl.BlockSpec((8, half), lambda i, place: (0, 0))],
        ),
        out_shape=[shape((rows, width), full)]
        + [shape((rows, half), low)] * 2
        + [shape((8, half), full)],
        compiler_params=params(),
        cost_estimate=cost(8 * rows * width * half, rows * width * 20 + half * width * 8),
        name="backward",
    )(place, grad, *pieces, *slopes, *extra)


def first_back_kernel(
    total_ref, second_ref, normed_ref, inverse_ref, gain_ref, weight_ref, picked_ref,
    resid_ref, low_ref, context_ref, sums_ref,
):
    grad_first = second_ref[...] + total_ref[...]
    normed = normed_ref[...]
    resid = norm_backward(grad_first, normed, inverse_ref[:, :1], gain_ref[...])
    upper = resid.astype(low)
    lower = (resid - upper.astype(full)).astype(low)
    low_ref[...] = upper
    picked = picked_ref[...]
    resid_ref[...] = dot(picked, upper) + dot(picked, lower)
    grad_context = dot(upper, weight_ref[...], 1, 1).astype(low)
    context_ref[...] = dot(picked, grad_context).astype(low)
    add_rows(sums_ref, (grad_first * normed, grad_first, resid))


def first_back(total, second, normed, inverse, gain, weight, picked, length):
    rows, width = normed.shape
    slots = picked.shape[1]
    seqs, per_seq = rows // length, length // slots
    by_seq = lambda n, w: pl.BlockSpec((n, w), lambda s: (s, 0))
    whole = lambda a: pl.BlockSpec(a.shape, lambda s: (0,) * a.ndim)
    return pl.pallas_call(
        first_back_kernel,
        grid=(seqs,),
        in_specs=[
            by_seq(slots, width),
            by_seq(slots, width),
            pl.BlockSpec((slots, width), lambda s: (s * per_seq, 0)),
            by_seq(slots, 128),
            whole(gain),
            whole(weight),
            by_seq(length, slots),
        ],
        out_specs=[
            by_seq(length, width),
            by_seq(slots, width),
            by_seq(length, width),
            pl.BlockSpec((8, width), lambda s: (0, 0)),
        ],
        out_shape=[
            shape((rows, width), full),
            shape((seqs * slots, width), low),
            shape((rows, width), low),
            shape((8, width), full),
        ],
        compiler_params=params(),
        cost_estimate=cost(2 * rows * width * (width + slots), rows * width * 12),
        name="first_back",
    )(total, second, normed, inverse, gain, weight, picked)


def input_kernel(place, resid_ref, own_ref, other_ref, *refs):
    weights, out_ref = refs[:6], refs[6]
    total = resid_ref[...]
    group = weights[0].shape[1]
    for side, grads in enumerate((own_ref, other_ref)):
        for n in range(3):
            total += dot(grads[:, n * group : (n + 1) * group], weights[3 * side + n][...], 1, 1)
    out_ref[...] = total.astype(low)


def input_grad(place, resid, own, other, weights):
    rows, width = resid.shape
    group = own.shape[1] // 3
    block_rows = 256
    block = pl.BlockSpec((block_rows, width), lambda i, place: (i, 0))
    wide = pl.BlockSpec((block_rows, 3 * group), lambda i, place: (i, 0))
    specs = [
        pl.BlockSpec((width, group), lambda i, place, side=side: (0, place[3] ^ side))
        for side in range(2)
        for n in range(3)
    ]
    return pl.pallas_call(
        input_kernel,
        grid_spec=pltpu.PrefetchScalarGridSpec(
            num_scalar_prefetch=1,
            grid=(rows // block_rows,),
            in_specs=[block, wide, wide] + specs,
            out_specs=block,
        ),
        out_shape=shape((rows, width), low),
        compiler_params=params(),
        cost_estimate=cost(12 * rows * width * group, rows * width * 12),
        name="input_grad",
    )(place, resid, own, other, *weights, *weights)


def make_local(n_dp):
    bits = n_dp.bit_length() - 1

    def swap(a, bit):
        return lax.ppermute(a, "dp", [(i, i ^ (1 << bit)) for i in range(n_dp)])

    def swap_tp(a):
        return lax.ppermute(a, "tp", [(0, 1), (1, 0)])

    def added(a, b):
        return (a.astype(full) + b.astype(full)).astype(low)

    def in_order(mine, other, bit, axis):
        return jnp.concatenate(
            [jnp.where(bit == 0, mine, other), jnp.where(bit == 0, other, mine)], axis
        )

    def local(
        tokens,
        masked_positions,
        cotangent,
        query_weight,
        query_bias,
        key_weight,
        value_weight,
        value_bias,
        output_weight,
        output_bias,
        first_gain,
        first_shift,
        up_weight,
        up_bias,
        down_weight,
        lowering_offset,
        second_gain,
        second_shift,
        channel_filter_scores,
        mask_noise,
    ):
        rows, width = tokens.shape
        seqs, slots = masked_positions.shape
        length = rows // seqs
        own_heads = channel_filter_scores.shape[0]
        depth = width // (2 * own_heads)
        scale = depth ** (-0.5)
        pairs = own_heads * depth // 128
        half = up_weight.shape[1] // 2
        dp, tp = lax.axis_index("dp"), lax.axis_index("tp")
        bit = [(dp >> b) & 1 for b in range(bits)]
        quarter = 2 * bit[0] + bit[1]

        def place(side):
            return jnp.stack([(tp ^ side) * pairs, quarter, bit[0], tp]).astype(jnp.int32)

        own, other = place(0), place(1)

        def halves(a, axis, which):
            n = a.shape[axis] // 2
            return lax.dynamic_slice_in_dim(a, which * n, n, axis)

        def quarter_of(a, axis):
            n = a.shape[axis] // 4
            return lax.dynamic_slice_in_dim(a, quarter * n, n, axis)

        gate = jax.nn.sigmoid(
            (channel_filter_scores.astype(full) + mask_noise.astype(full)) / heat
        ).astype(low)
        gate_0 = swap_tp(quarter_of(gate, 1))
        gate_1 = swap(gate_0, 1)
        gate_2, gate_3 = swap(gate_0, 0), swap(gate_1, 0)
        other_gates = (gate_0, gate_1, gate_2, gate_3)
        own_gates = (gate,) * 4

        up_q, down_q = swap_tp(quarter_of(up_weight, 1)), swap_tp(quarter_of(down_weight, 0))
        bias_o = swap_tp(up_bias)
        up_near = in_order(up_q, swap(up_q, 1), bit[1], 1)
        down_near = in_order(down_q, swap(down_q, 1), bit[1], 0)
        up_far, down_far = swap(up_near, 0), swap(down_near, 0)
        bias_own = up_bias[None, :]
        bias_near = halves(bias_o, 0, bit[0])[None, :]
        bias_far = halves(bias_o, 0, 1 - bit[0])[None, :]
        own_pieces = (up_weight, down_weight, bias_own) * 2
        other_pieces = (up_near, down_near, bias_near, up_far, down_far, bias_far)

        row = lambda v: v[None, :]

        queries = ((dot(tokens, query_weight) + query_bias).astype(low).astype(full) * scale).astype(
            low
        )
        keys = dot(tokens, key_weight).astype(low)
        values = (dot(tokens, value_weight) + value_bias).astype(low)
        earlier = attend(own, queries, keys, values, own_gates, True, [], length)
        context, logsum = attend(
            other, queries, keys, values, other_gates, False, earlier, length
        )

        order, picked, context_c, x, normed, inverse = first_norm(
            masked_positions,
            context,
            tokens,
            output_weight,
            row(output_bias),
            row(first_gain),
            row(first_shift),
            length,
        )
        total, own_a0, own_a1, own_s0, own_s1 = forward(
            own, x, own_pieces, True, None, length, slots
        )
        total, far_a0, far_a1, far_s0, far_s1 = forward(
            other, x, other_pieces, False, total, length, slots
        )
        layer_output, grad_second, grad_forward, sums_second = second_norm(
            total,
            normed,
            cotangent,
            order,
            picked,
            row(lowering_offset),
            row(first_gain),
            row(first_shift),
            row(second_gain),
            row(second_shift),
        )

        def reduce_rows(mine, axis):
            for b in range(1, bits):
                keep, send = halves(mine, axis, bit[b]), halves(mine, axis, 1 - bit[b])
                mine = added(keep, swap(send, b))
            for b in range(bits - 1, 0, -1):
                mine = in_order(mine, swap(mine, b), bit[b], axis)
            return mine

        def reduce_chunk(grad, axis, final_axis):
            send_far, send_own = grad(1, 1).astype(low), grad(0, 1).astype(low)
            got_far, got_own = swap(send_far, 0), swap(send_own, 0)
            keep_far = (grad(1, 0) + got_far.astype(full)).astype(low)
            got = swap_tp(keep_far)
            keep_own = (grad(0, 0) + got_own.astype(full) + got.astype(full)).astype(low)
            mine = reduce_rows(keep_own, axis)
            return in_order(mine, swap(mine, 0), bit[0], final_axis)

        actives = ((own_a0, own_a1), (far_a0, far_a1))
        down_grad = reduce_chunk(
            lambda side, r: dot(actives[side][r], grad_forward, 0, 0), 0, 0
        )

        back, own_h0, own_h1, own_sums = backward(
            own, grad_forward, own_pieces, True, (own_s0, own_s1), None, slots
        )
        back, far_h0, far_h1, far_sums = backward(
            other, grad_forward, other_pieces, False, (far_s0, far_s1), back, slots
        )
        x_c = x.reshape(seqs, length, width)[:, :slots].reshape(seqs * slots, width)
        hiddens = ((own_h0, own_h1), (far_h0, far_h1))
        up_grad = reduce_chunk(lambda side, r: dot(x_c, hiddens[side][r], 0, 0), 0, 1)

        resid, grad_attention, grad_context, sums_first = first_back(
            back, grad_second, normed, inverse, row(first_gain), output_weight, picked, length
        )
        context_h = [halves(context_c, 1, bit[0]), halves(context_c, 1, 1 - bit[0])]
        attention_h = [halves(grad_attention, 1, tp), halves(grad_attention, 1, 1 - tp)]
        output_grad = reduce_chunk(
            lambda side, r: dot(context_h[r], attention_h[side], 0, 0), 0, 0
        )

        grads_far, mask_far, sums_far = attend_back(
            other, queries, keys, values, grad_context, logsum, other_gates, False, length, scale
        )
        grads_own, mask_own, sums_own = attend_back(
            own, queries, keys, values, grad_context, logsum, own_gates, True, length, scale
        )
        masks = (mask_own, mask_far)
        mask_grad = reduce_chunk(
            lambda side, r: halves(masks[side], 1, bit[0] ^ r).astype(full), 1, 1
        )
        tokens_h = [halves(tokens, 1, bit[0]), halves(tokens, 1, 1 - bit[0])]
        grads_all = (grads_own, grads_far)
        qkv_grad = reduce_chunk(lambda side, r: dot(tokens_h[r], grads_all[side], 0, 0), 0, 0)
        tokens_grad = input_grad(
            own, resid, grads_own, grads_far, (query_weight, key_weight, value_weight)
        )

        def both(mine, theirs):
            return in_order(mine, theirs, tp, 0)

        def hidden_half(sums):
            return in_order(sums[0], sums[1], bit[0], 0)

        vectors = jnp.concatenate(
            [
                both(hidden_half(own_sums), hidden_half(far_sums)),
                both(sums_own[0], sums_far[0]),
                both(sums_own[1], sums_far[1]),
                sums_first[0],
                sums_first[1],
                sums_first[2],
                sums_second[0],
                sums_second[1],
                sums_second[2],
            ]
        ).reshape(-1, 128)
        vectors = vectors + swap_tp(vectors)
        for b in range(bits):
            vectors = vectors + swap(vectors, b)
        vectors = vectors.reshape(-1)
        hidden_all = 4 * half
        up_bias_grad = halves(vectors[:hidden_all], 0, tp)
        rest = vectors[hidden_all:].reshape(-1, width)
        rest = halves(rest, 1, tp)
        query_bias_grad, value_bias_grad, fg, fs, ob, sg, ss, db = [rest[i] for i in range(8)]

        group = own_heads * depth
        qkv_grad = qkv_grad.astype(full)
        exact = jax.nn.sigmoid(
            (channel_filter_scores.astype(full) + mask_noise.astype(full)) / heat
        )
        return (
            layer_output,
            tokens_grad,
            qkv_grad[:, :group],
            query_bias_grad,
            qkv_grad[:, group : 2 * group],
            qkv_grad[:, 2 * group :],
            value_bias_grad,
            output_grad.astype(full),
            ob,
            fg,
            fs,
            up_grad.astype(full),
            up_bias_grad,
            down_grad.astype(full),
            db,
            sg,
            ss,
            mask_grad.astype(full) * exact * (1.0 - exact) / heat,
        )

    return local


def solution(mesh):
    in_specs = (
        P(("dp", "tp"), None),
        P(("dp", "tp"), None),
        P(("dp", "tp"), None),
        P(),
        P(),
        P(),
        P(),
        P(),
        P(),
        P(),
        P(),
        P(),
        P(None, "tp"),
        P("tp"),
        P("tp", None),
        P(),
        P(),
        P(),
        P("tp", None, None),
        P("tp", None, None),
    )
    out_specs = (
        P(("dp", "tp"), None),
        P(("dp", "tp"), None),
        P(None, "tp"),
        P("tp"),
        P(None, "tp"),
        P(None, "tp"),
        P("tp"),
        P(None, "tp"),
        P("tp"),
        P("tp"),
        P("tp"),
        P(None, "tp"),
        P("tp"),
        P("tp", None),
        P("tp"),
        P("tp"),
        P("tp"),
        P("tp", None, None),
    )
    local = make_local(mesh.shape["dp"])
    return jax.shard_map(local, mesh=mesh, in_specs=in_specs, out_specs=out_specs, check_vma=False)
```

```python
import functools

import jax
import jax.numpy as jnp
from jax import lax
from jax.experimental import pallas as pl
from jax.experimental.pallas import tpu as pltpu
from jax.sharding import PartitionSpec as P

heat = 0.6
epsilon = 1e-06
low = jnp.bfloat16
full = jnp.float32
MIB = 1 << 20
vmem_mib = 28
kernel_flops = 8_000_000_000
early, late = 0.0, 1.0


orders = {
    "down": (1,),
    "mask0": (2,),
    "mask1": (1,),
    "qkv": (),
    "up": (1, 2),
}


def dot(left, right, left_dim=1, right_dim=0):
    return lax.dot_general(
        left, right, (((left_dim,), (right_dim,)), ((), ())), preferred_element_type=full
    )


def shape(dims, kind):
    return jax.ShapeDtypeStruct(dims, kind)


class Flow:
    def __init__(self, n_dp):
        self.n_dp = n_dp
        self.token = None
        self.sends = []
        self.tasks = []
        self.done = {}
        self.now = 0.0
        self.free = {}
        self.started = False
        self.fillers = []

    def call(
        self, kernel, name, grid, places, args, in_specs, out_shape, out_specs,
        us, aliases=None, scratch=(), spaces="", out_spaces="", polled=True,
    ):
        if self.token is not None and polled:
            self.poll()
        self.now += us
        after = ([] if self.token is None else [self.token]) + self.sends
        self.sends = []
        place_of = {"v": pltpu.VMEM, "h": pltpu.HBM}
        args = [
            pltpu.with_memory_space_constraint(a, place_of[c]) if c in place_of else a
            for a, c in zip(args, spaces, strict=True)
        ]
        out_shape = [
            place_of[c](a.shape, a.dtype) if c in place_of else a
            for a, c in zip(out_shape, out_spaces, strict=True)
        ]
        first, many, outs = len(places) + len(args), len(after), len(out_shape)

        def run(*refs):
            refs = refs[:first] + refs[first + many :]
            kernel(*refs[: first + outs], *refs[first + outs + 1 :])
            refs[first + outs][...] = jnp.zeros((8, 128), full)

        result = pl.pallas_call(
            run,
            grid_spec=pltpu.PrefetchScalarGridSpec(
                num_scalar_prefetch=len(places),
                grid=grid,
                in_specs=list(in_specs) + [pl.BlockSpec(memory_space=pl.ANY)] * many,
                out_specs=list(out_specs) + [pl.BlockSpec((8, 128), lambda *_: (0, 0))],
                scratch_shapes=list(scratch),
            ),
            out_shape=list(out_shape) + [shape((8, 128), full)],
            input_output_aliases=aliases or {},
            compiler_params=pltpu.CompilerParams(vmem_limit_bytes=vmem_mib * MIB),
            cost_estimate=pl.CostEstimate(
                flops=kernel_flops, bytes_accessed=1, transcendentals=0
            ),
            name=name,
        )(*places, *args, *after)
        self.token = result[-1]
        return result[:-1]

    def pin(self, arrays):
        arrays = [self.token, *arrays]
        anywhere = [pl.BlockSpec(memory_space=pl.ANY)] * len(arrays)

        def run(*refs):
            pass

        self.token, *arrays = pl.pallas_call(
            run,
            in_specs=anywhere,
            out_specs=anywhere,
            out_shape=[shape(a.shape, a.dtype) for a in arrays],
            input_output_aliases={i: i for i in range(len(arrays))},
            compiler_params=pltpu.CompilerParams(vmem_limit_bytes=MIB),
            cost_estimate=pl.CostEstimate(flops=1, bytes_accessed=1, transcendentals=0),
            name="turn",
        )(*arrays)
        return arrays

    def swap(self, a, way):
        if way == "tp":
            got = lax.ppermute(a, "tp", [(0, 1), (1, 0)])
        else:
            got = lax.ppermute(a, "dp", [(i, i ^ (1 << way)) for i in range(self.n_dp)])
        kilobytes = a.size * a.dtype.itemsize / 1e3
        rate, delay = (400.0, 2.0) if way == 0 else (22.0, 3.5) if way == 3 else (44.0 if self.now > 70 else 38.0, 2.5)
        link = 2 if way == 3 else way
        self.now += 0.8 if self.started and way else 1.4 if way else 0.5
        self.started = self.started or way != 0
        self.free[link] = max(self.free.get(link, 0.0), self.now) + kilobytes / rate
        return got, self.free[link] + delay

    def start(self, task):
        self.tasks.append([task, *self.advance(task, None)])

    def advance(self, task, values):
        try:
            arrays, due, sends = task.send(values)
        except StopIteration:
            return [], None
        self.sends += sends
        self.now += 0.5
        return arrays, due

    def is_due(self, entry, slack):
        due = entry[2]
        return due in self.done if isinstance(due, str) else due <= self.now + slack

    def poll(self, slack=early):
        due = [entry for entry in self.tasks if self.is_due(entry, slack)]
        if not due:
            return
        for entry in due:
            if not isinstance(entry[2], str):
                self.now = max(self.now, entry[2])
        arrays = self.pin([a for entry in due for a in entry[1]])
        self.now += 0.5
        self.started = False
        for entry in due:
            mine, arrays = arrays[: len(entry[1])], arrays[len(entry[1]) :]
            entry[1:] = self.advance(entry[0], mine)
        self.tasks = [entry for entry in self.tasks if entry[1]]

    def wait(self, ready, slack=late):
        while not ready():
            if self.fillers and self.fillers[0][0] < 5.0:
                self.fillers.pop(0)[1]()
            if any(self.is_due(entry, 0.0) for entry in self.tasks):
                self.poll(slack)
                continue
            soonest = min(e[2] for e in self.tasks if not isinstance(e[2], str))
            fits = [n for n, (us, _) in enumerate(self.fillers) if us <= soonest - self.now + 2.0]
            if fits:
                self.fillers.pop(fits[0])[1]()
                continue
            self.now = max(self.now, soonest)
            self.poll(slack)


def head_lanes(width):
    lane = lax.broadcasted_iota(jnp.int32, (1, width), 1)
    first = lane < width // 2
    return first, (first.astype(full).astype(low), (1.0 - first.astype(full)).astype(low))


def quarter_rows(place, length, s, r):
    part = length // 4
    return pl.ds(pl.multiple_of(s * length + (place[1] ^ r) * part, part), part)


def rows_of(ref, place, length, s):
    return jnp.concatenate([ref[quarter_rows(place, length, s, r), :] for r in range(4)], 0)


def write_rows(ref, value, place, length, s):
    part = length // 4
    for r in range(4):
        ref[quarter_rows(place, length, s, r), :] = value[r * part : (r + 1) * part]


def attend_kernel(place, q_ref, k_ref, v_ref, *rest, length, add):
    gates, (context_ref, logsum_ref) = rest[:4], rest[-2:]
    first, lanes = head_lanes(q_ref.shape[1])
    levels = [jnp.concatenate([g[h] for g in gates], 0) for h in range(2)]
    for s in range(q_ref.shape[0] // length):
        queries = rows_of(q_ref, place, length, s)
        keys = k_ref[s * length : (s + 1) * length, :]
        values = v_ref[s * length : (s + 1) * length, :]
        mixed, logs = [], []
        for h in range(2):
            scores = dot(queries * lanes[h], keys, 1, 1)
            peak = jnp.max(scores, -1, keepdims=True)
            expo = jnp.exp(scores - peak)
            total = jnp.sum(expo, -1, keepdims=True)
            weights = (expo * levels[h].astype(full)).astype(low)
            mixed.append(dot(weights, values) * (1.0 / total))
            logs.append(peak + jnp.log(total))
        write_rows(context_ref, jnp.where(first, mixed[0], mixed[1]).astype(low), place, length, s)
        here = 2 * pl.program_id(0) if add else 0
        lane = lax.broadcasted_iota(jnp.int32, first.shape, 1)
        columns = jnp.where(lane == here, logs[0], jnp.where(lane == here + 1, logs[1], 0.0))
        for r in range(4):
            rows = quarter_rows(place, length, s, r)
            part = columns[r * (length // 4) : (r + 1) * (length // 4)]
            if add:

                @pl.when(pl.program_id(0) == 0)
                def _():
                    logsum_ref[rows, :] = part

                @pl.when(pl.program_id(0) > 0)
                def _():
                    logsum_ref[rows, :] += part

            else:
                logsum_ref[rows, :] = part


def gate_specs(own, part, length, begin=0):
    if own:
        return [
            pl.BlockSpec((2, part, length), lambda hp, place, r=r: (begin + hp, place[1] ^ r, 0))
            for r in range(4)
        ]
    return [
        pl.BlockSpec((2, part, length), lambda hp, place, r=r: (begin + hp, r, 0)) for r in range(4)
    ]


def head_columns(rows, lanes, side, pairs, first=0):
    return pl.BlockSpec(
        (rows, lanes), lambda hp, place: (0, (place[0] ^ side) * pairs + first + hp)
    )


def attend_own(flow, place, queries, keys, values, gate, length):
    rows, width = queries.shape
    pairs, part = gate.shape[0] // 2, length // 4
    column = head_columns(rows, 128, 0, pairs)
    return flow.call(
        functools.partial(attend_kernel, length=length, add=True),
        "attend_own",
        (pairs,),
        [place],
        [queries, keys, values] + [gate] * 4,
        [column] * 3 + gate_specs(True, part, length),
        [shape((rows, width), low), shape((rows, 128), full)],
        [column, pl.BlockSpec((rows, 128), lambda hp, place: (0, 0))],
        spaces="hhhhhhh",
        out_spaces="hh",
        us=8.7,
    )


def attend_far_kernel(place, q_ref, k_ref, v_ref, *rest, length):
    gates, outs = rest[:4], rest[-3:]
    attend_kernel(place, q_ref, k_ref, v_ref, *gates, *outs[:2], length=length, add=False)
    part = length // 4
    for r in range(4):
        outs[2][:, r * part : (r + 1) * part, :] = gates[r][...]


def attend_far(flow, place, queries, keys, values, gates, pair, pairs, earlier, length):
    rows, width = queries.shape
    column = head_columns(rows, 128, 1, pairs, pair)
    return flow.call(
        functools.partial(attend_far_kernel, length=length),
        "attend_far",
        (1,),
        [place],
        [queries, keys, values, *gates, *earlier],
        [column] * 3
        + [pl.BlockSpec(g.shape, lambda hp, place: (0, 0, 0)) for g in gates]
        + [pl.BlockSpec(memory_space=pl.ANY)] * len(earlier),
        [
            shape((rows, width), low),
            shape((rows, 128), full),
            shape((2 * pairs, length, length), low),
        ],
        [
            column,
            pl.BlockSpec((rows, 128), lambda hp, place: (0, 0)),
            pl.BlockSpec((2, length, length), lambda hp, place: (pair, 0, 0)),
        ],
        aliases=dict(zip((8, 9), (0, 2))) if len(earlier) == 2 else {8: 0},
        spaces="hhh----" + "h" * len(earlier),
        out_spaces="hhh",
        us=5.3,
    )


def attend_back_kernel(place, q_ref, k_ref, v_ref, d_ref, logsum_ref, tokens_ref, *rest, length, scale, lane):
    gates = rest[:4]
    grads_ref, keep_ref, send_ref, keep_w, send_w, sums_ref = rest[-6:]
    hp = pl.program_id(0)
    group = grads_ref.shape[1] // 3
    width = q_ref.shape[1]
    part = length // 4
    first, lanes = head_lanes(width)
    levels = [jnp.concatenate([g[h] for g in gates], 0) for h in range(2)]
    masks = [None, None]
    sums_q = sums_v = 0.0
    for s in range(q_ref.shape[0] // length):
        here = slice(s * length, (s + 1) * length)
        queries, grads = rows_of(q_ref, place, length, s), rows_of(d_ref, place, length, s)
        logs = rows_of(logsum_ref, place, length, s)[:, lane : lane + 2]
        keys, values = k_ref[here, :], v_ref[here, :]
        totals = None
        for h in range(2):
            own_q, own_d, own_k = queries * lanes[h], grads * lanes[h], keys * lanes[h]
            sloped, weighted, produced = [], [], []
            for c in range(0, length, 128):
                tile = slice(c, c + 128)
                probs = jnp.exp(dot(own_q[tile], keys, 1, 1) - logs[tile, h : h + 1])
                product = dot(own_d[tile], values, 1, 1) * probs
                level = levels[h][tile].astype(full)
                gated = product * level
                rest = jnp.sum(gated, -1, keepdims=True)
                sloped.append((gated - probs * rest).astype(low))
                weighted.append((probs * level).astype(low))
                produced.append(product)
            slopes, weights = jnp.concatenate(sloped, 0), jnp.concatenate(weighted, 0)
            product = jnp.concatenate(produced, 0)
            masks[h] = product if masks[h] is None else masks[h] + product
            new = (dot(slopes, own_k), dot(own_q, slopes, 0, 0).T, dot(own_d, weights, 0, 0).T)
            totals = new if totals is None else tuple(a + b for a, b in zip(totals, new))
        grad_q, grad_k, grad_v = (
            (totals[0] * scale).astype(low),
            totals[1].astype(low),
            totals[2].astype(low),
        )
        for n, grad in enumerate((grad_q, grad_k, grad_v)):
            at = pl.ds(pl.multiple_of(n * group + hp * width, width), width)
            if n == 0:
                for r in range(4):
                    rows = quarter_rows(place, length, s, r)
                    grads_ref[rows, at] = grad[r * part : (r + 1) * part]
            else:
                grads_ref[here, at] = grad
        sums_q += jnp.sum(grad_q.astype(full), 0, keepdims=True)
        sums_v += jnp.sum(grad_v.astype(full), 0, keepdims=True)
    for h in range(2):
        mask = masks[h].astype(low)
        keep_ref[h] = mask[: 2 * part]
        send_ref[h] = mask[2 * part :]
    sums_ref[...] = jnp.concatenate([sums_q, sums_v, jnp.zeros((6, width), full)], 0)
    half = tokens_ref.shape[1] // 2
    for n in range(3):
        at = pl.ds(pl.multiple_of(n * group + hp * width, width), width)
        grad = grads_ref[:, at]
        for r, ref in enumerate((keep_w, send_w)):
            rows = tokens_ref[:, pl.ds(pl.multiple_of((place[2] ^ r) * half, half), half)]
            ref[:, n * width : (n + 1) * width] = dot(rows, grad, 0, 0).astype(low)


def attend_back(
    flow, place, queries, keys, values, grad_context, logsum, tokens, gate, side, length,
    scale, begin, masks, at, heads_held, weights,
):
    rows, width = queries.shape
    heads, part, lanes = gate.shape[0], length // 4, 128
    pairs = heads // 2
    column = head_columns(rows, lanes, side, pairs, begin)
    group = lanes
    mask = pl.BlockSpec((2, length // 2, length), lambda hp, place: (at, 0, 0))
    anywhere = [pl.BlockSpec(memory_space=pl.ANY)]
    held = [*weights, *masks]
    aliases = {11: 3, 12: 4}
    if masks:
        aliases.update({13: 1, 14: 2})
    return flow.call(
        functools.partial(
            attend_back_kernel, length=length, scale=scale, lane=0 if side else 2 * begin
        ),
        "attend_back",
        (1,),
        [place],
        [queries, keys, values, grad_context, logsum, tokens] + [gate] * 4 + held,
        [column] * 4
        + [pl.BlockSpec(logsum.shape, lambda hp, place: (0, 0))]
        + [pl.BlockSpec(tokens.shape, lambda hp, place: (0, 0))]
        + gate_specs(side == 0, part, length, begin)
        + anywhere * len(held),
        [shape((rows, 3 * group), low)]
        + [shape((heads_held, length // 2, length), low)] * 2
        + [shape(weights[0].shape, low)] * 2
        + [shape((8, group), full)],
        [pl.BlockSpec((rows, 3 * group), lambda hp, place: (0, 0))]
        + [mask] * 2
        + [pl.BlockSpec((width // 2, 3 * lanes), lambda hp, place: (0, begin))] * 2
        + [pl.BlockSpec((8, lanes), lambda hp, place: (0, hp))],
        aliases=aliases,
        spaces="hhh-h-" + "h" * 4 + "-" * len(held),
        out_spaces="h-----",
        us=8.8,
    )


def norm_forward(hidden, gain, shift):
    centre = hidden - jnp.mean(hidden, -1, keepdims=True)
    spread = jnp.mean(centre * centre, -1, keepdims=True)
    inverse = lax.rsqrt(spread + epsilon)
    normed = centre * inverse
    return normed * gain + shift, normed, inverse


def norm_backward(incoming, normed, inverse, gain):
    scaled = incoming * gain
    return inverse * (
        scaled
        - jnp.mean(scaled, -1, keepdims=True)
        - normed * jnp.mean(scaled * normed, -1, keepdims=True)
    )


def add_rows(ref, rows):
    packed = jnp.concatenate(
        [jnp.sum(row, 0, keepdims=True) for row in rows]
        + [jnp.zeros((8 - len(rows), ref.shape[1]), full)],
        0,
    )

    @pl.when(pl.program_id(0) == 0)
    def _():
        ref[...] = packed

    @pl.when(pl.program_id(0) > 0)
    def _():
        ref[...] += packed


def first_norm_kernel(
    slots_ref, context_ref, tokens_ref, weight_ref, bias_ref, gain_ref, shift_ref,
    order_ref, picked_ref, compact_ref, low_ref, kept_ref, normed_ref, inverse_ref,
):
    length, slots = tokens_ref.shape[0], slots_ref.shape[-1]
    position = lax.broadcasted_iota(jnp.int32, (length, slots), 0)
    hit = (position == slots_ref[pl.ds(pl.program_id(0), 1), :]).astype(full)
    chosen = jnp.max(hit, -1, keepdims=True)
    row = lax.broadcasted_iota(jnp.int32, (length, length), 0)
    column = lax.broadcasted_iota(jnp.int32, (length, length), 1)
    lower = (column <= row).astype(full).astype(low)
    upto = dot(lower, jnp.broadcast_to(chosen, (length, 128)).astype(low))[:, :1]
    count = jnp.sum(chosen, 0, keepdims=True)
    at = lax.broadcasted_iota(jnp.int32, (length, 1), 0).astype(full)
    target = jnp.where(chosen > 0, upto - 1.0, count + at - upto)
    order = (column.astype(full) == target).astype(full)
    picked_ref[...] = (order * chosen)[:, :slots].astype(low)
    order = order.astype(low)
    order_ref[...] = order
    context = dot(order, context_ref[...], 0, 0).astype(low)
    tokens = dot(order, tokens_ref[...], 0, 0)
    compact_ref[...] = context[:slots]
    attention = dot(context, weight_ref[...]) + bias_ref[...]
    out, normed, inverse = norm_forward(tokens + attention, gain_ref[...], shift_ref[...])
    out = out.astype(low)
    low_ref[...] = out
    kept_ref[...] = out[:slots]
    normed_ref[...] = normed
    inverse_ref[...] = jnp.broadcast_to(inverse[:slots], (slots, 128))


def by_seq(n, w):
    return pl.BlockSpec((n, w), lambda s: (s, 0))


def whole_of(a):
    return pl.BlockSpec(a.shape, lambda *_: (0,) * a.ndim)


def first_norm(flow, positions, context, tokens, weight, bias, gain, shift, length):
    rows, width = tokens.shape
    seqs, slots = positions.shape
    vectors = [weight, bias, gain, shift]
    return flow.call(
        first_norm_kernel,
        "first_norm",
        (seqs,),
        [],
        [positions, context, tokens, *vectors],
        [
            whole_of(positions),
            by_seq(length, width),
            by_seq(length, width),
        ]
        + [whole_of(v) for v in vectors],
        [
            shape((rows, length), low),
            shape((rows, slots), low),
            shape((seqs * slots, width), low),
            shape((rows, width), low),
            shape((seqs * slots, width), low),
            shape((rows, width), full),
            shape((seqs * slots, 128), full),
        ],
        [
            by_seq(length, length),
            by_seq(length, slots),
            by_seq(slots, width),
            by_seq(length, width),
            by_seq(slots, width),
            by_seq(length, width),
            by_seq(slots, 128),
        ],
        spaces="-h-----",
        out_spaces="-------",
        us=9,
    )


def gelu_parts(hidden):
    size = jnp.abs(hidden)
    t = 1.0 / (1.0 + (0.3275911 * 0.7071067811865476) * size)
    poly = 1.061405429 * t - 1.453152027
    poly = poly * t + 1.421413741
    poly = poly * t - 0.284496736
    poly = poly * t + 0.254829592
    bell = jnp.exp(hidden * hidden * -0.5)
    tail = 0.5 * poly * t * bell
    below = jnp.where(hidden > 0, 1.0 - tail, tail)
    return below, bell


def far_pieces(pieces, held, sems, order):
    i = pl.program_id(0)

    def copies(n):
        r = order[n]
        return [
            pltpu.make_async_copy(pieces[r][j], held[j].at[n % 2], sems.at[j, n % 2])
            for j in range(2)
        ]

    for n in range(4):

        @pl.when(i == n)
        def _(n=n):
            if n == 0:
                for copy in copies(0):
                    copy.start()
            if n < 3:
                for copy in copies(n + 1):
                    copy.start()
            for copy in copies(n):
                copy.wait()

    slot = lax.rem(i, 2)
    return held[0][slot], held[1][slot]


def forward_kernel(place, x_ref, *refs, own, length, slots):
    if own:
        (up_ref, down_ref, bias_ref, total_ref, active_ref, slope_ref) = refs
        up, down = up_ref[...], down_ref[...]
    else:
        pieces, refs = refs[:8], refs[8:]
        bias_ref, start_ref, total_ref, active_ref, slope_ref, *held, sems = refs
        pieces = [pieces[2 * r : 2 * r + 2] for r in range(4)]
        up, down = far_pieces(pieces, held, sems, (0, 1, 2, 3))

    @pl.when(pl.program_id(0) == 0)
    def _():
        total_ref[...] = jnp.zeros_like(total_ref) if own else start_ref[...]

    bias = bias_ref[...]
    for block in range(x_ref.shape[0] // slots):
        rows = slice(block * slots, (block + 1) * slots)
        hidden = dot(x_ref[rows, :], up) + bias
        below, bell = gelu_parts(hidden)
        active = (hidden * below).astype(low)
        s, part = divmod(block, length // slots)
        if part == 0:
            kept = slice(s * slots, (s + 1) * slots)
            active_ref[kept, :] = active
            slope_ref[kept, :] = below + hidden * bell * 0.3989422804014327
        total_ref[rows, :] += dot(active, down)


def own_specs(width, part, first):
    return [
        pl.BlockSpec((width, part), lambda i, place: (0, place[1] ^ i ^ first)),
        pl.BlockSpec((part, width), lambda i, place: (place[1] ^ i ^ first, 0)),
    ]


def far_scratch(width, part):
    return [
        pltpu.VMEM((2, width, part), low),
        pltpu.VMEM((2, part, width), low),
        pltpu.SemaphoreType.DMA((2, 2)),
    ]


def forward(flow, place, x, weights, bias, start, length, slots):
    rows, width = x.shape
    own = start is None
    part = bias.shape[1] // 4
    kept = rows // length * slots
    whole = pl.BlockSpec((rows, width), lambda i, place: (0, 0))
    wide = pl.BlockSpec((kept, part), lambda i, place: (0, i))
    anywhere = pl.BlockSpec(memory_space=pl.ANY)
    return flow.call(
        functools.partial(forward_kernel, own=own, length=length, slots=slots),
        "forward",
        (4,),
        [place],
        [x, *weights, bias] + ([] if own else [start]),
        [whole]
        + (own_specs(width, part, 0) if own else [anywhere] * 8)
        + [pl.BlockSpec((1, part), lambda i, place: (0, place[1] ^ i))]
        + ([] if own else [whole]),
        [shape((rows, width), full), shape((kept, 4 * part), low), shape((kept, 4 * part), full)],
        [whole, wide, wide],
        scratch=[] if own else far_scratch(width, part),
        spaces="----" if own else "-" * 11,
        out_spaces="-hh",
        us=14.5,
    )


def second_norm_kernel(
    total_ref, normed_ref, cotangent_ref, order_ref, picked_ref,
    offset_ref, gain1_ref, shift1_ref, gain2_ref, shift2_ref,
    out_ref, grad_ref, low_ref, sums_ref,
):
    slots = picked_ref.shape[1]
    first_out = normed_ref[...] * gain1_ref[...] + shift1_ref[...]
    gain = gain2_ref[...]
    out, normed, inverse = norm_forward(
        first_out + (total_ref[...] + offset_ref[...]), gain, shift2_ref[...]
    )
    out_ref[...] = dot(order_ref[...], out.astype(low)).astype(low)
    grad_out = dot(picked_ref[...], cotangent_ref[...], 0, 0)
    normed, inverse = normed[:slots], inverse[:slots]
    grad = norm_backward(grad_out, normed, inverse, gain)
    grad_ref[...] = grad
    low_ref[...] = grad.astype(low)
    add_rows(sums_ref, (grad_out * normed, grad_out, grad))


def second_norm(flow, total, normed, cotangent, order, picked, vectors):
    rows, width = total.shape
    length, slots = order.shape[1], picked.shape[1]
    seqs = rows // length
    return flow.call(
        second_norm_kernel,
        "second_norm",
        (seqs,),
        [],
        [total, normed, cotangent, order, picked, *vectors],
        [by_seq(length, width)] * 3
        + [by_seq(length, length), by_seq(length, slots)]
        + [whole_of(v) for v in vectors],
        [
            shape((rows, width), low),
            shape((seqs * slots, width), full),
            shape((seqs * slots, width), low),
            shape((8, width), full),
        ],
        [
            by_seq(length, width),
            by_seq(slots, width),
            by_seq(slots, width),
            pl.BlockSpec((8, width), lambda s: (0, 0)),
        ],
        spaces="-" * (5 + len(vectors)),
        out_spaces="----",
        us=6,
    )


def backward_kernel(place, grad_ref, x_ref, *refs, own):
    if own:
        (up_ref, down_ref, active_ref, slope_ref, start_ref), refs = refs[:5], refs[5:]
        up, down = up_ref[...], down_ref[...]
    else:
        pieces, (active_ref, slope_ref), refs = refs[:8], refs[8:10], refs[10:]
        refs, (*held, sems) = refs[:6], refs[6:]
        pieces = [pieces[2 * r : 2 * r + 2] for r in range(4)]
        up, down = far_pieces(pieces, held, sems, (2, 3, 0, 1))
    total_ref, down_send, down_keep, up_send, up_keep, sums_ref = refs
    i = pl.program_id(0)

    @pl.when(i == 0)
    def _():
        total_ref[...] = start_ref[...] if own else jnp.zeros_like(total_ref)

    grad = grad_ref[...]
    grad_active = dot(grad, down, 1, 1)
    grad_hidden = (grad_active * slope_ref[...]).astype(low)
    total_ref[...] += dot(grad_hidden, up, 1, 1)
    down_grad = dot(active_ref[...], grad, 0, 0).astype(low)
    up_grad = dot(x_ref[...], grad_hidden, 0, 0).astype(low)

    @pl.when(i < 2)
    def _():
        down_send[...] = down_grad
        up_send[...] = up_grad

    @pl.when(i >= 2)
    def _():
        down_keep[...] = down_grad
        up_keep[...] = up_grad

    sums = jnp.sum(grad_hidden.astype(full), 0, keepdims=True)
    sums_ref[...] = jnp.broadcast_to(sums, sums_ref.shape)


def backward(flow, place, grad, x, weights, active, slope, start):
    rows, width = grad.shape
    own = start is not None
    part = active.shape[1] // 4
    whole = pl.BlockSpec((rows, width), lambda i, place: (0, 0))
    wide = pl.BlockSpec((rows, part), lambda i, place: (0, i ^ 2))
    anywhere = pl.BlockSpec(memory_space=pl.ANY)
    return flow.call(
        functools.partial(backward_kernel, own=own),
        "backward",
        (4,),
        [place],
        [grad, x, *weights, active, slope] + ([start] if own else []),
        [whole, whole]
        + (own_specs(width, part, 2) if own else [anywhere] * 8)
        + [wide, wide]
        + ([whole] if own else []),
        [shape((rows, width), full)]
        + [shape((2 * part, width), low)] * 2
        + [shape((width, 2 * part), low)] * 2
        + [shape((8, 4 * part), full)],
        [
            whole,
            pl.BlockSpec((part, width), lambda i, place: (jnp.minimum(i, 1), 0)),
            pl.BlockSpec((part, width), lambda i, place: (jnp.maximum(i - 2, 0), 0)),
            pl.BlockSpec((width, part), lambda i, place: (0, jnp.minimum(i, 1))),
            pl.BlockSpec((width, part), lambda i, place: (0, jnp.maximum(i - 2, 0))),
            pl.BlockSpec((8, part), lambda i, place: (0, i ^ 2)),
        ],
        scratch=[] if own else far_scratch(width, part),
        spaces="----hh-" if own else "-" * 10 + "hh",
        out_spaces="------",
        us=12,
    )


def first_back_kernel(
    place, total_ref, second_ref, normed_ref, inverse_ref, gain_ref, weight_ref, picked_ref,
    rows_ref, resid_ref, context_ref, sums_ref, *refs,
):
    s = pl.program_id(0)
    grad_refs, total_grads = refs[:4], refs[4:]
    grad_first = second_ref[...] + total_ref[...]
    normed = normed_ref[...]
    resid = norm_backward(grad_first, normed, inverse_ref[:, :1], gain_ref[...])
    upper = resid.astype(low)
    lower = (resid - upper.astype(full)).astype(low)
    picked = picked_ref[...]
    resid_ref[...] = dot(picked, upper) + dot(picked, lower)
    grad_context = dot(upper, weight_ref[...], 1, 1).astype(low)
    context_ref[...] = dot(picked, grad_context).astype(low)
    add_rows(sums_ref, (grad_first * normed, grad_first, resid))
    weight_grad = dot(rows_ref[...], upper, 0, 0)

    @pl.when(s == 0)
    def _():
        total_grads[0][...] = weight_grad

    @pl.when(s > 0)
    def _():
        total_grads[0][...] += weight_grad

    @pl.when(s == pl.num_programs(0) - 1)
    def _():
        half = weight_ref.shape[0] // 2
        for side in range(2):
            for r in range(2):
                down = pl.ds(pl.multiple_of((place[2] ^ r) * half, half), half)
                along = pl.ds(pl.multiple_of((place[0] ^ side) * half, half), half)
                grad_refs[2 * side + r][...] = total_grads[0][down, along].astype(low)


def first_back(flow, place, total, second, normed, inverse, gain, weight, picked, rows_c, length):
    rows, width = normed.shape
    slots = picked.shape[1]
    seqs, per_seq = rows // length, length // slots
    half = width // 2
    seq = lambda n, w: pl.BlockSpec((n, w), lambda s, place: (s, 0))
    fixed = lambda n, w: pl.BlockSpec((n, w), lambda s, place: (0, 0))
    return flow.call(
        first_back_kernel,
        "first_back",
        (seqs,),
        [place],
        [total, second, normed, inverse, gain, weight, picked, rows_c],
        [
            seq(slots, width),
            seq(slots, width),
            pl.BlockSpec((slots, width), lambda s, place: (s * per_seq, 0)),
            seq(slots, 128),
            whole_of(gain),
            whole_of(weight),
            seq(length, slots),
            seq(slots, width),
        ],
        [shape((rows, width), full), shape((rows, width), low), shape((8, width), full)]
        + [shape((half, 4 * half), low)] * 4,
        [seq(length, width), seq(length, width), fixed(8, width)]
        + [pl.BlockSpec((half, half), lambda s, place: (0, 3))] * 4,
        scratch=[pltpu.VMEM((width, width), full)],
        spaces="--------",
        out_spaces="h------",
        us=10,
    )


def project_kernel(tokens_ref, *refs, scale):
    weights, (bias_q, bias_v), outs = refs[:3], refs[3:5], refs[5:]
    tokens = tokens_ref[...]
    queries = (dot(tokens, weights[0][...]) + bias_q[...]).astype(low)
    outs[0][...] = (queries.astype(full) * scale).astype(low)
    outs[1][...] = dot(tokens, weights[1][...]).astype(low)
    outs[2][...] = (dot(tokens, weights[2][...]) + bias_v[...]).astype(low)


def project(flow, tokens, weights, biases, scale):
    rows, width = tokens.shape
    block = pl.BlockSpec((256, width), lambda i: (i, 0))
    return flow.call(
        functools.partial(project_kernel, scale=scale),
        "project",
        (rows // 256,),
        [],
        [tokens, *weights, *biases],
        [block] + [whole_of(v) for v in (*weights, *biases)],
        [shape((rows, width), low)] * 3,
        [block] * 3,
        spaces="-" * 6,
        out_spaces="hhh",
        us=8.5,
    )


def input_kernel(place, resid_ref, *refs, blocks):
    grads, weights, out_ref = refs[: len(blocks)], refs[len(blocks) : -1], refs[-1]
    total = resid_ref[...]
    for ref, (side, start, group) in zip(grads, blocks):
        for n in range(3):
            weight = weights[3 * side + n][:, start : start + group]
            total += dot(ref[:, n * group : (n + 1) * group], weight, 1, 1)
    out_ref[...] = total.astype(low)


def input_grad(flow, place, resid, parts, weights):
    rows, width = resid.shape
    half = width // 2
    block = pl.BlockSpec((256, width), lambda i, place: (i, 0))
    grads = [part[2] for part in parts]
    specs = [
        pl.BlockSpec((width, half), lambda i, place, side=side: (0, place[0] ^ side))
        for side in range(2)
        for n in range(3)
    ]
    return flow.call(
        functools.partial(
            input_kernel, blocks=[(side, start, g.shape[1] // 3) for side, start, g in parts]
        ),
        "input_grad",
        (rows // 256,),
        [place],
        [resid, *grads, *weights, *weights],
        [block]
        + [pl.BlockSpec((256, g.shape[1]), lambda i, place: (i, 0)) for g in grads]
        + specs,
        [shape((rows, width), low)],
        [block],
        spaces="h" * (1 + len(parts)) + "-" * 6,
        out_spaces="h",
        polled=False,
        us=12.3,
    )[0]


def gate_kernel(place, scores_ref, noise_ref, gate_ref, *parts):
    gate = jax.nn.sigmoid((scores_ref[...].astype(full) + noise_ref[...].astype(full)) / heat)
    gate_ref[...] = gate.astype(low)
    part = gate_ref.shape[1] // 4
    mine = pl.ds(pl.multiple_of(place[1] * part, part), part)
    for p, ref in enumerate(parts):

        @pl.when(pl.program_id(0) == p)
        def _(ref=ref):
            ref[...] = gate_ref[:, mine, :]


def gates(flow, place, scores, noise):
    heads, length, _ = scores.shape
    pairs, part = heads // 2, length // 4
    block = pl.BlockSpec((2, length, length), lambda i, place: (i, 0, 0))
    return flow.call(
        gate_kernel,
        "gates",
        (pairs,),
        [place],
        [scores, noise],
        [block, block],
        [shape(scores.shape, low)] + [shape((2, part, length), low)] * pairs,
        [block] + [pl.BlockSpec((2, part, length), lambda i, place: (0, 0, 0))] * pairs,
        spaces="--",
        out_spaces="h" + "-" * pairs,
        us=5.5,
    )


def mask_kernel(place, scores_ref, noise_ref, mine_ref, got_ref, *refs):
    out_ref = refs[-1]
    half = mine_ref.shape[1]
    for side, ref in enumerate((mine_ref, got_ref)):
        core = place[2] ^ side
        rows = pl.ds(pl.multiple_of(core * half, half), half)
        gate = jax.nn.sigmoid(
            (scores_ref[:, rows, :].astype(full) + noise_ref[:, rows, :].astype(full)) / heat
        )
        out_ref[:, rows, :] = ref[...].astype(full) * (gate * (1.0 - gate) / heat)


def mask_grad(flow, place, scores, noise, mine, got, begin, earlier):
    heads, length, _ = scores.shape
    block = pl.BlockSpec((1, length, length), lambda i, place: (begin + i, 0, 0))
    half = pl.BlockSpec((1, length // 2, length), lambda i, place: (i, 0, 0))
    return flow.call(
        mask_kernel,
        "mask_grad",
        (mine.shape[0],),
        [place],
        [scores, noise, mine, got, *earlier],
        [block, block, half, half] + [pl.BlockSpec(memory_space=pl.ANY)] * len(earlier),
        [shape(scores.shape, full)],
        [block],
        aliases={5: 0} if earlier else {},
        spaces="hh--" + "h" * len(earlier),
        out_spaces="h",
        polled=False,
        us=mine.shape[0],
    )


def make_local(n_dp):
    bits = n_dp.bit_length() - 1

    def added(a, b):
        return (a.astype(full) + b.astype(full)).astype(low)

    def in_order(mine, other, bit, axis):
        return jnp.concatenate(
            [jnp.where(bit == 0, mine, other), jnp.where(bit == 0, other, mine)], axis
        )

    def local(
        tokens,
        masked_positions,
        cotangent,
        query_weight,
        query_bias,
        key_weight,
        value_weight,
        value_bias,
        output_weight,
        output_bias,
        first_gain,
        first_shift,
        up_weight,
        up_bias,
        down_weight,
        lowering_offset,
        second_gain,
        second_shift,
        channel_filter_scores,
        mask_noise,
    ):
        rows, width = tokens.shape
        seqs, slots = masked_positions.shape
        length = rows // seqs
        own_heads = channel_filter_scores.shape[0]
        depth = width // (2 * own_heads)
        scale = depth ** (-0.5)
        pairs = own_heads * depth // 128
        dp, tp = lax.axis_index("dp"), lax.axis_index("tp")
        bit = [(dp >> b) & 1 for b in range(bits)]
        quarter = 2 * bit[0] + bit[1]

        place = jnp.stack([tp, quarter, bit[0]]).astype(jnp.int32)

        def halves(a, axis, which):
            n = a.shape[axis] // 2
            return lax.dynamic_slice_in_dim(a, which * n, n, axis)

        def quarter_of(a, axis):
            n = a.shape[axis] // 4
            return lax.dynamic_slice_in_dim(a, quarter * n, n, axis)

        flow = Flow(n_dp)
        swap = flow.swap
        row = lambda v: v[None, :]
        projections = (query_weight, key_weight, value_weight)

        gate, *gate_parts = gates(flow, place, channel_filter_scores, mask_noise)
        far_gates = {}

        def gather_gate(p):
            near = gate_parts[p]
            got, due = swap(near, "tp")
            (near,) = yield [got], due, [near]
            (beside, due), (over, _) = swap(near, 1), swap(near, 0)
            beside, over = yield [beside, over], due, []
            corner, due = swap(beside, 0)
            (corner,) = yield [corner], due, []
            far_gates[p] = near, beside, over, corner

        far_weights = {}

        def gather_weight(n, mine):
            near, due = swap(mine, "tp")
            (near,) = yield [near], due, [mine]
            (beside, due), (over, _) = swap(near, 1), swap(near, 0)
            beside, over = yield [beside, over], due, []
            corner, due = swap(beside, 0)
            (corner,) = yield [corner], due, []
            far_weights[n] = near, beside, over, corner

        for p in range(pairs):
            flow.start(gather_gate(p))
        flow.start(gather_weight(0, quarter_of(up_weight, 1)))
        flow.start(gather_weight(1, quarter_of(down_weight, 0)))
        bias_far, _ = swap(up_bias, "tp")
        bias_far = row(bias_far)

        queries, keys, values = project(
            flow, tokens, projections, (query_bias, value_bias), scale
        )
        context, logsum = attend_own(flow, place, queries, keys, values, gate, length)
        earlier, logsums = [context], [[], logsum]
        for p in range(pairs):
            flow.wait(lambda: p in far_gates)
            context, part, far_gate = attend_far(
                flow, place, queries, keys, values, far_gates[p], p, pairs, earlier, length
            )
            logsums[0].append(part)
            earlier = [context, far_gate]

        order, picked, context_c, x, x_c, normed, inverse = first_norm(
            flow,
            masked_positions,
            context,
            tokens,
            output_weight,
            output_bias,
            first_gain,
            first_shift,
            length,
        )
        own_weights, own_bias = (up_weight, down_weight), row(up_bias)
        total, own_active, own_slope = forward(
            flow, place, x, own_weights, own_bias, None, length, slots
        )
        flow.wait(lambda: len(far_weights) == 2)
        far = [far_weights[n][r] for r in range(4) for n in range(2)]
        total, far_active, far_slope = forward(
            flow, place, x, far, bias_far, total, length, slots
        )
        vectors = [lowering_offset, first_gain, first_shift, second_gain, second_shift]
        layer_output, grad_second, grad_forward, sums_second = second_norm(
            flow, total, normed, cotangent, order, picked, vectors
        )

        def first_half(a, axis):
            return lax.slice_in_dim(a, 0, a.shape[axis] // 2, axis=axis)

        def last_half(a, axis):
            return lax.slice_in_dim(a, a.shape[axis] // 2, a.shape[axis], axis=axis)

        done = flow.done
        first_ways = tuple(range(1, bits))

        def split(a, way, axis, relative_axis):
            if way == 1 and relative_axis is not None:
                return first_half(a, relative_axis), last_half(a, relative_axis)
            return halves(a, axis, bit[way]), halves(a, axis, 1 - bit[way])

        def summed(mine, ways, axis, relative_axis):
            for way in ways:
                keep, send = split(mine, way, axis, relative_axis)
                got, due = swap(send, way)
                (got,) = yield [got], due, [send]
                mine = added(keep, got)
            return mine

        def core_sum(keep, send):
            got, due = swap(send, 0)
            (got,) = yield [got], due, [send]
            return keep, got

        def reduce_far(parts, keep, send):
            keep, got = yield from core_sum(keep, send)
            for name, pick, axis, relative_axis, before in parts:
                piece = added(pick(keep), pick(got))
                flow.start(send_far(name, piece, axis, relative_axis, before))

        def send_far(name, mine, axis, relative_axis, before):
            mine = yield from summed(mine, before, axis, relative_axis)
            got, due = swap(mine, "tp")
            (got,) = yield [got], due, [mine]
            done[name] = got

        def reduce_own(parts, keep, send):
            keep, got = yield from core_sum(keep, send)
            for name, pick, axis, relative_axis, before in parts:
                piece = added(pick(keep), pick(got))
                flow.start(rest_own(name, piece, axis, relative_axis, before))

        def rest_own(name, mine, axis, relative_axis, before):
            mine = yield from summed(mine, before, axis, relative_axis)
            (mine,) = yield [mine], name, []
            mine = added(mine, done[name])
            after = tuple(way for way in first_ways if way not in before)
            mine = yield from summed(mine, after[:-1], axis, relative_axis)
            got, due = swap(mine, after[-1])
            (got,) = yield [got], due, [mine]
            mine = added(mine, got)
            for way in reversed(before + after[:-1]):
                got, due = swap(mine, way)
                (got,) = yield [got], due, [mine]
                along = relative_axis if way == 1 and relative_axis is not None else axis
                mine = in_order(mine, got, bit[way], along)
            got, due = swap(mine, 0)
            (got,) = yield [got], due, [mine]
            done[name + " whole"] = (mine, got)

        def spread(name, axis):
            return in_order(*done[name + " whole"], bit[0], axis).astype(full)

        def whole(a):
            return a

        def add_vectors(name, mine):
            for way in ("tp",) + tuple(range(bits)):
                got, due = swap(mine, way)
                (got,) = yield [got], due + 5.0, [mine]
                mine = mine + got
            done[name] = mine

        def both(mine, theirs):
            return in_order(mine, theirs, tp, 0)

        def hidden_half(sums):
            by = [jnp.split(sums[0], 4)[r] for r in range(4)]
            return in_order(
                in_order(by[0], by[1], bit[1], 0), in_order(by[2], by[3], bit[1], 0), bit[0], 0
            )

        parts_down = [("down", whole, 0, 0, orders["down"])]
        parts_up = [("up", whole, 0, 1, orders["up"])]
        parts_qkv = [("qkv", whole, 0, None, orders["qkv"])]
        mask_pairs = [(0, pairs - 1), (pairs - 1, 1)]
        parts_mask = [
            ("mask" + str(n), whole, 2, 1, orders["mask" + str(n)]) for n in range(len(mask_pairs))
        ]

        back, down_send, down_keep, up_send, up_keep, far_sums = backward(
            flow, place, grad_forward, x_c, far, far_active, far_slope, None
        )
        flow.start(reduce_far(parts_down, down_keep, down_send))
        flow.start(reduce_far(parts_up, up_keep, up_send))
        back, down_send, down_keep, up_send, up_keep, own_sums = backward(
            flow, place, grad_forward, x_c, own_weights, own_active, own_slope, back
        )
        flow.start(reduce_own(parts_down, down_keep, down_send))
        flow.start(reduce_own(parts_up, up_keep, up_send))

        resid, grad_context, sums_first, own_keep, own_send, far_keep, far_send = first_back(
            flow,
            place,
            back,
            grad_second,
            normed,
            inverse,
            first_gain,
            output_weight,
            picked,
            context_c,
            length,
        )
        early = [both(hidden_half(own_sums), hidden_half(far_sums))]
        early += [sums_first[i] for i in range(3)] + [sums_second[i] for i in range(3)]
        def back_part(side, gate, p, masks, at, held, weights):
            logsum = logsums[0][p] if side else logsums[1]
            return attend_back(
                flow, place, queries, keys, values, grad_context, logsum, tokens, gate, side,
                length, scale, p, masks, at, held, weights,
            )

        sums_parts, grads = [[], []], []
        for side in (1, 0):
            begin = (reduce_own, reduce_far)[side]
            weights = ((own_keep, own_send), (far_keep, far_send))[side]
            masks = ()
            for p in range(pairs):
                first, many = [part for part in mask_pairs if part[0] <= p < sum(part)][0]
                grad, *masks, w_keep, w_send, part = back_part(
                    side, (gate, far_gate)[side], p, masks, p - first, 2 * many, weights
                )
                weights = (w_keep, w_send)
                grads.append((side, p * 128, grad))
                sums_parts[side].append(part)
                if p == first + many - 1:
                    number = mask_pairs.index((first, many))
                    flow.start(begin(parts_mask[number : number + 1], *masks))
                    masks = ()
            flow.start(begin(parts_qkv, *weights))
        sums_own, sums_far = (jnp.concatenate(part, 1) for part in sums_parts)
        vectors = early + [both(sums_own[i], sums_far[i]) for i in range(2)]
        flow.start(add_vectors("vectors", jnp.concatenate(vectors).reshape(-1, 128)))
        results = {}

        def tokens_part():
            results["tokens"] = input_grad(flow, place, resid, grads, projections)

        flow.fillers.append((7.0, tokens_part))
        masks = []

        def mask_part(p, mine, got):
            masks[:] = mask_grad(
                flow, place, channel_filter_scores, mask_noise, mine, got, 2 * mask_pairs[p][0],
                list(masks),
            )

        def watch():
            for p, (name, *_) in enumerate(parts_mask):
                pair = done.pop(name + " whole", None)
                if pair is not None:
                    flow.fillers.insert(0, (4.0, functools.partial(mask_part, p, *pair)))
            return not flow.tasks

        flow.wait(watch)
        for _, filler in flow.fillers:
            filler()
        down_grad, up_grad, qkv_grad = spread("down", 0), spread("up", 1), spread("qkv", 0)
        hidden_all = 2 * up_weight.shape[1]
        vectors = done["vectors"].reshape(-1)
        up_bias_grad = halves(vectors[:hidden_all], 0, tp)
        vectors = halves(vectors[hidden_all:].reshape(-1, width), 1, tp)
        fg, fs, ob, sg, ss, db, query_bias_grad, value_bias_grad = [vectors[i] for i in range(8)]

        group = own_heads * depth
        output_grad = qkv_grad[:, 3 * group :]
        by_pair = [jnp.split(part, 3, 1) for part in jnp.split(qkv_grad[:, : 3 * group], pairs, 1)]
        qkv_grads = [jnp.concatenate([part[n] for part in by_pair], 1) for n in range(3)]
        return (
            layer_output,
            results["tokens"],
            qkv_grads[0],
            query_bias_grad,
            qkv_grads[1],
            qkv_grads[2],
            value_bias_grad,
            output_grad,
            ob,
            fg,
            fs,
            up_grad,
            up_bias_grad,
            down_grad,
            db,
            sg,
            ss,
            masks[0],
        )

    return local


def solution(mesh):
    in_specs = (
        P(("dp", "tp"), None),
        P(("dp", "tp"), None),
        P(("dp", "tp"), None),
        P(),
        P(),
        P(),
        P(),
        P(),
        P(),
        P(),
        P(),
        P(),
        P(None, "tp"),
        P("tp"),
        P("tp", None),
        P(),
        P(),
        P(),
        P("tp", None, None),
        P("tp", None, None),
    )
    out_specs = (
        P(("dp", "tp"), None),
        P(("dp", "tp"), None),
        P(None, "tp"),
        P("tp"),
        P(None, "tp"),
        P(None, "tp"),
        P("tp"),
        P(None, "tp"),
        P("tp"),
        P("tp"),
        P("tp"),
        P(None, "tp"),
        P("tp"),
        P("tp", None),
        P("tp"),
        P("tp"),
        P("tp"),
        P("tp", None, None),
    )
    local = make_local(mesh.shape["dp"])
    return jax.shard_map(local, mesh=mesh, in_specs=in_specs, out_specs=out_specs, check_vma=False)
```

```python
import functools

import jax
import jax.numpy as jnp
from jax import lax
from jax.experimental import pallas as pl
from jax.experimental.pallas import tpu as pltpu
from jax.sharding import PartitionSpec as P

heat = 0.6
epsilon = 1e-06
low = jnp.bfloat16
full = jnp.float32
MIB = 1 << 20
vmem_mib = 32
kernel_flops = 8_000_000_000
early, late = 0.0, 1.0


orders = {
    "down": (1,),
    "mask0": (2,),
    "mask1": (1,),
    "qkv": (),
    "up": (1, 2),
}


def dot(left, right, left_dim=1, right_dim=0):
    return lax.dot_general(
        left, right, (((left_dim,), (right_dim,)), ((), ())), preferred_element_type=full
    )


def shape(dims, kind):
    return jax.ShapeDtypeStruct(dims, kind)


class Flow:
    def __init__(self, n_dp):
        self.n_dp = n_dp
        self.token = None
        self.sends = []
        self.tasks = []
        self.done = {}
        self.now = 0.0
        self.free = {}
        self.started = False
        self.fillers = []

    def call(
        self, kernel, name, grid, places, args, in_specs, out_shape, out_specs,
        us, aliases=None, scratch=(), spaces="", out_spaces="", polled=True,
    ):
        if self.token is not None and polled:
            self.poll()
        self.now += us
        after = ([] if self.token is None else [self.token]) + self.sends
        self.sends = []
        place_of = {"v": pltpu.VMEM, "h": pltpu.HBM}
        args = [
            pltpu.with_memory_space_constraint(a, place_of[c]) if c in place_of else a
            for a, c in zip(args, spaces, strict=True)
        ]
        out_shape = [
            place_of[c](a.shape, a.dtype) if c in place_of else a
            for a, c in zip(out_shape, out_spaces, strict=True)
        ]
        first, many, outs = len(places) + len(args), len(after), len(out_shape)

        def run(*refs):
            refs = refs[:first] + refs[first + many :]
            kernel(*refs[: first + outs], *refs[first + outs + 1 :])
            refs[first + outs][...] = jnp.zeros((8, 128), full)

        result = pl.pallas_call(
            run,
            grid_spec=pltpu.PrefetchScalarGridSpec(
                num_scalar_prefetch=len(places),
                grid=grid,
                in_specs=list(in_specs) + [pl.BlockSpec(memory_space=pl.ANY)] * many,
                out_specs=list(out_specs) + [pl.BlockSpec((8, 128), lambda *_: (0, 0))],
                scratch_shapes=list(scratch),
            ),
            out_shape=list(out_shape) + [shape((8, 128), full)],
            input_output_aliases=aliases or {},
            compiler_params=pltpu.CompilerParams(vmem_limit_bytes=vmem_mib * MIB),
            cost_estimate=pl.CostEstimate(
                flops=kernel_flops, bytes_accessed=1, transcendentals=0
            ),
            name=name,
        )(*places, *args, *after)
        self.token = result[-1]
        return result[:-1]

    def pin(self, arrays):
        arrays = [self.token, *arrays]
        anywhere = [pl.BlockSpec(memory_space=pl.ANY)] * len(arrays)

        def run(*refs):
            pass

        self.token, *arrays = pl.pallas_call(
            run,
            in_specs=anywhere,
            out_specs=anywhere,
            out_shape=[shape(a.shape, a.dtype) for a in arrays],
            input_output_aliases={i: i for i in range(len(arrays))},
            compiler_params=pltpu.CompilerParams(vmem_limit_bytes=MIB),
            cost_estimate=pl.CostEstimate(flops=1, bytes_accessed=1, transcendentals=0),
            name="turn",
        )(*arrays)
        return arrays

    def swap(self, a, way):
        if way == "tp":
            got = lax.ppermute(a, "tp", [(0, 1), (1, 0)])
        else:
            got = lax.ppermute(a, "dp", [(i, i ^ (1 << way)) for i in range(self.n_dp)])
        kilobytes = a.size * a.dtype.itemsize / 1e3
        rate, delay = (400.0, 2.0) if way == 0 else (22.0, 3.5) if way == 3 else (44.0 if self.now > 70 else 38.0, 2.5)
        link = 2 if way == 3 else way
        self.now += 0.8 if self.started and way else 1.4 if way else 0.5
        self.started = self.started or way != 0
        self.free[link] = max(self.free.get(link, 0.0), self.now) + kilobytes / rate
        return got, self.free[link] + delay

    def start(self, task):
        self.tasks.append([task, *self.advance(task, None)])

    def advance(self, task, values):
        try:
            arrays, due, sends = task.send(values)
        except StopIteration:
            return [], None
        self.sends += sends
        self.now += 0.5
        return arrays, due

    def is_due(self, entry, slack):
        due = entry[2]
        return due in self.done if isinstance(due, str) else due <= self.now + slack

    def poll(self, slack=early):
        due = [entry for entry in self.tasks if self.is_due(entry, slack)]
        if not due:
            return
        for entry in due:
            if not isinstance(entry[2], str):
                self.now = max(self.now, entry[2])
        arrays = self.pin([a for entry in due for a in entry[1]])
        self.now += 0.5
        self.started = False
        for entry in due:
            mine, arrays = arrays[: len(entry[1])], arrays[len(entry[1]) :]
            entry[1:] = self.advance(entry[0], mine)
        self.tasks = [entry for entry in self.tasks if entry[1]]

    def wait(self, ready, slack=late):
        while not ready():
            if self.fillers and self.fillers[0][0] < 5.0:
                self.fillers.pop(0)[1]()
            if any(self.is_due(entry, 0.0) for entry in self.tasks):
                self.poll(slack)
                continue
            soonest = min(e[2] for e in self.tasks if not isinstance(e[2], str))
            fits = [n for n, (us, _) in enumerate(self.fillers) if us <= soonest - self.now + 2.0]
            if fits:
                self.fillers.pop(fits[0])[1]()
                continue
            self.now = max(self.now, soonest)
            self.poll(slack)


def head_lanes(width):
    lane = lax.broadcasted_iota(jnp.int32, (1, width), 1)
    first = lane < width // 2
    return first, (first.astype(full).astype(low), (1.0 - first.astype(full)).astype(low))


def quarter_rows(place, length, s, r):
    part = length // 4
    return pl.ds(pl.multiple_of(s * length + (place[1] ^ r) * part, part), part)


def rows_of(ref, place, length, s):
    return jnp.concatenate([ref[quarter_rows(place, length, s, r), :] for r in range(4)], 0)


def write_rows(ref, value, place, length, s):
    part = length // 4
    for r in range(4):
        ref[quarter_rows(place, length, s, r), :] = value[r * part : (r + 1) * part]


def attend_kernel(place, q_ref, k_ref, v_ref, *rest, length, add):
    gates, (context_ref, logsum_ref) = rest[:4], rest[-2:]
    first, lanes = head_lanes(q_ref.shape[1])
    levels = [jnp.concatenate([g[h] for g in gates], 0) for h in range(2)]
    for s in range(q_ref.shape[0] // length):
        queries = rows_of(q_ref, place, length, s)
        keys = k_ref[s * length : (s + 1) * length, :]
        values = v_ref[s * length : (s + 1) * length, :]
        mixed, logs = [], []
        for h in range(2):
            scores = dot(queries * lanes[h], keys, 1, 1)
            peak = jnp.max(scores, -1, keepdims=True)
            expo = jnp.exp(scores - peak)
            total = jnp.sum(expo, -1, keepdims=True)
            weights = (expo * levels[h].astype(full)).astype(low)
            mixed.append(dot(weights, values) * (1.0 / total))
            logs.append(peak + jnp.log(total))
        write_rows(context_ref, jnp.where(first, mixed[0], mixed[1]).astype(low), place, length, s)
        here = 2 * pl.program_id(0) if add else 0
        lane = lax.broadcasted_iota(jnp.int32, first.shape, 1)
        columns = jnp.where(lane == here, logs[0], jnp.where(lane == here + 1, logs[1], 0.0))
        for r in range(4):
            rows = quarter_rows(place, length, s, r)
            part = columns[r * (length // 4) : (r + 1) * (length // 4)]
            if add:

                @pl.when(pl.program_id(0) == 0)
                def _():
                    logsum_ref[rows, :] = part

                @pl.when(pl.program_id(0) > 0)
                def _():
                    logsum_ref[rows, :] += part

            else:
                logsum_ref[rows, :] = part


def gate_specs(own, part, length, begin=0):
    if own:
        return [
            pl.BlockSpec((2, part, length), lambda hp, place, r=r: (begin + hp, place[1] ^ r, 0))
            for r in range(4)
        ]
    return [
        pl.BlockSpec((2, part, length), lambda hp, place, r=r: (begin + hp, r, 0)) for r in range(4)
    ]


def head_columns(rows, lanes, side, pairs, first=0):
    return pl.BlockSpec(
        (rows, lanes), lambda hp, place: (0, (place[0] ^ side) * pairs + first + hp)
    )


def attend_own(flow, place, queries, keys, values, gate, length):
    rows, width = queries.shape
    pairs, part = gate.shape[0] // 2, length // 4
    column = head_columns(rows, 128, 0, pairs)
    return flow.call(
        functools.partial(attend_kernel, length=length, add=True),
        "attend_own",
        (pairs,),
        [place],
        [queries, keys, values] + [gate] * 4,
        [column] * 3 + gate_specs(True, part, length),
        [shape((rows, width), low), shape((rows, 128), full)],
        [column, pl.BlockSpec((rows, 128), lambda hp, place: (0, 0))],
        spaces="hhhhhhh",
        out_spaces="hh",
        us=8.7,
    )


def attend_far_kernel(place, q_ref, k_ref, v_ref, *rest, length):
    gates, outs = rest[:4], rest[-3:]
    attend_kernel(place, q_ref, k_ref, v_ref, *gates, *outs[:2], length=length, add=False)
    part = length // 4
    for r in range(4):
        outs[2][:, r * part : (r + 1) * part, :] = gates[r][...]


def attend_far(flow, place, queries, keys, values, gates, pair, pairs, earlier, length):
    rows, width = queries.shape
    column = head_columns(rows, 128, 1, pairs, pair)
    return flow.call(
        functools.partial(attend_far_kernel, length=length),
        "attend_far",
        (1,),
        [place],
        [queries, keys, values, *gates, *earlier],
        [column] * 3
        + [pl.BlockSpec(g.shape, lambda hp, place: (0, 0, 0)) for g in gates]
        + [pl.BlockSpec(memory_space=pl.ANY)] * len(earlier),
        [
            shape((rows, width), low),
            shape((rows, 128), full),
            shape((2 * pairs, length, length), low),
        ],
        [
            column,
            pl.BlockSpec((rows, 128), lambda hp, place: (0, 0)),
            pl.BlockSpec((2, length, length), lambda hp, place: (pair, 0, 0)),
        ],
        aliases=dict(zip((8, 9), (0, 2))) if len(earlier) == 2 else {8: 0},
        spaces="hhh----" + "h" * len(earlier),
        out_spaces="hhh",
        us=5.3,
    )


def attend_back_kernel(place, q_ref, k_ref, v_ref, d_ref, logsum_ref, tokens_ref, *rest, length, scale, lane):
    gates = rest[:4]
    grads_ref, keep_ref, send_ref, keep_w, send_w, sums_ref = rest[-6:]
    hp = pl.program_id(0)
    group = grads_ref.shape[1] // 3
    width = q_ref.shape[1]
    part = length // 4
    first, lanes = head_lanes(width)
    levels = [jnp.concatenate([g[h] for g in gates], 0) for h in range(2)]
    masks = [None, None]
    sums_q = sums_v = 0.0
    for s in range(q_ref.shape[0] // length):
        here = slice(s * length, (s + 1) * length)
        queries, grads = rows_of(q_ref, place, length, s), rows_of(d_ref, place, length, s)
        logs = rows_of(logsum_ref, place, length, s)[:, lane : lane + 2]
        keys, values = k_ref[here, :], v_ref[here, :]
        totals = None
        for h in range(2):
            own_q, own_d, own_k = queries * lanes[h], grads * lanes[h], keys * lanes[h]
            sloped, weighted, produced = [], [], []
            for c in range(0, length, 128):
                tile = slice(c, c + 128)
                probs = jnp.exp(dot(own_q[tile], keys, 1, 1) - logs[tile, h : h + 1])
                product = dot(own_d[tile], values, 1, 1) * probs
                level = levels[h][tile].astype(full)
                gated = product * level
                rest = jnp.sum(gated, -1, keepdims=True)
                sloped.append((gated - probs * rest).astype(low))
                weighted.append((probs * level).astype(low))
                produced.append(product)
            slopes, weights = jnp.concatenate(sloped, 0), jnp.concatenate(weighted, 0)
            product = jnp.concatenate(produced, 0)
            masks[h] = product if masks[h] is None else masks[h] + product
            new = (dot(slopes, own_k), dot(own_q, slopes, 0, 0).T, dot(own_d, weights, 0, 0).T)
            totals = new if totals is None else tuple(a + b for a, b in zip(totals, new))
        grad_q, grad_k, grad_v = (
            (totals[0] * scale).astype(low),
            totals[1].astype(low),
            totals[2].astype(low),
        )
        for n, grad in enumerate((grad_q, grad_k, grad_v)):
            at = pl.ds(pl.multiple_of(n * group + hp * width, width), width)
            if n == 0:
                for r in range(4):
                    rows = quarter_rows(place, length, s, r)
                    grads_ref[rows, at] = grad[r * part : (r + 1) * part]
            else:
                grads_ref[here, at] = grad
        sums_q += jnp.sum(grad_q.astype(full), 0, keepdims=True)
        sums_v += jnp.sum(grad_v.astype(full), 0, keepdims=True)
    for h in range(2):
        mask = masks[h].astype(low)
        keep_ref[h] = mask[: 2 * part]
        send_ref[h] = mask[2 * part :]
    sums_ref[...] = jnp.concatenate([sums_q, sums_v, jnp.zeros((6, width), full)], 0)
    half = tokens_ref.shape[1] // 2
    for n in range(3):
        at = pl.ds(pl.multiple_of(n * group + hp * width, width), width)
        grad = grads_ref[:, at]
        for r, ref in enumerate((keep_w, send_w)):
            rows = tokens_ref[:, pl.ds(pl.multiple_of((place[2] ^ r) * half, half), half)]
            ref[:, n * width : (n + 1) * width] = dot(rows, grad, 0, 0).astype(low)


def attend_back(
    flow, place, queries, keys, values, grad_context, logsum, tokens, gate, side, length,
    scale, begin, masks, at, heads_held, weights,
):
    rows, width = queries.shape
    heads, part, lanes = gate.shape[0], length // 4, 128
    pairs = heads // 2
    column = head_columns(rows, lanes, side, pairs, begin)
    group = lanes
    mask = pl.BlockSpec((2, length // 2, length), lambda hp, place: (at, 0, 0))
    anywhere = [pl.BlockSpec(memory_space=pl.ANY)]
    held = [*weights, *masks]
    aliases = {11: 3, 12: 4}
    if masks:
        aliases.update({13: 1, 14: 2})
    return flow.call(
        functools.partial(
            attend_back_kernel, length=length, scale=scale, lane=0 if side else 2 * begin
        ),
        "attend_back",
        (1,),
        [place],
        [queries, keys, values, grad_context, logsum, tokens] + [gate] * 4 + held,
        [column] * 4
        + [pl.BlockSpec(logsum.shape, lambda hp, place: (0, 0))]
        + [pl.BlockSpec(tokens.shape, lambda hp, place: (0, 0))]
        + gate_specs(side == 0, part, length, begin)
        + anywhere * len(held),
        [shape((rows, 3 * group), low)]
        + [shape((heads_held, length // 2, length), low)] * 2
        + [shape(weights[0].shape, low)] * 2
        + [shape((8, group), full)],
        [pl.BlockSpec((rows, 3 * group), lambda hp, place: (0, 0))]
        + [mask] * 2
        + [pl.BlockSpec((width // 2, 3 * lanes), lambda hp, place: (0, begin))] * 2
        + [pl.BlockSpec((8, lanes), lambda hp, place: (0, hp))],
        aliases=aliases,
        spaces="hhh-h-" + "h" * 4 + "-" * len(held),
        out_spaces="h-----",
        us=8.8,
    )


def norm_forward(hidden, gain, shift):
    centre = hidden - jnp.mean(hidden, -1, keepdims=True)
    spread = jnp.mean(centre * centre, -1, keepdims=True)
    inverse = lax.rsqrt(spread + epsilon)
    normed = centre * inverse
    return normed * gain + shift, normed, inverse


def norm_backward(incoming, normed, inverse, gain):
    scaled = incoming * gain
    return inverse * (
        scaled
        - jnp.mean(scaled, -1, keepdims=True)
        - normed * jnp.mean(scaled * normed, -1, keepdims=True)
    )


def add_rows(ref, rows):
    packed = jnp.concatenate(
        [jnp.sum(row, 0, keepdims=True) for row in rows]
        + [jnp.zeros((8 - len(rows), ref.shape[1]), full)],
        0,
    )

    @pl.when(pl.program_id(0) == 0)
    def _():
        ref[...] = packed

    @pl.when(pl.program_id(0) > 0)
    def _():
        ref[...] += packed


def first_norm_kernel(
    slots_ref, context_ref, tokens_ref, weight_ref, bias_ref, gain_ref, shift_ref,
    order_ref, picked_ref, compact_ref, low_ref, kept_ref, normed_ref, inverse_ref,
):
    length, slots = tokens_ref.shape[0], slots_ref.shape[-1]
    position = lax.broadcasted_iota(jnp.int32, (length, slots), 0)
    hit = (position == slots_ref[pl.ds(pl.program_id(0), 1), :]).astype(full)
    chosen = jnp.max(hit, -1, keepdims=True)
    row = lax.broadcasted_iota(jnp.int32, (length, length), 0)
    column = lax.broadcasted_iota(jnp.int32, (length, length), 1)
    lower = (column <= row).astype(full).astype(low)
    upto = dot(lower, jnp.broadcast_to(chosen, (length, 128)).astype(low))[:, :1]
    count = jnp.sum(chosen, 0, keepdims=True)
    at = lax.broadcasted_iota(jnp.int32, (length, 1), 0).astype(full)
    target = jnp.where(chosen > 0, upto - 1.0, count + at - upto)
    order = (column.astype(full) == target).astype(full)
    picked_ref[...] = (order * chosen)[:, :slots].astype(low)
    order = order.astype(low)
    order_ref[...] = order
    context = dot(order, context_ref[...], 0, 0).astype(low)
    tokens = dot(order, tokens_ref[...], 0, 0)
    compact_ref[...] = context[:slots]
    attention = dot(context, weight_ref[...]) + bias_ref[...]
    out, normed, inverse = norm_forward(tokens + attention, gain_ref[...], shift_ref[...])
    out = out.astype(low)
    low_ref[...] = out
    kept_ref[...] = out[:slots]
    normed_ref[...] = normed
    inverse_ref[...] = jnp.broadcast_to(inverse[:slots], (slots, 128))


def by_seq(n, w):
    return pl.BlockSpec((n, w), lambda s: (s, 0))


def whole_of(a):
    return pl.BlockSpec(a.shape, lambda *_: (0,) * a.ndim)


def first_norm(flow, positions, context, tokens, weight, bias, gain, shift, length):
    rows, width = tokens.shape
    seqs, slots = positions.shape
    vectors = [weight, bias, gain, shift]
    return flow.call(
        first_norm_kernel,
        "first_norm",
        (seqs,),
        [],
        [positions, context, tokens, *vectors],
        [
            whole_of(positions),
            by_seq(length, width),
            by_seq(length, width),
        ]
        + [whole_of(v) for v in vectors],
        [
            shape((rows, length), low),
            shape((rows, slots), low),
            shape((seqs * slots, width), low),
            shape((rows, width), low),
            shape((seqs * slots, width), low),
            shape((rows, width), full),
            shape((seqs * slots, 128), full),
        ],
        [
            by_seq(length, length),
            by_seq(length, slots),
            by_seq(slots, width),
            by_seq(length, width),
            by_seq(slots, width),
            by_seq(length, width),
            by_seq(slots, 128),
        ],
        spaces="-h-----",
        out_spaces="-------",
        us=9,
    )


def gelu_parts(hidden):
    size = jnp.abs(hidden)
    t = 1.0 / (1.0 + (0.3275911 * 0.7071067811865476) * size)
    poly = 1.061405429 * t - 1.453152027
    poly = poly * t + 1.421413741
    poly = poly * t - 0.284496736
    poly = poly * t + 0.254829592
    bell = jnp.exp(hidden * hidden * -0.5)
    tail = 0.5 * poly * t * bell
    below = jnp.where(hidden > 0, 1.0 - tail, tail)
    return below, bell


def far_pieces(place, pieces, held, sems, order):
    i = pl.program_id(0)
    part = pieces[0][0].shape[1]
    along = place[1] & 1

    def copies(n):
        for x in range(2):
            up, down = pieces[2 * order[n] + x]
            at = pl.ds(pl.multiple_of((along ^ x) * part, part), part)
            yield pltpu.make_async_copy(up, held[0].at[n, :, at], sems.at[n, 2 * x])
            yield pltpu.make_async_copy(down, held[1].at[n, at, :], sems.at[n, 2 * x + 1])

    @pl.when(i == 0)
    def _():
        for n in range(2):
            for copy in copies(n):
                copy.start()

    for n in range(2):

        @pl.when(i == n)
        def _(n=n):
            for copy in copies(n):
                copy.wait()

    return held[0][i], held[1][i]


def forward_kernel(place, x_ref, *refs, own, length, slots):
    if own:
        (up_ref, down_ref, bias_ref, total_ref, active_ref, slope_ref) = refs
        up, down = up_ref[...], down_ref[...]
    else:
        pieces, refs = refs[:8], refs[8:]
        bias_ref, start_ref, total_ref, active_ref, slope_ref, *held, sems = refs
        pieces = [pieces[2 * r : 2 * r + 2] for r in range(4)]
        up, down = far_pieces(place, pieces, held, sems, (0, 1))

    @pl.when(pl.program_id(0) == 0)
    def _():
        total_ref[...] = jnp.zeros_like(total_ref) if own else start_ref[...]

    bias = bias_ref[...]
    step = 256
    for block in range(x_ref.shape[0] // slots):
        rows = slice(block * slots, (block + 1) * slots)
        s, part = divmod(block, length // slots)
        kept = slice(s * slots, (s + 1) * slots)
        x = x_ref[rows, :]
        parts = []
        for c in range(0, up.shape[1], step):
            hidden = dot(x, up[:, c : c + step]) + bias[:, c : c + step]
            below, bell = gelu_parts(hidden)
            active = (hidden * below).astype(low)
            parts.append(active)
            if part == 0:
                active_ref[kept, c : c + step] = active
                slope_ref[kept, c : c + step] = below + hidden * bell * 0.3989422804014327
        total_ref[rows, :] += dot(jnp.concatenate(parts, 1), down)


def own_specs(width, half, first):
    return [
        pl.BlockSpec((width, half), lambda i, place: (0, place[2] ^ i ^ first)),
        pl.BlockSpec((half, width), lambda i, place: (place[2] ^ i ^ first, 0)),
    ]


def far_scratch(width, half):
    return [
        pltpu.VMEM((2, width, half), low),
        pltpu.VMEM((2, half, width), low),
        pltpu.SemaphoreType.DMA((2, 4)),
    ]


def forward(flow, place, x, weights, bias, start, length, slots):
    rows, width = x.shape
    own = start is None
    half = bias.shape[1] // 2
    kept = rows // length * slots
    whole = pl.BlockSpec((rows, width), lambda i, place: (0, 0))
    wide = pl.BlockSpec((kept, half), lambda i, place: (0, i))
    anywhere = pl.BlockSpec(memory_space=pl.ANY)
    return flow.call(
        functools.partial(forward_kernel, own=own, length=length, slots=slots),
        "forward",
        (2,),
        [place],
        [x, *weights, bias] + ([] if own else [start]),
        [whole]
        + (own_specs(width, half, 0) if own else [anywhere] * 8)
        + [pl.BlockSpec((1, half), lambda i, place: (0, place[2] ^ i))]
        + ([] if own else [whole]),
        [shape((rows, width), full), shape((kept, 2 * half), low), shape((kept, 2 * half), full)],
        [whole, wide, wide],
        scratch=[] if own else far_scratch(width, half),
        spaces="----" if own else "-" * 11,
        out_spaces="-hh",
        us=14.5,
    )


def second_norm_kernel(
    total_ref, normed_ref, cotangent_ref, order_ref, picked_ref,
    offset_ref, gain1_ref, shift1_ref, gain2_ref, shift2_ref,
    out_ref, grad_ref, low_ref, sums_ref,
):
    slots = picked_ref.shape[1]
    first_out = normed_ref[...] * gain1_ref[...] + shift1_ref[...]
    gain = gain2_ref[...]
    out, normed, inverse = norm_forward(
        first_out + (total_ref[...] + offset_ref[...]), gain, shift2_ref[...]
    )
    out_ref[...] = dot(order_ref[...], out.astype(low)).astype(low)
    grad_out = dot(picked_ref[...], cotangent_ref[...], 0, 0)
    normed, inverse = normed[:slots], inverse[:slots]
    grad = norm_backward(grad_out, normed, inverse, gain)
    grad_ref[...] = grad
    low_ref[...] = grad.astype(low)
    add_rows(sums_ref, (grad_out * normed, grad_out, grad))


def second_norm(flow, total, normed, cotangent, order, picked, vectors):
    rows, width = total.shape
    length, slots = order.shape[1], picked.shape[1]
    seqs = rows // length
    return flow.call(
        second_norm_kernel,
        "second_norm",
        (seqs,),
        [],
        [total, normed, cotangent, order, picked, *vectors],
        [by_seq(length, width)] * 3
        + [by_seq(length, length), by_seq(length, slots)]
        + [whole_of(v) for v in vectors],
        [
            shape((rows, width), low),
            shape((seqs * slots, width), full),
            shape((seqs * slots, width), low),
            shape((8, width), full),
        ],
        [
            by_seq(length, width),
            by_seq(slots, width),
            by_seq(slots, width),
            pl.BlockSpec((8, width), lambda s: (0, 0)),
        ],
        spaces="-" * (5 + len(vectors)),
        out_spaces="----",
        us=6,
    )


def backward_kernel(place, grad_ref, x_ref, *refs, own):
    if own:
        (up_ref, down_ref, active_ref, slope_ref, start_ref), refs = refs[:5], refs[5:]
        up, down = up_ref[...], down_ref[...]
    else:
        pieces, (active_ref, slope_ref), refs = refs[:8], refs[8:10], refs[10:]
        refs, (*held, sems) = refs[:6], refs[6:]
        pieces = [pieces[2 * r : 2 * r + 2] for r in range(4)]
        up, down = far_pieces(place, pieces, held, sems, (1, 0))
    total_ref, down_send, down_keep, up_send, up_keep, sums_ref = refs
    i = pl.program_id(0)

    @pl.when(i == 0)
    def _():
        total_ref[...] = start_ref[...] if own else jnp.zeros_like(total_ref)

    grad = grad_ref[...]
    step = 256
    parts = []
    for c in range(0, up.shape[1], step):
        grad_active = dot(grad, down[c : c + step, :], 1, 1)
        grad_hidden = (grad_active * slope_ref[:, c : c + step]).astype(low)
        parts.append(grad_hidden)
        sums = jnp.sum(grad_hidden.astype(full), 0, keepdims=True)
        sums_ref[:, c : c + step] = jnp.broadcast_to(sums, (sums_ref.shape[0], step))
    grad_hidden = jnp.concatenate(parts, 1)
    total_ref[...] += dot(grad_hidden, up, 1, 1)
    down_grad = dot(active_ref[...], grad, 0, 0).astype(low)
    up_grad = dot(x_ref[...], grad_hidden, 0, 0).astype(low)

    @pl.when(i == 0)
    def _():
        down_send[...] = down_grad
        up_send[...] = up_grad

    @pl.when(i == 1)
    def _():
        down_keep[...] = down_grad
        up_keep[...] = up_grad


def backward(flow, place, grad, x, weights, active, slope, start):
    rows, width = grad.shape
    own = start is not None
    half = active.shape[1] // 2
    whole = pl.BlockSpec((rows, width), lambda i, place: (0, 0))
    wide = pl.BlockSpec((rows, half), lambda i, place: (0, i ^ 1))
    anywhere = pl.BlockSpec(memory_space=pl.ANY)
    down_part = pl.BlockSpec((half, width), lambda i, place: (0, 0))
    up_part = pl.BlockSpec((width, half), lambda i, place: (0, 0))
    return flow.call(
        functools.partial(backward_kernel, own=own),
        "backward",
        (2,),
        [place],
        [grad, x, *weights, active, slope] + ([start] if own else []),
        [whole, whole]
        + (own_specs(width, half, 1) if own else [anywhere] * 8)
        + [wide, wide]
        + ([whole] if own else []),
        [shape((rows, width), full)]
        + [shape((half, width), low)] * 2
        + [shape((width, half), low)] * 2
        + [shape((8, 2 * half), full)],
        [whole, down_part, down_part, up_part, up_part]
        + [pl.BlockSpec((8, half), lambda i, place: (0, i ^ 1))],
        scratch=[] if own else far_scratch(width, half),
        spaces="----hh-" if own else "-" * 10 + "hh",
        out_spaces="------",
        us=12,
    )


def first_back_kernel(
    place, total_ref, second_ref, normed_ref, inverse_ref, gain_ref, weight_ref, picked_ref,
    rows_ref, resid_ref, context_ref, sums_ref, *refs,
):
    s = pl.program_id(0)
    grad_refs, total_grads = refs[:4], refs[4:]
    grad_first = second_ref[...] + total_ref[...]
    normed = normed_ref[...]
    resid = norm_backward(grad_first, normed, inverse_ref[:, :1], gain_ref[...])
    upper = resid.astype(low)
    lower = (resid - upper.astype(full)).astype(low)
    picked = picked_ref[...]
    resid_ref[...] = dot(picked, upper) + dot(picked, lower)
    grad_context = dot(upper, weight_ref[...], 1, 1).astype(low)
    context_ref[...] = dot(picked, grad_context).astype(low)
    add_rows(sums_ref, (grad_first * normed, grad_first, resid))
    weight_grad = dot(rows_ref[...], upper, 0, 0)

    @pl.when(s == 0)
    def _():
        total_grads[0][...] = weight_grad

    @pl.when(s > 0)
    def _():
        total_grads[0][...] += weight_grad

    @pl.when(s == pl.num_programs(0) - 1)
    def _():
        half = weight_ref.shape[0] // 2
        for side in range(2):
            for r in range(2):
                down = pl.ds(pl.multiple_of((place[2] ^ r) * half, half), half)
                along = pl.ds(pl.multiple_of((place[0] ^ side) * half, half), half)
                grad_refs[2 * side + r][...] = total_grads[0][down, along].astype(low)


def first_back(flow, place, total, second, normed, inverse, gain, weight, picked, rows_c, length):
    rows, width = normed.shape
    slots = picked.shape[1]
    seqs, per_seq = rows // length, length // slots
    half = width // 2
    seq = lambda n, w: pl.BlockSpec((n, w), lambda s, place: (s, 0))
    fixed = lambda n, w: pl.BlockSpec((n, w), lambda s, place: (0, 0))
    return flow.call(
        first_back_kernel,
        "first_back",
        (seqs,),
        [place],
        [total, second, normed, inverse, gain, weight, picked, rows_c],
        [
            seq(slots, width),
            seq(slots, width),
            pl.BlockSpec((slots, width), lambda s, place: (s * per_seq, 0)),
            seq(slots, 128),
            whole_of(gain),
            whole_of(weight),
            seq(length, slots),
            seq(slots, width),
        ],
        [shape((rows, width), full), shape((rows, width), low), shape((8, width), full)]
        + [shape((half, 4 * half), low)] * 4,
        [seq(length, width), seq(length, width), fixed(8, width)]
        + [pl.BlockSpec((half, half), lambda s, place: (0, 3))] * 4,
        scratch=[pltpu.VMEM((width, width), full)],
        spaces="--------",
        out_spaces="h------",
        us=10,
    )


def project_kernel(tokens_ref, *refs, scale):
    weights, (bias_q, bias_v), outs = refs[:3], refs[3:5], refs[5:]
    tokens = tokens_ref[...]
    queries = (dot(tokens, weights[0][...]) + bias_q[...]).astype(low)
    outs[0][...] = (queries.astype(full) * scale).astype(low)
    outs[1][...] = dot(tokens, weights[1][...]).astype(low)
    outs[2][...] = (dot(tokens, weights[2][...]) + bias_v[...]).astype(low)


def project(flow, tokens, weights, biases, scale):
    rows, width = tokens.shape
    block = pl.BlockSpec((256, width), lambda i: (i, 0))
    return flow.call(
        functools.partial(project_kernel, scale=scale),
        "project",
        (rows // 256,),
        [],
        [tokens, *weights, *biases],
        [block] + [whole_of(v) for v in (*weights, *biases)],
        [shape((rows, width), low)] * 3,
        [block] * 3,
        spaces="-" * 6,
        out_spaces="hhh",
        us=8.5,
    )


def input_kernel(place, resid_ref, *refs, blocks):
    grads, weights, out_ref = refs[: len(blocks)], refs[len(blocks) : -1], refs[-1]
    total = resid_ref[...]
    for ref, (side, start, group) in zip(grads, blocks):
        for n in range(3):
            weight = weights[3 * side + n][:, start : start + group]
            total += dot(ref[:, n * group : (n + 1) * group], weight, 1, 1)
    out_ref[...] = total.astype(low)


def input_grad(flow, place, resid, parts, weights):
    rows, width = resid.shape
    half = width // 2
    block = pl.BlockSpec((256, width), lambda i, place: (i, 0))
    grads = [part[2] for part in parts]
    specs = [
        pl.BlockSpec((width, half), lambda i, place, side=side: (0, place[0] ^ side))
        for side in range(2)
        for n in range(3)
    ]
    return flow.call(
        functools.partial(
            input_kernel, blocks=[(side, start, g.shape[1] // 3) for side, start, g in parts]
        ),
        "input_grad",
        (rows // 256,),
        [place],
        [resid, *grads, *weights, *weights],
        [block]
        + [pl.BlockSpec((256, g.shape[1]), lambda i, place: (i, 0)) for g in grads]
        + specs,
        [shape((rows, width), low)],
        [block],
        spaces="h" * (1 + len(parts)) + "-" * 6,
        out_spaces="h",
        polled=False,
        us=12.3,
    )[0]


def gate_kernel(place, scores_ref, noise_ref, gate_ref, *parts):
    gate = jax.nn.sigmoid((scores_ref[...].astype(full) + noise_ref[...].astype(full)) / heat)
    gate_ref[...] = gate.astype(low)
    part = gate_ref.shape[1] // 4
    mine = pl.ds(pl.multiple_of(place[1] * part, part), part)
    for p, ref in enumerate(parts):

        @pl.when(pl.program_id(0) == p)
        def _(ref=ref):
            ref[...] = gate_ref[:, mine, :]


def gates(flow, place, scores, noise):
    heads, length, _ = scores.shape
    pairs, part = heads // 2, length // 4
    block = pl.BlockSpec((2, length, length), lambda i, place: (i, 0, 0))
    return flow.call(
        gate_kernel,
        "gates",
        (pairs,),
        [place],
        [scores, noise],
        [block, block],
        [shape(scores.shape, low)] + [shape((2, part, length), low)] * pairs,
        [block] + [pl.BlockSpec((2, part, length), lambda i, place: (0, 0, 0))] * pairs,
        spaces="--",
        out_spaces="h" + "-" * pairs,
        us=5.5,
    )


def mask_kernel(place, scores_ref, noise_ref, mine_ref, got_ref, *refs):
    out_ref = refs[-1]
    half = mine_ref.shape[1]
    for side, ref in enumerate((mine_ref, got_ref)):
        core = place[2] ^ side
        rows = pl.ds(pl.multiple_of(core * half, half), half)
        gate = jax.nn.sigmoid(
            (scores_ref[:, rows, :].astype(full) + noise_ref[:, rows, :].astype(full)) / heat
        )
        out_ref[:, rows, :] = ref[...].astype(full) * (gate * (1.0 - gate) / heat)


def mask_grad(flow, place, scores, noise, mine, got, begin, earlier):
    heads, length, _ = scores.shape
    block = pl.BlockSpec((1, length, length), lambda i, place: (begin + i, 0, 0))
    half = pl.BlockSpec((1, length // 2, length), lambda i, place: (i, 0, 0))
    return flow.call(
        mask_kernel,
        "mask_grad",
        (mine.shape[0],),
        [place],
        [scores, noise, mine, got, *earlier],
        [block, block, half, half] + [pl.BlockSpec(memory_space=pl.ANY)] * len(earlier),
        [shape(scores.shape, full)],
        [block],
        aliases={5: 0} if earlier else {},
        spaces="hh--" + "h" * len(earlier),
        out_spaces="h",
        polled=False,
        us=mine.shape[0],
    )


def make_local(n_dp):
    bits = n_dp.bit_length() - 1

    def added(a, b):
        return (a.astype(full) + b.astype(full)).astype(low)

    def in_order(mine, other, bit, axis):
        return jnp.concatenate(
            [jnp.where(bit == 0, mine, other), jnp.where(bit == 0, other, mine)], axis
        )

    def local(
        tokens,
        masked_positions,
        cotangent,
        query_weight,
        query_bias,
        key_weight,
        value_weight,
        value_bias,
        output_weight,
        output_bias,
        first_gain,
        first_shift,
        up_weight,
        up_bias,
        down_weight,
        lowering_offset,
        second_gain,
        second_shift,
        channel_filter_scores,
        mask_noise,
    ):
        rows, width = tokens.shape
        seqs, slots = masked_positions.shape
        length = rows // seqs
        own_heads = channel_filter_scores.shape[0]
        depth = width // (2 * own_heads)
        scale = depth ** (-0.5)
        pairs = own_heads * depth // 128
        dp, tp = lax.axis_index("dp"), lax.axis_index("tp")
        bit = [(dp >> b) & 1 for b in range(bits)]
        quarter = 2 * bit[0] + bit[1]

        place = jnp.stack([tp, quarter, bit[0]]).astype(jnp.int32)

        def halves(a, axis, which):
            n = a.shape[axis] // 2
            return lax.dynamic_slice_in_dim(a, which * n, n, axis)

        def quarter_of(a, axis):
            n = a.shape[axis] // 4
            return lax.dynamic_slice_in_dim(a, quarter * n, n, axis)

        flow = Flow(n_dp)
        swap = flow.swap
        row = lambda v: v[None, :]
        projections = (query_weight, key_weight, value_weight)

        gate, *gate_parts = gates(flow, place, channel_filter_scores, mask_noise)
        far_gates = {}

        def gather_gate(p):
            near = gate_parts[p]
            got, due = swap(near, "tp")
            (near,) = yield [got], due, [near]
            (beside, due), (over, _) = swap(near, 1), swap(near, 0)
            beside, over = yield [beside, over], due, []
            corner, due = swap(beside, 0)
            (corner,) = yield [corner], due, []
            far_gates[p] = near, beside, over, corner

        far_weights = {}

        def gather_weight(n, mine):
            near, due = swap(mine, "tp")
            (near,) = yield [near], due, [mine]
            (beside, due), (over, _) = swap(near, 1), swap(near, 0)
            beside, over = yield [beside, over], due, []
            corner, due = swap(beside, 0)
            (corner,) = yield [corner], due, []
            far_weights[n] = near, beside, over, corner

        for p in range(pairs):
            flow.start(gather_gate(p))
        flow.start(gather_weight(0, quarter_of(up_weight, 1)))
        flow.start(gather_weight(1, quarter_of(down_weight, 0)))
        bias_far, _ = swap(up_bias, "tp")
        bias_far = row(bias_far)

        queries, keys, values = project(
            flow, tokens, projections, (query_bias, value_bias), scale
        )
        context, logsum = attend_own(flow, place, queries, keys, values, gate, length)
        earlier, logsums = [context], [[], logsum]
        for p in range(pairs):
            flow.wait(lambda: p in far_gates)
            context, part, far_gate = attend_far(
                flow, place, queries, keys, values, far_gates[p], p, pairs, earlier, length
            )
            logsums[0].append(part)
            earlier = [context, far_gate]

        order, picked, context_c, x, x_c, normed, inverse = first_norm(
            flow,
            masked_positions,
            context,
            tokens,
            output_weight,
            output_bias,
            first_gain,
            first_shift,
            length,
        )
        own_weights, own_bias = (up_weight, down_weight), row(up_bias)
        total, own_active, own_slope = forward(
            flow, place, x, own_weights, own_bias, None, length, slots
        )
        flow.wait(lambda: len(far_weights) == 2)
        far = [far_weights[n][r] for r in range(4) for n in range(2)]
        total, far_active, far_slope = forward(
            flow, place, x, far, bias_far, total, length, slots
        )
        vectors = [lowering_offset, first_gain, first_shift, second_gain, second_shift]
        layer_output, grad_second, grad_forward, sums_second = second_norm(
            flow, total, normed, cotangent, order, picked, vectors
        )

        def first_half(a, axis):
            return lax.slice_in_dim(a, 0, a.shape[axis] // 2, axis=axis)

        def last_half(a, axis):
            return lax.slice_in_dim(a, a.shape[axis] // 2, a.shape[axis], axis=axis)

        done = flow.done
        first_ways = tuple(range(1, bits))

        def split(a, way, axis, relative_axis):
            if way == 1 and relative_axis is not None:
                return first_half(a, relative_axis), last_half(a, relative_axis)
            return halves(a, axis, bit[way]), halves(a, axis, 1 - bit[way])

        def summed(mine, ways, axis, relative_axis):
            for way in ways:
                keep, send = split(mine, way, axis, relative_axis)
                got, due = swap(send, way)
                (got,) = yield [got], due, [send]
                mine = added(keep, got)
            return mine

        def core_sum(keep, send):
            got, due = swap(send, 0)
            (got,) = yield [got], due, [send]
            return keep, got

        def reduce_far(parts, keep, send):
            keep, got = yield from core_sum(keep, send)
            for name, pick, axis, relative_axis, before in parts:
                piece = added(pick(keep), pick(got))
                flow.start(send_far(name, piece, axis, relative_axis, before))

        def send_far(name, mine, axis, relative_axis, before):
            mine = yield from summed(mine, before, axis, relative_axis)
            got, due = swap(mine, "tp")
            (got,) = yield [got], due, [mine]
            done[name] = got

        def reduce_own(parts, keep, send):
            keep, got = yield from core_sum(keep, send)
            for name, pick, axis, relative_axis, before in parts:
                piece = added(pick(keep), pick(got))
                flow.start(rest_own(name, piece, axis, relative_axis, before))

        def rest_own(name, mine, axis, relative_axis, before):
            mine = yield from summed(mine, before, axis, relative_axis)
            (mine,) = yield [mine], name, []
            mine = added(mine, done[name])
            after = tuple(way for way in first_ways if way not in before)
            mine = yield from summed(mine, after[:-1], axis, relative_axis)
            got, due = swap(mine, after[-1])
            (got,) = yield [got], due, [mine]
            mine = added(mine, got)
            for way in reversed(before + after[:-1]):
                got, due = swap(mine, way)
                (got,) = yield [got], due, [mine]
                along = relative_axis if way == 1 and relative_axis is not None else axis
                mine = in_order(mine, got, bit[way], along)
            got, due = swap(mine, 0)
            (got,) = yield [got], due, [mine]
            done[name + " whole"] = (mine, got)

        def spread(name, axis):
            return in_order(*done[name + " whole"], bit[0], axis).astype(full)

        def whole(a):
            return a

        def add_vectors(name, mine):
            for way in ("tp",) + tuple(range(bits)):
                got, due = swap(mine, way)
                (got,) = yield [got], due + 5.0, [mine]
                mine = mine + got
            done[name] = mine

        def both(mine, theirs):
            return in_order(mine, theirs, tp, 0)

        def hidden_half(sums):
            return in_order(*jnp.split(sums[0], 2), bit[0], 0)

        parts_down = [("down", whole, 0, None, orders["down"])]
        parts_up = [("up", whole, 0, None, orders["up"])]
        parts_qkv = [("qkv", whole, 0, None, orders["qkv"])]
        mask_pairs = [(0, pairs - 1), (pairs - 1, 1)]
        parts_mask = [
            ("mask" + str(n), whole, 2, 1, orders["mask" + str(n)]) for n in range(len(mask_pairs))
        ]

        back, down_send, down_keep, up_send, up_keep, far_sums = backward(
            flow, place, grad_forward, x_c, far, far_active, far_slope, None
        )
        flow.start(reduce_far(parts_down, down_keep, down_send))
        flow.start(reduce_far(parts_up, up_keep, up_send))
        back, down_send, down_keep, up_send, up_keep, own_sums = backward(
            flow, place, grad_forward, x_c, own_weights, own_active, own_slope, back
        )
        flow.start(reduce_own(parts_down, down_keep, down_send))
        flow.start(reduce_own(parts_up, up_keep, up_send))

        resid, grad_context, sums_first, own_keep, own_send, far_keep, far_send = first_back(
            flow,
            place,
            back,
            grad_second,
            normed,
            inverse,
            first_gain,
            output_weight,
            picked,
            context_c,
            length,
        )
        early = [both(hidden_half(own_sums), hidden_half(far_sums))]
        early += [sums_first[i] for i in range(3)] + [sums_second[i] for i in range(3)]
        def back_part(side, gate, p, masks, at, held, weights):
            logsum = logsums[0][p] if side else logsums[1]
            return attend_back(
                flow, place, queries, keys, values, grad_context, logsum, tokens, gate, side,
                length, scale, p, masks, at, held, weights,
            )

        sums_parts, grads = [[], []], []
        for side in (1, 0):
            begin = (reduce_own, reduce_far)[side]
            weights = ((own_keep, own_send), (far_keep, far_send))[side]
            masks = ()
            for p in range(pairs):
                first, many = [part for part in mask_pairs if part[0] <= p < sum(part)][0]
                grad, *masks, w_keep, w_send, part = back_part(
                    side, (gate, far_gate)[side], p, masks, p - first, 2 * many, weights
                )
                weights = (w_keep, w_send)
                grads.append((side, p * 128, grad))
                sums_parts[side].append(part)
                if p == first + many - 1:
                    number = mask_pairs.index((first, many))
                    flow.start(begin(parts_mask[number : number + 1], *masks))
                    masks = ()
            flow.start(begin(parts_qkv, *weights))
        sums_own, sums_far = (jnp.concatenate(part, 1) for part in sums_parts)
        vectors = early + [both(sums_own[i], sums_far[i]) for i in range(2)]
        flow.start(add_vectors("vectors", jnp.concatenate(vectors).reshape(-1, 128)))
        results = {}

        def tokens_part():
            results["tokens"] = input_grad(flow, place, resid, grads, projections)

        flow.fillers.append((7.0, tokens_part))
        masks = []

        def mask_part(p, mine, got):
            masks[:] = mask_grad(
                flow, place, channel_filter_scores, mask_noise, mine, got, 2 * mask_pairs[p][0],
                list(masks),
            )

        def watch():
            for p, (name, *_) in enumerate(parts_mask):
                pair = done.pop(name + " whole", None)
                if pair is not None:
                    flow.fillers.insert(0, (4.0, functools.partial(mask_part, p, *pair)))
            return not flow.tasks

        flow.wait(watch)
        for _, filler in flow.fillers:
            filler()
        down_grad, up_grad, qkv_grad = spread("down", 0), spread("up", 1), spread("qkv", 0)
        hidden_all = 2 * up_weight.shape[1]
        vectors = done["vectors"].reshape(-1)
        up_bias_grad = halves(vectors[:hidden_all], 0, tp)
        vectors = halves(vectors[hidden_all:].reshape(-1, width), 1, tp)
        fg, fs, ob, sg, ss, db, query_bias_grad, value_bias_grad = [vectors[i] for i in range(8)]

        group = own_heads * depth
        output_grad = qkv_grad[:, 3 * group :]
        by_pair = [jnp.split(part, 3, 1) for part in jnp.split(qkv_grad[:, : 3 * group], pairs, 1)]
        qkv_grads = [jnp.concatenate([part[n] for part in by_pair], 1) for n in range(3)]
        return (
            layer_output,
            results["tokens"],
            qkv_grads[0],
            query_bias_grad,
            qkv_grads[1],
            qkv_grads[2],
            value_bias_grad,
            output_grad,
            ob,
            fg,
            fs,
            up_grad,
            up_bias_grad,
            down_grad,
            db,
            sg,
            ss,
            masks[0],
        )

    return local


def solution(mesh):
    in_specs = (
        P(("dp", "tp"), None),
        P(("dp", "tp"), None),
        P(("dp", "tp"), None),
        P(),
        P(),
        P(),
        P(),
        P(),
        P(),
        P(),
        P(),
        P(),
        P(None, "tp"),
        P("tp"),
        P("tp", None),
        P(),
        P(),
        P(),
        P("tp", None, None),
        P("tp", None, None),
    )
    out_specs = (
        P(("dp", "tp"), None),
        P(("dp", "tp"), None),
        P(None, "tp"),
        P("tp"),
        P(None, "tp"),
        P(None, "tp"),
        P("tp"),
        P(None, "tp"),
        P("tp"),
        P("tp"),
        P("tp"),
        P(None, "tp"),
        P("tp"),
        P("tp", None),
        P("tp"),
        P("tp"),
        P("tp"),
        P("tp", None, None),
    )
    local = make_local(mesh.shape["dp"])
    return jax.shard_map(local, mesh=mesh, in_specs=in_specs, out_specs=out_specs, check_vma=False)
```

```python
import functools

import jax
import jax.numpy as jnp
from jax import lax
from jax.experimental import pallas as pl
from jax.experimental.pallas import tpu as pltpu
from jax.sharding import PartitionSpec as P

heat = 0.6
epsilon = 1e-06
low = jnp.bfloat16
full = jnp.float32
MIB = 1 << 20
vmem_mib = 32
kernel_flops = 8_000_000_000
early, late = -2.0, 1.0


orders = {
    "down": (1,),
    "mask0": (2,),
    "mask1": (1,),
    "qkv": (),
    "up": (1, 2),
}


def dot(left, right, left_dim=1, right_dim=0):
    return lax.dot_general(
        left, right, (((left_dim,), (right_dim,)), ((), ())), preferred_element_type=full
    )


def shape(dims, kind):
    return jax.ShapeDtypeStruct(dims, kind)


class Flow:
    def __init__(self, n_dp):
        self.n_dp = n_dp
        self.token = None
        self.sends = []
        self.tasks = []
        self.done = {}
        self.now = 0.0
        self.free = {}
        self.started = False
        self.fillers = []

    def call(
        self, kernel, name, grid, places, args, in_specs, out_shape, out_specs,
        us, aliases=None, scratch=(), spaces="", out_spaces="", polled=True,
    ):
        if self.token is not None and polled:
            self.poll()
        self.now += us
        after = ([] if self.token is None else [self.token]) + self.sends
        self.sends = []
        place_of = {"v": pltpu.VMEM, "h": pltpu.HBM}
        args = [
            pltpu.with_memory_space_constraint(a, place_of[c]) if c in place_of else a
            for a, c in zip(args, spaces, strict=True)
        ]
        out_shape = [
            place_of[c](a.shape, a.dtype) if c in place_of else a
            for a, c in zip(out_shape, out_spaces, strict=True)
        ]
        first, many, outs = len(places) + len(args), len(after), len(out_shape)

        def run(*refs):
            refs = refs[:first] + refs[first + many :]
            kernel(*refs[: first + outs], *refs[first + outs + 1 :])
            refs[first + outs][...] = jnp.zeros((8, 128), full)

        result = pl.pallas_call(
            run,
            grid_spec=pltpu.PrefetchScalarGridSpec(
                num_scalar_prefetch=len(places),
                grid=grid,
                in_specs=list(in_specs) + [pl.BlockSpec(memory_space=pl.ANY)] * many,
                out_specs=list(out_specs) + [pl.BlockSpec((8, 128), lambda *_: (0, 0))],
                scratch_shapes=list(scratch),
            ),
            out_shape=list(out_shape) + [shape((8, 128), full)],
            input_output_aliases=aliases or {},
            compiler_params=pltpu.CompilerParams(vmem_limit_bytes=vmem_mib * MIB),
            cost_estimate=pl.CostEstimate(
                flops=kernel_flops, bytes_accessed=1, transcendentals=0
            ),
            name=name,
        )(*places, *args, *after)
        self.token = result[-1]
        return result[:-1]

    def pin(self, arrays):
        arrays = [self.token, *arrays]
        anywhere = [pl.BlockSpec(memory_space=pl.ANY)] * len(arrays)

        def run(*refs):
            pass

        self.token, *arrays = pl.pallas_call(
            run,
            in_specs=anywhere,
            out_specs=anywhere,
            out_shape=[shape(a.shape, a.dtype) for a in arrays],
            input_output_aliases={i: i for i in range(len(arrays))},
            compiler_params=pltpu.CompilerParams(vmem_limit_bytes=MIB),
            cost_estimate=pl.CostEstimate(flops=1, bytes_accessed=1, transcendentals=0),
            name="turn",
        )(*arrays)
        return arrays

    def swap(self, a, way):
        if way == "tp":
            got = lax.ppermute(a, "tp", [(0, 1), (1, 0)])
        else:
            got = lax.ppermute(a, "dp", [(i, i ^ (1 << way)) for i in range(self.n_dp)])
        kilobytes = a.size * a.dtype.itemsize / 1e3
        rate, delay = (400.0, 2.0) if way == 0 else (22.0, 3.5) if way == 3 else (44.0 if self.now > 70 else 38.0, 2.5)
        link = 2 if way == 3 else way
        self.now += 0.8 if self.started and way else 1.4 if way else 0.5
        self.started = self.started or way != 0
        self.free[link] = max(self.free.get(link, 0.0), self.now) + kilobytes / rate
        return got, self.free[link] + delay

    def start(self, task):
        self.tasks.append([task, *self.advance(task, None)])

    def advance(self, task, values):
        try:
            arrays, due, sends = task.send(values)
        except StopIteration:
            return [], None
        self.sends += sends
        self.now += 0.5
        return arrays, due

    def is_due(self, entry, slack):
        due = entry[2]
        return due in self.done if isinstance(due, str) else due <= self.now + slack

    def poll(self, slack=early):
        due = [entry for entry in self.tasks if self.is_due(entry, slack)]
        if not due:
            return
        for entry in due:
            if not isinstance(entry[2], str):
                self.now = max(self.now, entry[2])
        arrays = self.pin([a for entry in due for a in entry[1]])
        self.now += 0.5
        self.started = False
        for entry in due:
            mine, arrays = arrays[: len(entry[1])], arrays[len(entry[1]) :]
            entry[1:] = self.advance(entry[0], mine)
        self.tasks = [entry for entry in self.tasks if entry[1]]

    def wait(self, ready, slack=late):
        while not ready():
            if self.fillers and self.fillers[0][0] < 5.0:
                self.fillers.pop(0)[1]()
            if any(self.is_due(entry, 0.0) for entry in self.tasks):
                self.poll(slack)
                continue
            soonest = min(e[2] for e in self.tasks if not isinstance(e[2], str))
            fits = [n for n, (us, _) in enumerate(self.fillers) if us <= soonest - self.now + 2.0]
            if fits:
                self.fillers.pop(fits[0])[1]()
                continue
            self.now = max(self.now, soonest)
            self.poll(slack)


def head_lanes(width):
    lane = lax.broadcasted_iota(jnp.int32, (1, width), 1)
    first = lane < width // 2
    return first, (first.astype(full).astype(low), (1.0 - first.astype(full)).astype(low))


def quarter_rows(place, length, s, r):
    part = length // 4
    return pl.ds(pl.multiple_of(s * length + (place[1] ^ r) * part, part), part)


def rows_of(ref, place, length, s):
    return jnp.concatenate([ref[quarter_rows(place, length, s, r), :] for r in range(4)], 0)


def write_rows(ref, value, place, length, s):
    part = length // 4
    for r in range(4):
        ref[quarter_rows(place, length, s, r), :] = value[r * part : (r + 1) * part]


def attend_kernel(place, q_ref, k_ref, v_ref, *rest, length, add):
    gates, (context_ref, logsum_ref) = rest[:4], rest[-2:]
    first, lanes = head_lanes(q_ref.shape[1])
    levels = [jnp.concatenate([g[h] for g in gates], 0) for h in range(2)]
    for s in range(q_ref.shape[0] // length):
        queries = rows_of(q_ref, place, length, s)
        keys = k_ref[s * length : (s + 1) * length, :]
        values = v_ref[s * length : (s + 1) * length, :]
        mixed, logs = [], []
        for h in range(2):
            scores = dot(queries * lanes[h], keys, 1, 1)
            peak = jnp.max(scores, -1, keepdims=True)
            expo = jnp.exp(scores - peak)
            total = jnp.sum(expo, -1, keepdims=True)
            weights = (expo * levels[h].astype(full)).astype(low)
            mixed.append(dot(weights, values) * (1.0 / total))
            logs.append(peak + jnp.log(total))
        write_rows(context_ref, jnp.where(first, mixed[0], mixed[1]).astype(low), place, length, s)
        here = 2 * pl.program_id(0) if add else 0
        lane = lax.broadcasted_iota(jnp.int32, first.shape, 1)
        columns = jnp.where(lane == here, logs[0], jnp.where(lane == here + 1, logs[1], 0.0))
        for r in range(4):
            rows = quarter_rows(place, length, s, r)
            part = columns[r * (length // 4) : (r + 1) * (length // 4)]
            if add:

                @pl.when(pl.program_id(0) == 0)
                def _():
                    logsum_ref[rows, :] = part

                @pl.when(pl.program_id(0) > 0)
                def _():
                    logsum_ref[rows, :] += part

            else:
                logsum_ref[rows, :] = part


def gate_specs(own, part, length, begin=0):
    if own:
        return [
            pl.BlockSpec((2, part, length), lambda hp, place, r=r: (begin + hp, place[1] ^ r, 0))
            for r in range(4)
        ]
    return [
        pl.BlockSpec((2, part, length), lambda hp, place, r=r: (begin + hp, r, 0)) for r in range(4)
    ]


def head_columns(rows, lanes, side, pairs, first=0):
    return pl.BlockSpec(
        (rows, lanes), lambda hp, place: (0, (place[0] ^ side) * pairs + first + hp)
    )


def attend_own(flow, place, queries, keys, values, gate, length):
    rows, width = queries.shape
    pairs, part = gate.shape[0] // 2, length // 4
    column = head_columns(rows, 128, 0, pairs)
    return flow.call(
        functools.partial(attend_kernel, length=length, add=True),
        "attend_own",
        (pairs,),
        [place],
        [queries, keys, values] + [gate] * 4,
        [column] * 3 + gate_specs(True, part, length),
        [shape((rows, width), low), shape((rows, 128), full)],
        [column, pl.BlockSpec((rows, 128), lambda hp, place: (0, 0))],
        spaces="hhhhhhh",
        out_spaces="hh",
        us=8.7,
    )


def attend_far_kernel(place, q_ref, k_ref, v_ref, *rest, length):
    gates, outs = rest[:4], rest[-3:]
    attend_kernel(place, q_ref, k_ref, v_ref, *gates, *outs[:2], length=length, add=False)
    part = length // 4
    for r in range(4):
        outs[2][:, r * part : (r + 1) * part, :] = gates[r][...]


def attend_far(flow, place, queries, keys, values, gates, pair, pairs, earlier, length):
    rows, width = queries.shape
    column = head_columns(rows, 128, 1, pairs, pair)
    return flow.call(
        functools.partial(attend_far_kernel, length=length),
        "attend_far",
        (1,),
        [place],
        [queries, keys, values, *gates, *earlier],
        [column] * 3
        + [pl.BlockSpec(g.shape, lambda hp, place: (0, 0, 0)) for g in gates]
        + [pl.BlockSpec(memory_space=pl.ANY)] * len(earlier),
        [
            shape((rows, width), low),
            shape((rows, 128), full),
            shape((2 * pairs, length, length), low),
        ],
        [
            column,
            pl.BlockSpec((rows, 128), lambda hp, place: (0, 0)),
            pl.BlockSpec((2, length, length), lambda hp, place: (pair, 0, 0)),
        ],
        aliases=dict(zip((8, 9), (0, 2))) if len(earlier) == 2 else {8: 0},
        spaces="hhh----" + "h" * len(earlier),
        out_spaces="hhh",
        us=5.3,
    )


def attend_back_kernel(place, q_ref, k_ref, v_ref, d_ref, logsum_ref, tokens_ref, *rest, length, scale, lane):
    gates = rest[:4]
    grads_ref, keep_ref, send_ref, keep_w, send_w, sums_ref = rest[-6:]
    hp = pl.program_id(0)
    group = grads_ref.shape[1] // 3
    width = q_ref.shape[1]
    part = length // 4
    first, lanes = head_lanes(width)
    levels = [jnp.concatenate([g[h] for g in gates], 0) for h in range(2)]
    masks = [None, None]
    sums_q = sums_v = 0.0
    for s in range(q_ref.shape[0] // length):
        here = slice(s * length, (s + 1) * length)
        queries, grads = rows_of(q_ref, place, length, s), rows_of(d_ref, place, length, s)
        logs = rows_of(logsum_ref, place, length, s)[:, lane : lane + 2]
        keys, values = k_ref[here, :], v_ref[here, :]
        totals = None
        for h in range(2):
            own_q, own_d, own_k = queries * lanes[h], grads * lanes[h], keys * lanes[h]
            sloped, weighted, produced = [], [], []
            for c in range(0, length, 128):
                tile = slice(c, c + 128)
                probs = jnp.exp(dot(own_q[tile], keys, 1, 1) - logs[tile, h : h + 1])
                product = dot(own_d[tile], values, 1, 1) * probs
                level = levels[h][tile].astype(full)
                gated = product * level
                rest = jnp.sum(gated, -1, keepdims=True)
                sloped.append((gated - probs * rest).astype(low))
                weighted.append((probs * level).astype(low))
                produced.append(product)
            slopes, weights = jnp.concatenate(sloped, 0), jnp.concatenate(weighted, 0)
            product = jnp.concatenate(produced, 0)
            masks[h] = product if masks[h] is None else masks[h] + product
            new = (dot(slopes, own_k), dot(own_q, slopes, 0, 0).T, dot(own_d, weights, 0, 0).T)
            totals = new if totals is None else tuple(a + b for a, b in zip(totals, new))
        grad_q, grad_k, grad_v = (
            (totals[0] * scale).astype(low),
            totals[1].astype(low),
            totals[2].astype(low),
        )
        for n, grad in enumerate((grad_q, grad_k, grad_v)):
            at = pl.ds(pl.multiple_of(n * group + hp * width, width), width)
            if n == 0:
                for r in range(4):
                    rows = quarter_rows(place, length, s, r)
                    grads_ref[rows, at] = grad[r * part : (r + 1) * part]
            else:
                grads_ref[here, at] = grad
        sums_q += jnp.sum(grad_q.astype(full), 0, keepdims=True)
        sums_v += jnp.sum(grad_v.astype(full), 0, keepdims=True)
    for h in range(2):
        mask = masks[h].astype(low)
        keep_ref[h] = mask[: 2 * part]
        send_ref[h] = mask[2 * part :]
    sums_ref[...] = jnp.concatenate([sums_q, sums_v, jnp.zeros((6, width), full)], 0)
    half = tokens_ref.shape[1] // 2
    for n in range(3):
        at = pl.ds(pl.multiple_of(n * group + hp * width, width), width)
        grad = grads_ref[:, at]
        for r, ref in enumerate((keep_w, send_w)):
            rows = tokens_ref[:, pl.ds(pl.multiple_of((place[2] ^ r) * half, half), half)]
            ref[:, n * width : (n + 1) * width] = dot(rows, grad, 0, 0).astype(low)


def attend_back(
    flow, place, queries, keys, values, grad_context, logsum, tokens, gate, side, length,
    scale, begin, masks, at, heads_held, weights,
):
    rows, width = queries.shape
    heads, part, lanes = gate.shape[0], length // 4, 128
    pairs = heads // 2
    column = head_columns(rows, lanes, side, pairs, begin)
    group = lanes
    mask = pl.BlockSpec((2, length // 2, length), lambda hp, place: (at, 0, 0))
    anywhere = [pl.BlockSpec(memory_space=pl.ANY)]
    held = [*weights, *masks]
    aliases = {11: 3, 12: 4}
    if masks:
        aliases.update({13: 1, 14: 2})
    return flow.call(
        functools.partial(
            attend_back_kernel, length=length, scale=scale, lane=0 if side else 2 * begin
        ),
        "attend_back",
        (1,),
        [place],
        [queries, keys, values, grad_context, logsum, tokens] + [gate] * 4 + held,
        [column] * 4
        + [pl.BlockSpec(logsum.shape, lambda hp, place: (0, 0))]
        + [pl.BlockSpec(tokens.shape, lambda hp, place: (0, 0))]
        + gate_specs(side == 0, part, length, begin)
        + anywhere * len(held),
        [shape((rows, 3 * group), low)]
        + [shape((heads_held, length // 2, length), low)] * 2
        + [shape(weights[0].shape, low)] * 2
        + [shape((8, group), full)],
        [pl.BlockSpec((rows, 3 * group), lambda hp, place: (0, 0))]
        + [mask] * 2
        + [pl.BlockSpec((width // 2, 3 * lanes), lambda hp, place: (0, begin))] * 2
        + [pl.BlockSpec((8, lanes), lambda hp, place: (0, hp))],
        aliases=aliases,
        spaces="hhh-h-" + "h" * 4 + "-" * len(held),
        out_spaces="h-----",
        us=8.8,
    )


def norm_forward(hidden, gain, shift):
    centre = hidden - jnp.mean(hidden, -1, keepdims=True)
    spread = jnp.mean(centre * centre, -1, keepdims=True)
    inverse = lax.rsqrt(spread + epsilon)
    normed = centre * inverse
    return normed * gain + shift, normed, inverse


def norm_backward(incoming, normed, inverse, gain):
    scaled = incoming * gain
    return inverse * (
        scaled
        - jnp.mean(scaled, -1, keepdims=True)
        - normed * jnp.mean(scaled * normed, -1, keepdims=True)
    )


def add_rows(ref, rows):
    packed = jnp.concatenate(
        [jnp.sum(row, 0, keepdims=True) for row in rows]
        + [jnp.zeros((8 - len(rows), ref.shape[1]), full)],
        0,
    )

    @pl.when(pl.program_id(0) == 0)
    def _():
        ref[...] = packed

    @pl.when(pl.program_id(0) > 0)
    def _():
        ref[...] += packed


def first_norm_kernel(
    slots_ref, context_ref, tokens_ref, weight_ref, bias_ref, gain_ref, shift_ref,
    order_ref, picked_ref, compact_ref, low_ref, kept_ref, normed_ref, inverse_ref,
):
    length, slots = tokens_ref.shape[0], slots_ref.shape[-1]
    position = lax.broadcasted_iota(jnp.int32, (length, slots), 0)
    hit = (position == slots_ref[pl.ds(pl.program_id(0), 1), :]).astype(full)
    chosen = jnp.max(hit, -1, keepdims=True)
    row = lax.broadcasted_iota(jnp.int32, (length, length), 0)
    column = lax.broadcasted_iota(jnp.int32, (length, length), 1)
    lower = (column <= row).astype(full).astype(low)
    upto = dot(lower, jnp.broadcast_to(chosen, (length, 128)).astype(low))[:, :1]
    count = jnp.sum(chosen, 0, keepdims=True)
    at = lax.broadcasted_iota(jnp.int32, (length, 1), 0).astype(full)
    target = jnp.where(chosen > 0, upto - 1.0, count + at - upto)
    order = (column.astype(full) == target).astype(full)
    picked_ref[...] = (order * chosen)[:, :slots].astype(low)
    order = order.astype(low)
    order_ref[...] = order
    context = dot(order, context_ref[...], 0, 0).astype(low)
    tokens = dot(order, tokens_ref[...], 0, 0)
    compact_ref[...] = context[:slots]
    attention = dot(context, weight_ref[...]) + bias_ref[...]
    out, normed, inverse = norm_forward(tokens + attention, gain_ref[...], shift_ref[...])
    out = out.astype(low)
    low_ref[...] = out
    kept_ref[...] = out[:slots]
    normed_ref[...] = normed
    inverse_ref[...] = jnp.broadcast_to(inverse[:slots], (slots, 128))


def by_seq(n, w):
    return pl.BlockSpec((n, w), lambda s: (s, 0))


def whole_of(a):
    return pl.BlockSpec(a.shape, lambda *_: (0,) * a.ndim)


def first_norm(flow, positions, context, tokens, weight, bias, gain, shift, length):
    rows, width = tokens.shape
    seqs, slots = positions.shape
    vectors = [weight, bias, gain, shift]
    return flow.call(
        first_norm_kernel,
        "first_norm",
        (seqs,),
        [],
        [positions, context, tokens, *vectors],
        [
            whole_of(positions),
            by_seq(length, width),
            by_seq(length, width),
        ]
        + [whole_of(v) for v in vectors],
        [
            shape((rows, length), low),
            shape((rows, slots), low),
            shape((seqs * slots, width), low),
            shape((rows, width), low),
            shape((seqs * slots, width), low),
            shape((rows, width), full),
            shape((seqs * slots, 128), full),
        ],
        [
            by_seq(length, length),
            by_seq(length, slots),
            by_seq(slots, width),
            by_seq(length, width),
            by_seq(slots, width),
            by_seq(length, width),
            by_seq(slots, 128),
        ],
        spaces="-h-----",
        out_spaces="hhh-hhh",
        us=9,
    )


def gelu_parts(hidden):
    size = jnp.abs(hidden)
    t = 1.0 / (1.0 + (0.3275911 * 0.7071067811865476) * size)
    poly = 1.061405429 * t - 1.453152027
    poly = poly * t + 1.421413741
    poly = poly * t - 0.284496736
    poly = poly * t + 0.254829592
    bell = jnp.exp(hidden * hidden * -0.5)
    tail = 0.5 * poly * t * bell
    below = jnp.where(hidden > 0, 1.0 - tail, tail)
    return below, bell


def far_pieces(place, pieces, held, sems, order):
    i = pl.program_id(0)
    part = pieces[0][0].shape[1]
    along = place[1] & 1

    def copies(n):
        for x in range(2):
            up, down = pieces[2 * order[n] + x]
            at = pl.ds(pl.multiple_of((along ^ x) * part, part), part)
            yield pltpu.make_async_copy(up, held[0].at[n, :, at], sems.at[n, 2 * x])
            yield pltpu.make_async_copy(down, held[1].at[n, at, :], sems.at[n, 2 * x + 1])

    @pl.when(i == 0)
    def _():
        for n in range(2):
            for copy in copies(n):
                copy.start()

    for n in range(2):

        @pl.when(i == n)
        def _(n=n):
            for copy in copies(n):
                copy.wait()

    return held[0][i], held[1][i]


def forward_kernel(place, x_ref, *refs, own, length, slots):
    if own:
        (up_ref, down_ref, bias_ref, total_ref, active_ref, slope_ref) = refs
        up, down = up_ref[...], down_ref[...]
    else:
        pieces, refs = refs[:8], refs[8:]
        bias_ref, start_ref, total_ref, active_ref, slope_ref, *held, sems = refs
        pieces = [pieces[2 * r : 2 * r + 2] for r in range(4)]
        up, down = far_pieces(place, pieces, held, sems, (0, 1))

    @pl.when(pl.program_id(0) == 0)
    def _():
        total_ref[...] = jnp.zeros_like(total_ref) if own else start_ref[...]

    bias = bias_ref[...]
    step = 256
    for block in range(x_ref.shape[0] // slots):
        rows = slice(block * slots, (block + 1) * slots)
        s, part = divmod(block, length // slots)
        kept = slice(s * slots, (s + 1) * slots)
        x = x_ref[rows, :]
        parts = []
        for c in range(0, up.shape[1], step):
            hidden = dot(x, up[:, c : c + step]) + bias[:, c : c + step]
            below, bell = gelu_parts(hidden)
            active = (hidden * below).astype(low)
            parts.append(active)
            if part == 0:
                active_ref[kept, c : c + step] = active
                slope_ref[kept, c : c + step] = below + hidden * bell * 0.3989422804014327
        total_ref[rows, :] += dot(jnp.concatenate(parts, 1), down)


def own_specs(width, half, first):
    return [
        pl.BlockSpec((width, half), lambda i, place: (0, place[2] ^ i ^ first)),
        pl.BlockSpec((half, width), lambda i, place: (place[2] ^ i ^ first, 0)),
    ]


def far_scratch(width, half):
    return [
        pltpu.VMEM((2, width, half), low),
        pltpu.VMEM((2, half, width), low),
        pltpu.SemaphoreType.DMA((2, 4)),
    ]


def forward(flow, place, x, weights, bias, start, length, slots):
    rows, width = x.shape
    own = start is None
    half = bias.shape[1] // 2
    kept = rows // length * slots
    whole = pl.BlockSpec((rows, width), lambda i, place: (0, 0))
    wide = pl.BlockSpec((kept, half), lambda i, place: (0, i))
    anywhere = pl.BlockSpec(memory_space=pl.ANY)
    return flow.call(
        functools.partial(forward_kernel, own=own, length=length, slots=slots),
        "forward",
        (2,),
        [place],
        [x, *weights, bias] + ([] if own else [start]),
        [whole]
        + (own_specs(width, half, 0) if own else [anywhere] * 8)
        + [pl.BlockSpec((1, half), lambda i, place: (0, place[2] ^ i))]
        + ([] if own else [whole]),
        [shape((rows, width), full), shape((kept, 2 * half), low), shape((kept, 2 * half), full)],
        [whole, wide, wide],
        scratch=[] if own else far_scratch(width, half),
        spaces="----" if own else "-" * 11,
        out_spaces="-hh",
        us=14.5,
    )


def second_norm_kernel(
    total_ref, normed_ref, cotangent_ref, order_ref, picked_ref,
    offset_ref, gain1_ref, shift1_ref, gain2_ref, shift2_ref,
    out_ref, grad_ref, low_ref, sums_ref,
):
    slots = picked_ref.shape[1]
    first_out = normed_ref[...] * gain1_ref[...] + shift1_ref[...]
    gain = gain2_ref[...]
    out, normed, inverse = norm_forward(
        first_out + (total_ref[...] + offset_ref[...]), gain, shift2_ref[...]
    )
    out_ref[...] = dot(order_ref[...], out.astype(low)).astype(low)
    grad_out = dot(picked_ref[...], cotangent_ref[...], 0, 0)
    normed, inverse = normed[:slots], inverse[:slots]
    grad = norm_backward(grad_out, normed, inverse, gain)
    grad_ref[...] = grad
    low_ref[...] = grad.astype(low)
    add_rows(sums_ref, (grad_out * normed, grad_out, grad))


def second_norm(flow, total, normed, cotangent, order, picked, vectors):
    rows, width = total.shape
    length, slots = order.shape[1], picked.shape[1]
    seqs = rows // length
    return flow.call(
        second_norm_kernel,
        "second_norm",
        (seqs,),
        [],
        [total, normed, cotangent, order, picked, *vectors],
        [by_seq(length, width)] * 3
        + [by_seq(length, length), by_seq(length, slots)]
        + [whole_of(v) for v in vectors],
        [
            shape((rows, width), low),
            shape((seqs * slots, width), full),
            shape((seqs * slots, width), low),
            shape((8, width), full),
        ],
        [
            by_seq(length, width),
            by_seq(slots, width),
            by_seq(slots, width),
            pl.BlockSpec((8, width), lambda s: (0, 0)),
        ],
        spaces="-" * (5 + len(vectors)),
        out_spaces="----",
        us=6,
    )


def backward_kernel(place, grad_ref, x_ref, *refs, own):
    if own:
        (up_ref, down_ref, active_ref, slope_ref, start_ref), refs = refs[:5], refs[5:]
        up, down = up_ref[...], down_ref[...]
    else:
        pieces, (active_ref, slope_ref), refs = refs[:8], refs[8:10], refs[10:]
        refs, (*held, sems) = refs[:6], refs[6:]
        pieces = [pieces[2 * r : 2 * r + 2] for r in range(4)]
        up, down = far_pieces(place, pieces, held, sems, (1, 0))
    total_ref, down_send, down_keep, up_send, up_keep, sums_ref = refs
    i = pl.program_id(0)

    @pl.when(i == 0)
    def _():
        total_ref[...] = start_ref[...] if own else jnp.zeros_like(total_ref)

    grad = grad_ref[...]
    step = 256
    parts = []
    for c in range(0, up.shape[1], step):
        grad_active = dot(grad, down[c : c + step, :], 1, 1)
        grad_hidden = (grad_active * slope_ref[:, c : c + step]).astype(low)
        parts.append(grad_hidden)
        sums = jnp.sum(grad_hidden.astype(full), 0, keepdims=True)
        sums_ref[:, c : c + step] = jnp.broadcast_to(sums, (sums_ref.shape[0], step))
    grad_hidden = jnp.concatenate(parts, 1)
    total_ref[...] += dot(grad_hidden, up, 1, 1)
    down_grad = dot(active_ref[...], grad, 0, 0).astype(low)
    up_grad = dot(x_ref[...], grad_hidden, 0, 0).astype(low)

    @pl.when(i == 0)
    def _():
        down_send[...] = down_grad
        up_send[...] = up_grad

    @pl.when(i == 1)
    def _():
        down_keep[...] = down_grad
        up_keep[...] = up_grad


def backward(flow, place, grad, x, weights, active, slope, start):
    rows, width = grad.shape
    own = start is not None
    half = active.shape[1] // 2
    whole = pl.BlockSpec((rows, width), lambda i, place: (0, 0))
    wide = pl.BlockSpec((rows, half), lambda i, place: (0, i ^ 1))
    anywhere = pl.BlockSpec(memory_space=pl.ANY)
    down_part = pl.BlockSpec((half, width), lambda i, place: (0, 0))
    up_part = pl.BlockSpec((width, half), lambda i, place: (0, 0))
    return flow.call(
        functools.partial(backward_kernel, own=own),
        "backward",
        (2,),
        [place],
        [grad, x, *weights, active, slope] + ([start] if own else []),
        [whole, whole]
        + (own_specs(width, half, 1) if own else [anywhere] * 8)
        + [wide, wide]
        + ([whole] if own else []),
        [shape((rows, width), full)]
        + [shape((half, width), low)] * 2
        + [shape((width, half), low)] * 2
        + [shape((8, 2 * half), full)],
        [whole, down_part, down_part, up_part, up_part]
        + [pl.BlockSpec((8, half), lambda i, place: (0, i ^ 1))],
        scratch=[] if own else far_scratch(width, half),
        spaces="----hh-" if own else "-" * 10 + "hh",
        out_spaces="------",
        us=12,
    )


def first_back_kernel(
    place, total_ref, second_ref, normed_ref, inverse_ref, gain_ref, weight_ref, picked_ref,
    rows_ref, resid_ref, context_ref, sums_ref, *refs,
):
    s = pl.program_id(0)
    grad_refs, total_grads = refs[:4], refs[4:]
    grad_first = second_ref[...] + total_ref[...]
    normed = normed_ref[...]
    resid = norm_backward(grad_first, normed, inverse_ref[:, :1], gain_ref[...])
    upper = resid.astype(low)
    lower = (resid - upper.astype(full)).astype(low)
    picked = picked_ref[...]
    resid_ref[...] = dot(picked, upper) + dot(picked, lower)
    grad_context = dot(upper, weight_ref[...], 1, 1).astype(low)
    context_ref[...] = dot(picked, grad_context).astype(low)
    add_rows(sums_ref, (grad_first * normed, grad_first, resid))
    weight_grad = dot(rows_ref[...], upper, 0, 0)

    @pl.when(s == 0)
    def _():
        total_grads[0][...] = weight_grad

    @pl.when(s > 0)
    def _():
        total_grads[0][...] += weight_grad

    @pl.when(s == pl.num_programs(0) - 1)
    def _():
        half = weight_ref.shape[0] // 2
        for side in range(2):
            for r in range(2):
                down = pl.ds(pl.multiple_of((place[2] ^ r) * half, half), half)
                along = pl.ds(pl.multiple_of((place[0] ^ side) * half, half), half)
                grad_refs[2 * side + r][...] = total_grads[0][down, along].astype(low)


def first_back(flow, place, total, second, normed, inverse, gain, weight, picked, rows_c, length):
    rows, width = normed.shape
    slots = picked.shape[1]
    seqs, per_seq = rows // length, length // slots
    half = width // 2
    seq = lambda n, w: pl.BlockSpec((n, w), lambda s, place: (s, 0))
    fixed = lambda n, w: pl.BlockSpec((n, w), lambda s, place: (0, 0))
    return flow.call(
        first_back_kernel,
        "first_back",
        (seqs,),
        [place],
        [total, second, normed, inverse, gain, weight, picked, rows_c],
        [
            seq(slots, width),
            seq(slots, width),
            pl.BlockSpec((slots, width), lambda s, place: (s * per_seq, 0)),
            seq(slots, 128),
            whole_of(gain),
            whole_of(weight),
            seq(length, slots),
            seq(slots, width),
        ],
        [shape((rows, width), full), shape((rows, width), low), shape((8, width), full)]
        + [shape((half, 4 * half), low)] * 4,
        [seq(length, width), seq(length, width), fixed(8, width)]
        + [pl.BlockSpec((half, half), lambda s, place: (0, 3))] * 4,
        scratch=[pltpu.VMEM((width, width), full)],
        spaces="--------",
        out_spaces="h------",
        us=10,
    )


def project_kernel(tokens_ref, *refs, scale):
    weights, (bias_q, bias_v), outs = refs[:3], refs[3:5], refs[5:]
    tokens = tokens_ref[...]
    queries = (dot(tokens, weights[0][...]) + bias_q[...]).astype(low)
    outs[0][...] = (queries.astype(full) * scale).astype(low)
    outs[1][...] = dot(tokens, weights[1][...]).astype(low)
    outs[2][...] = (dot(tokens, weights[2][...]) + bias_v[...]).astype(low)


def project(flow, tokens, weights, biases, scale):
    rows, width = tokens.shape
    block = pl.BlockSpec((256, width), lambda i: (i, 0))
    return flow.call(
        functools.partial(project_kernel, scale=scale),
        "project",
        (rows // 256,),
        [],
        [tokens, *weights, *biases],
        [block] + [whole_of(v) for v in (*weights, *biases)],
        [shape((rows, width), low)] * 3,
        [block] * 3,
        spaces="-" * 6,
        out_spaces="hhh",
        us=8.5,
    )


def input_kernel(place, resid_ref, *refs, blocks):
    grads, weights, out_ref = refs[: len(blocks)], refs[len(blocks) : -1], refs[-1]
    total = resid_ref[...]
    for ref, (side, start, group) in zip(grads, blocks):
        for n in range(3):
            weight = weights[3 * side + n][:, start : start + group]
            total += dot(ref[:, n * group : (n + 1) * group], weight, 1, 1)
    out_ref[...] = total.astype(low)


def input_grad(flow, place, resid, parts, weights):
    rows, width = resid.shape
    half = width // 2
    block = pl.BlockSpec((256, width), lambda i, place: (i, 0))
    grads = [part[2] for part in parts]
    specs = [
        pl.BlockSpec((width, half), lambda i, place, side=side: (0, place[0] ^ side))
        for side in range(2)
        for n in range(3)
    ]
    return flow.call(
        functools.partial(
            input_kernel, blocks=[(side, start, g.shape[1] // 3) for side, start, g in parts]
        ),
        "input_grad",
        (rows // 256,),
        [place],
        [resid, *grads, *weights, *weights],
        [block]
        + [pl.BlockSpec((256, g.shape[1]), lambda i, place: (i, 0)) for g in grads]
        + specs,
        [shape((rows, width), low)],
        [block],
        spaces="h" * (1 + len(parts)) + "-" * 6,
        out_spaces="h",
        polled=False,
        us=12.3,
    )[0]


def gate_kernel(place, scores_ref, noise_ref, gate_ref, *parts):
    gate = jax.nn.sigmoid((scores_ref[...].astype(full) + noise_ref[...].astype(full)) / heat)
    gate_ref[...] = gate.astype(low)
    part = gate_ref.shape[1] // 4
    mine = pl.ds(pl.multiple_of(place[1] * part, part), part)
    for p, ref in enumerate(parts):

        @pl.when(pl.program_id(0) == p)
        def _(ref=ref):
            ref[...] = gate_ref[:, mine, :]


def gates(flow, place, scores, noise):
    heads, length, _ = scores.shape
    pairs, part = heads // 2, length // 4
    block = pl.BlockSpec((2, length, length), lambda i, place: (i, 0, 0))
    return flow.call(
        gate_kernel,
        "gates",
        (pairs,),
        [place],
        [scores, noise],
        [block, block],
        [shape(scores.shape, low)] + [shape((2, part, length), low)] * pairs,
        [block] + [pl.BlockSpec((2, part, length), lambda i, place: (0, 0, 0))] * pairs,
        spaces="--",
        out_spaces="h" + "-" * pairs,
        us=5.5,
    )


def mask_kernel(place, scores_ref, noise_ref, mine_ref, got_ref, *refs):
    out_ref = refs[-1]
    half = mine_ref.shape[1]
    for side, ref in enumerate((mine_ref, got_ref)):
        core = place[2] ^ side
        rows = pl.ds(pl.multiple_of(core * half, half), half)
        gate = jax.nn.sigmoid(
            (scores_ref[:, rows, :].astype(full) + noise_ref[:, rows, :].astype(full)) / heat
        )
        out_ref[:, rows, :] = ref[...].astype(full) * (gate * (1.0 - gate) / heat)


def mask_grad(flow, place, scores, noise, mine, got, begin, earlier):
    heads, length, _ = scores.shape
    block = pl.BlockSpec((1, length, length), lambda i, place: (begin + i, 0, 0))
    half = pl.BlockSpec((1, length // 2, length), lambda i, place: (i, 0, 0))
    return flow.call(
        mask_kernel,
        "mask_grad",
        (mine.shape[0],),
        [place],
        [scores, noise, mine, got, *earlier],
        [block, block, half, half] + [pl.BlockSpec(memory_space=pl.ANY)] * len(earlier),
        [shape(scores.shape, full)],
        [block],
        aliases={5: 0} if earlier else {},
        spaces="hh--" + "h" * len(earlier),
        out_spaces="h",
        polled=False,
        us=mine.shape[0],
    )


def make_local(n_dp):
    bits = n_dp.bit_length() - 1

    def added(a, b):
        return (a.astype(full) + b.astype(full)).astype(low)

    def in_order(mine, other, bit, axis):
        return jnp.concatenate(
            [jnp.where(bit == 0, mine, other), jnp.where(bit == 0, other, mine)], axis
        )

    def local(
        tokens,
        masked_positions,
        cotangent,
        query_weight,
        query_bias,
        key_weight,
        value_weight,
        value_bias,
        output_weight,
        output_bias,
        first_gain,
        first_shift,
        up_weight,
        up_bias,
        down_weight,
        lowering_offset,
        second_gain,
        second_shift,
        channel_filter_scores,
        mask_noise,
    ):
        rows, width = tokens.shape
        seqs, slots = masked_positions.shape
        length = rows // seqs
        own_heads = channel_filter_scores.shape[0]
        depth = width // (2 * own_heads)
        scale = depth ** (-0.5)
        pairs = own_heads * depth // 128
        dp, tp = lax.axis_index("dp"), lax.axis_index("tp")
        bit = [(dp >> b) & 1 for b in range(bits)]
        quarter = 2 * bit[0] + bit[1]

        place = jnp.stack([tp, quarter, bit[0]]).astype(jnp.int32)

        def halves(a, axis, which):
            n = a.shape[axis] // 2
            return lax.dynamic_slice_in_dim(a, which * n, n, axis)

        def quarter_of(a, axis):
            n = a.shape[axis] // 4
            return lax.dynamic_slice_in_dim(a, quarter * n, n, axis)

        flow = Flow(n_dp)
        swap = flow.swap
        row = lambda v: v[None, :]
        projections = (query_weight, key_weight, value_weight)

        gate, *gate_parts = gates(flow, place, channel_filter_scores, mask_noise)
        far_gates = {}

        def gather_gate(p):
            near = gate_parts[p]
            got, due = swap(near, "tp")
            (near,) = yield [got], due, [near]
            (beside, due), (over, _) = swap(near, 1), swap(near, 0)
            beside, over = yield [beside, over], due, []
            corner, due = swap(beside, 0)
            (corner,) = yield [corner], due, []
            far_gates[p] = near, beside, over, corner

        far_weights = {}

        def gather_weight(n, mine):
            near, due = swap(mine, "tp")
            (near,) = yield [near], due + (4.0, 10.0)[n], [mine]
            (beside, due), (over, _) = swap(near, 1), swap(near, 0)
            extra = [lax.ppermute(up_bias, "tp", [(0, 1), (1, 0)])] if n == 0 else []
            beside, over, *extra = yield [beside, over, *extra], due, []
            if extra:
                far_weights["bias"] = extra[0]
            corner, due = swap(beside, 0)
            (corner,) = yield [corner], due, []
            far_weights[n] = near, beside, over, corner

        for p in range(pairs):
            flow.start(gather_gate(p))
        flow.start(gather_weight(0, quarter_of(up_weight, 1)))
        flow.start(gather_weight(1, quarter_of(down_weight, 0)))

        queries, keys, values = project(
            flow, tokens, projections, (query_bias, value_bias), scale
        )
        context, logsum = attend_own(flow, place, queries, keys, values, gate, length)
        earlier, logsums = [context], [[], logsum]
        for p in range(pairs):
            flow.wait(lambda: p in far_gates)
            context, part, far_gate = attend_far(
                flow, place, queries, keys, values, far_gates[p], p, pairs, earlier, length
            )
            logsums[0].append(part)
            earlier = [context, far_gate]

        order, picked, context_c, x, x_c, normed, inverse = first_norm(
            flow,
            masked_positions,
            context,
            tokens,
            output_weight,
            output_bias,
            first_gain,
            first_shift,
            length,
        )
        own_weights, own_bias = (up_weight, down_weight), row(up_bias)
        total, own_active, own_slope = forward(
            flow, place, x, own_weights, own_bias, None, length, slots
        )
        flow.wait(lambda: len(far_weights) == 3)
        bias_far = row(far_weights["bias"])
        far = [far_weights[n][r] for r in range(4) for n in range(2)]
        total, far_active, far_slope = forward(
            flow, place, x, far, bias_far, total, length, slots
        )
        vectors = [lowering_offset, first_gain, first_shift, second_gain, second_shift]
        layer_output, grad_second, grad_forward, sums_second = second_norm(
            flow, total, normed, cotangent, order, picked, vectors
        )

        def first_half(a, axis):
            return lax.slice_in_dim(a, 0, a.shape[axis] // 2, axis=axis)

        def last_half(a, axis):
            return lax.slice_in_dim(a, a.shape[axis] // 2, a.shape[axis], axis=axis)

        done = flow.done
        first_ways = tuple(range(1, bits))

        def split(a, way, axis, relative_axis):
            if way == 1 and relative_axis is not None:
                return first_half(a, relative_axis), last_half(a, relative_axis)
            return halves(a, axis, bit[way]), halves(a, axis, 1 - bit[way])

        def summed(mine, ways, axis, relative_axis):
            for way in ways:
                keep, send = split(mine, way, axis, relative_axis)
                got, due = swap(send, way)
                (got,) = yield [got], due, [send]
                mine = added(keep, got)
            return mine

        def core_sum(keep, send):
            got, due = swap(send, 0)
            (got,) = yield [got], due, [send]
            return keep, got

        def reduce_far(parts, keep, send):
            keep, got = yield from core_sum(keep, send)
            for name, pick, axis, relative_axis, before in parts:
                piece = added(pick(keep), pick(got))
                flow.start(send_far(name, piece, axis, relative_axis, before))

        def send_far(name, mine, axis, relative_axis, before):
            mine = yield from summed(mine, before, axis, relative_axis)
            got, due = swap(mine, "tp")
            (got,) = yield [got], due, [mine]
            done[name] = got

        def reduce_own(parts, keep, send):
            keep, got = yield from core_sum(keep, send)
            for name, pick, axis, relative_axis, before in parts:
                piece = added(pick(keep), pick(got))
                flow.start(rest_own(name, piece, axis, relative_axis, before))

        def rest_own(name, mine, axis, relative_axis, before):
            mine = yield from summed(mine, before, axis, relative_axis)
            (mine,) = yield [mine], name, []
            mine = added(mine, done[name])
            after = tuple(way for way in first_ways if way not in before)
            mine = yield from summed(mine, after[:-1], axis, relative_axis)
            got, due = swap(mine, after[-1])
            (got,) = yield [got], due, [mine]
            mine = added(mine, got)
            for way in reversed(before + after[:-1]):
                got, due = swap(mine, way)
                (got,) = yield [got], due, [mine]
                along = relative_axis if way == 1 and relative_axis is not None else axis
                mine = in_order(mine, got, bit[way], along)
            got, due = swap(mine, 0)
            (got,) = yield [got], due, [mine]
            done[name + " whole"] = (mine, got)

        def spread(name, axis):
            return in_order(*done[name + " whole"], bit[0], axis).astype(full)

        def whole(a):
            return a

        def add_vectors(name, mine):
            for way in ("tp",) + tuple(range(bits)):
                got, due = swap(mine, way)
                (got,) = yield [got], due + 5.0, [mine]
                mine = mine + got
            done[name] = mine

        def both(mine, theirs):
            return in_order(mine, theirs, tp, 0)

        def hidden_half(sums):
            return in_order(*jnp.split(sums[0], 2), bit[0], 0)

        parts_down = [("down", whole, 0, None, orders["down"])]
        parts_up = [("up", whole, 0, None, orders["up"])]
        parts_qkv = [("qkv", whole, 0, None, orders["qkv"])]
        mask_pairs = [(0, pairs - 1), (pairs - 1, 1)]
        parts_mask = [
            ("mask" + str(n), whole, 2, 1, orders["mask" + str(n)]) for n in range(len(mask_pairs))
        ]

        back, down_send, down_keep, up_send, up_keep, far_sums = backward(
            flow, place, grad_forward, x_c, far, far_active, far_slope, None
        )
        flow.start(reduce_far(parts_down, down_keep, down_send))
        flow.start(reduce_far(parts_up, up_keep, up_send))
        back, down_send, down_keep, up_send, up_keep, own_sums = backward(
            flow, place, grad_forward, x_c, own_weights, own_active, own_slope, back
        )
        flow.start(reduce_own(parts_down, down_keep, down_send))
        flow.start(reduce_own(parts_up, up_keep, up_send))

        resid, grad_context, sums_first, own_keep, own_send, far_keep, far_send = first_back(
            flow,
            place,
            back,
            grad_second,
            normed,
            inverse,
            first_gain,
            output_weight,
            picked,
            context_c,
            length,
        )
        early = [both(hidden_half(own_sums), hidden_half(far_sums))]
        early += [sums_first[i] for i in range(3)] + [sums_second[i] for i in range(3)]
        def back_part(side, gate, p, masks, at, held, weights):
            logsum = logsums[0][p] if side else logsums[1]
            return attend_back(
                flow, place, queries, keys, values, grad_context, logsum, tokens, gate, side,
                length, scale, p, masks, at, held, weights,
            )

        sums_parts, grads = [[], []], []
        for side in (1, 0):
            begin = (reduce_own, reduce_far)[side]
            weights = ((own_keep, own_send), (far_keep, far_send))[side]
            masks = ()
            for p in range(pairs):
                first, many = [part for part in mask_pairs if part[0] <= p < sum(part)][0]
                grad, *masks, w_keep, w_send, part = back_part(
                    side, (gate, far_gate)[side], p, masks, p - first, 2 * many, weights
                )
                weights = (w_keep, w_send)
                grads.append((side, p * 128, grad))
                sums_parts[side].append(part)
                if p == first + many - 1:
                    number = mask_pairs.index((first, many))
                    flow.start(begin(parts_mask[number : number + 1], *masks))
                    masks = ()
            flow.start(begin(parts_qkv, *weights))
        sums_own, sums_far = (jnp.concatenate(part, 1) for part in sums_parts)
        vectors = early + [both(sums_own[i], sums_far[i]) for i in range(2)]
        flow.start(add_vectors("vectors", jnp.concatenate(vectors).reshape(-1, 128)))
        results = {}

        def tokens_part():
            results["tokens"] = input_grad(flow, place, resid, grads, projections)

        flow.fillers.append((7.0, tokens_part))
        masks = []

        def mask_part(p, mine, got):
            for name, axis in (("down", 0), ("up", 1)):
                if name + " whole" in done and name not in results:
                    results[name] = spread(name, axis)
                    flow.sends.append(results[name])
            masks[:] = mask_grad(
                flow, place, channel_filter_scores, mask_noise, mine, got, 2 * mask_pairs[p][0],
                list(masks),
            )

        def watch():
            for p, (name, *_) in enumerate(parts_mask):
                pair = done.pop(name + " whole", None)
                if pair is not None:
                    flow.fillers.insert(0, (4.0, functools.partial(mask_part, p, *pair)))
            return not flow.tasks

        flow.wait(watch)
        for _, filler in flow.fillers:
            filler()
        for name, axis in (("down", 0), ("up", 1)):
            if name not in results:
                results[name] = spread(name, axis)
        down_grad, up_grad, qkv_grad = results["down"], results["up"], spread("qkv", 0)
        hidden_all = 2 * up_weight.shape[1]
        vectors = done["vectors"].reshape(-1)
        up_bias_grad = halves(vectors[:hidden_all], 0, tp)
        vectors = halves(vectors[hidden_all:].reshape(-1, width), 1, tp)
        fg, fs, ob, sg, ss, db, query_bias_grad, value_bias_grad = [vectors[i] for i in range(8)]

        group = own_heads * depth
        output_grad = qkv_grad[:, 3 * group :]
        by_pair = [jnp.split(part, 3, 1) for part in jnp.split(qkv_grad[:, : 3 * group], pairs, 1)]
        qkv_grads = [jnp.concatenate([part[n] for part in by_pair], 1) for n in range(3)]
        return (
            layer_output,
            results["tokens"],
            qkv_grads[0],
            query_bias_grad,
            qkv_grads[1],
            qkv_grads[2],
            value_bias_grad,
            output_grad,
            ob,
            fg,
            fs,
            up_grad,
            up_bias_grad,
            down_grad,
            db,
            sg,
            ss,
            masks[0],
        )

    return local


def solution(mesh):
    in_specs = (
        P(("dp", "tp"), None),
        P(("dp", "tp"), None),
        P(("dp", "tp"), None),
        P(),
        P(),
        P(),
        P(),
        P(),
        P(),
        P(),
        P(),
        P(),
        P(None, "tp"),
        P("tp"),
        P("tp", None),
        P(),
        P(),
        P(),
        P("tp", None, None),
        P("tp", None, None),
    )
    out_specs = (
        P(("dp", "tp"), None),
        P(("dp", "tp"), None),
        P(None, "tp"),
        P("tp"),
        P(None, "tp"),
        P(None, "tp"),
        P("tp"),
        P(None, "tp"),
        P("tp"),
        P("tp"),
        P("tp"),
        P(None, "tp"),
        P("tp"),
        P("tp", None),
        P("tp"),
        P("tp"),
        P("tp"),
        P("tp", None, None),
    )
    local = make_local(mesh.shape["dp"])
    return jax.shard_map(local, mesh=mesh, in_specs=in_specs, out_specs=out_specs, check_vma=False)
```

```python
import functools

import jax
import jax.numpy as jnp
from jax import lax
from jax.experimental import pallas as pl
from jax.experimental.pallas import tpu as pltpu
from jax.sharding import PartitionSpec as P

heat = 0.6
epsilon = 1e-06
low = jnp.bfloat16
full = jnp.float32
MIB = 1 << 20
vmem_mib = 32
kernel_flops = 8_000_000_000
early, late = -2.0, 1.0


orders = {
    "down": (1,),
    "mask0": (2,),
    "mask1": (1,),
    "qkv": (),
    "up": (1, 2),
}


def dot(left, right, left_dim=1, right_dim=0):
    return lax.dot_general(
        left, right, (((left_dim,), (right_dim,)), ((), ())), preferred_element_type=full
    )


def shape(dims, kind):
    return jax.ShapeDtypeStruct(dims, kind)


class Flow:
    def __init__(self, n_dp):
        self.n_dp = n_dp
        self.token = None
        self.sends = []
        self.tasks = []
        self.done = {}
        self.now = 0.0
        self.free = {}
        self.started = False
        self.fillers = []

    def call(
        self, kernel, name, grid, places, args, in_specs, out_shape, out_specs,
        us, aliases=None, scratch=(), spaces="", out_spaces="", polled=True,
    ):
        if self.token is not None and polled:
            self.poll()
        self.now += us
        after = ([] if self.token is None else [self.token]) + self.sends
        self.sends = []
        place_of = {"v": pltpu.VMEM, "h": pltpu.HBM}
        args = [
            pltpu.with_memory_space_constraint(a, place_of[c]) if c in place_of else a
            for a, c in zip(args, spaces, strict=True)
        ]
        out_shape = [
            place_of[c](a.shape, a.dtype) if c in place_of else a
            for a, c in zip(out_shape, out_spaces, strict=True)
        ]
        first, many, outs = len(places) + len(args), len(after), len(out_shape)

        def run(*refs):
            refs = refs[:first] + refs[first + many :]
            kernel(*refs[: first + outs], *refs[first + outs + 1 :])
            refs[first + outs][...] = jnp.zeros((8, 128), full)

        result = pl.pallas_call(
            run,
            grid_spec=pltpu.PrefetchScalarGridSpec(
                num_scalar_prefetch=len(places),
                grid=grid,
                in_specs=list(in_specs) + [pl.BlockSpec(memory_space=pl.ANY)] * many,
                out_specs=list(out_specs) + [pl.BlockSpec((8, 128), lambda *_: (0, 0))],
                scratch_shapes=list(scratch),
            ),
            out_shape=list(out_shape) + [shape((8, 128), full)],
            input_output_aliases=aliases or {},
            compiler_params=pltpu.CompilerParams(vmem_limit_bytes=vmem_mib * MIB),
            cost_estimate=pl.CostEstimate(
                flops=kernel_flops, bytes_accessed=1, transcendentals=0
            ),
            name=name,
        )(*places, *args, *after)
        self.token = result[-1]
        return result[:-1]

    def pin(self, arrays):
        arrays = [self.token, *arrays]
        anywhere = [pl.BlockSpec(memory_space=pl.ANY)] * len(arrays)

        def run(*refs):
            pass

        self.token, *arrays = pl.pallas_call(
            run,
            in_specs=anywhere,
            out_specs=anywhere,
            out_shape=[shape(a.shape, a.dtype) for a in arrays],
            input_output_aliases={i: i for i in range(len(arrays))},
            compiler_params=pltpu.CompilerParams(vmem_limit_bytes=MIB),
            cost_estimate=pl.CostEstimate(flops=1, bytes_accessed=1, transcendentals=0),
            name="turn",
        )(*arrays)
        return arrays

    def swap(self, a, way):
        if way == "tp":
            got = lax.ppermute(a, "tp", [(0, 1), (1, 0)])
        else:
            got = lax.ppermute(a, "dp", [(i, i ^ (1 << way)) for i in range(self.n_dp)])
        kilobytes = a.size * a.dtype.itemsize / 1e3
        rate, delay = (400.0, 2.0) if way == 0 else (22.0, 3.5) if way == 3 else (44.0 if self.now > 70 else 38.0, 2.5)
        link = 2 if way == 3 else way
        self.now += 0.8 if self.started and way else 1.4 if way else 0.5
        self.started = self.started or way != 0
        self.free[link] = max(self.free.get(link, 0.0), self.now) + kilobytes / rate
        return got, self.free[link] + delay

    def start(self, task):
        self.tasks.append([task, *self.advance(task, None)])

    def advance(self, task, values):
        try:
            arrays, due, sends = task.send(values)
        except StopIteration:
            return [], None
        self.sends += sends
        self.now += 0.5
        return arrays, due

    def is_due(self, entry, slack):
        due = entry[2]
        return due in self.done if isinstance(due, str) else due <= self.now + slack

    def poll(self, slack=early):
        due = [entry for entry in self.tasks if self.is_due(entry, slack)]
        if not due:
            return
        for entry in due:
            if not isinstance(entry[2], str):
                self.now = max(self.now, entry[2])
        arrays = self.pin([a for entry in due for a in entry[1]])
        self.now += 0.5
        self.started = False
        for entry in due:
            mine, arrays = arrays[: len(entry[1])], arrays[len(entry[1]) :]
            entry[1:] = self.advance(entry[0], mine)
        self.tasks = [entry for entry in self.tasks if entry[1]]

    def wait(self, ready, slack=late):
        while not ready():
            if self.fillers and self.fillers[0][0] < 5.0:
                self.fillers.pop(0)[1]()
            if any(self.is_due(entry, 0.0) for entry in self.tasks):
                self.poll(slack)
                continue
            soonest = min(e[2] for e in self.tasks if not isinstance(e[2], str))
            fits = [n for n, (us, _) in enumerate(self.fillers) if us <= soonest - self.now + 2.0]
            if fits:
                self.fillers.pop(fits[0])[1]()
                continue
            self.now = max(self.now, soonest)
            self.poll(slack)


def head_lanes(width):
    lane = lax.broadcasted_iota(jnp.int32, (1, width), 1)
    first = lane < width // 2
    return first, (first.astype(full).astype(low), (1.0 - first.astype(full)).astype(low))


def quarter_rows(place, length, s, r):
    part = length // 4
    return pl.ds(pl.multiple_of(s * length + (place[1] ^ r) * part, part), part)


def rows_of(ref, place, length, s):
    return jnp.concatenate([ref[quarter_rows(place, length, s, r), :] for r in range(4)], 0)


def write_rows(ref, value, place, length, s):
    part = length // 4
    for r in range(4):
        ref[quarter_rows(place, length, s, r), :] = value[r * part : (r + 1) * part]


def attend_kernel(place, q_ref, k_ref, v_ref, *rest, length, add):
    gates, (context_ref, logsum_ref) = rest[:4], rest[-2:]
    first, lanes = head_lanes(q_ref.shape[1])
    levels = [jnp.concatenate([g[h] for g in gates], 0) for h in range(2)]
    for s in range(q_ref.shape[0] // length):
        queries = rows_of(q_ref, place, length, s)
        keys = k_ref[s * length : (s + 1) * length, :]
        values = v_ref[s * length : (s + 1) * length, :]
        mixed, logs = [], []
        for h in range(2):
            scores = dot(queries * lanes[h], keys, 1, 1)
            peak = jnp.max(scores, -1, keepdims=True)
            expo = jnp.exp(scores - peak)
            total = jnp.sum(expo, -1, keepdims=True)
            weights = (expo * levels[h].astype(full)).astype(low)
            mixed.append(dot(weights, values) * (1.0 / total))
            logs.append(peak + jnp.log(total))
        write_rows(context_ref, jnp.where(first, mixed[0], mixed[1]).astype(low), place, length, s)
        here = 2 * pl.program_id(0) if add else 0
        lane = lax.broadcasted_iota(jnp.int32, first.shape, 1)
        columns = jnp.where(lane == here, logs[0], jnp.where(lane == here + 1, logs[1], 0.0))
        for r in range(4):
            rows = quarter_rows(place, length, s, r)
            part = columns[r * (length // 4) : (r + 1) * (length // 4)]
            if add:

                @pl.when(pl.program_id(0) == 0)
                def _():
                    logsum_ref[rows, :] = part

                @pl.when(pl.program_id(0) > 0)
                def _():
                    logsum_ref[rows, :] += part

            else:
                logsum_ref[rows, :] = part


def gate_specs(own, part, length, begin=0):
    if own:
        return [
            pl.BlockSpec((2, part, length), lambda hp, place, r=r: (begin + hp, place[1] ^ r, 0))
            for r in range(4)
        ]
    return [
        pl.BlockSpec((2, part, length), lambda hp, place, r=r: (begin + hp, r, 0)) for r in range(4)
    ]


def head_columns(rows, lanes, side, pairs, first=0):
    return pl.BlockSpec(
        (rows, lanes), lambda hp, place: (0, (place[0] ^ side) * pairs + first + hp)
    )


def attend_own(flow, place, queries, keys, values, gate, length):
    rows, width = queries.shape
    pairs, part = gate.shape[0] // 2, length // 4
    column = head_columns(rows, 128, 0, pairs)
    return flow.call(
        functools.partial(attend_kernel, length=length, add=True),
        "attend_own",
        (pairs,),
        [place],
        [queries, keys, values] + [gate] * 4,
        [column] * 3 + gate_specs(True, part, length),
        [shape((rows, width), low), shape((rows, 128), full)],
        [column, pl.BlockSpec((rows, 128), lambda hp, place: (0, 0))],
        spaces="hhhhhhh",
        out_spaces="hh",
        us=8.7,
    )


def attend_far_kernel(place, q_ref, k_ref, v_ref, *rest, length):
    gates, outs = rest[:4], rest[-3:]
    attend_kernel(place, q_ref, k_ref, v_ref, *gates, *outs[:2], length=length, add=False)
    part = length // 4
    for r in range(4):
        outs[2][:, r * part : (r + 1) * part, :] = gates[r][...]


def attend_far(flow, place, queries, keys, values, gates, pair, pairs, earlier, length):
    rows, width = queries.shape
    column = head_columns(rows, 128, 1, pairs, pair)
    return flow.call(
        functools.partial(attend_far_kernel, length=length),
        "attend_far",
        (1,),
        [place],
        [queries, keys, values, *gates, *earlier],
        [column] * 3
        + [pl.BlockSpec(g.shape, lambda hp, place: (0, 0, 0)) for g in gates]
        + [pl.BlockSpec(memory_space=pl.ANY)] * len(earlier),
        [
            shape((rows, width), low),
            shape((rows, 128), full),
            shape((2 * pairs, length, length), low),
        ],
        [
            column,
            pl.BlockSpec((rows, 128), lambda hp, place: (0, 0)),
            pl.BlockSpec((2, length, length), lambda hp, place: (pair, 0, 0)),
        ],
        aliases=dict(zip((8, 9), (0, 2))) if len(earlier) == 2 else {8: 0},
        spaces="hhh----" + "h" * len(earlier),
        out_spaces="hhh",
        us=5.3,
    )


def attend_back_kernel(place, q_ref, k_ref, v_ref, d_ref, logsum_ref, tokens_ref, *rest, length, scale, lane):
    gates = rest[:4]
    grads_ref, keep_ref, send_ref, keep_w, send_w, sums_ref = rest[-6:]
    hp = pl.program_id(0)
    group = grads_ref.shape[1] // 3
    width = q_ref.shape[1]
    part = length // 4
    first, lanes = head_lanes(width)
    levels = [jnp.concatenate([g[h] for g in gates], 0) for h in range(2)]
    masks = [None, None]
    sums_q = sums_v = 0.0
    for s in range(q_ref.shape[0] // length):
        here = slice(s * length, (s + 1) * length)
        queries, grads = rows_of(q_ref, place, length, s), rows_of(d_ref, place, length, s)
        logs = rows_of(logsum_ref, place, length, s)[:, lane : lane + 2]
        keys, values = k_ref[here, :], v_ref[here, :]
        totals = None
        for h in range(2):
            own_q, own_d, own_k = queries * lanes[h], grads * lanes[h], keys * lanes[h]
            sloped, weighted, produced = [], [], []
            for c in range(0, length, 128):
                tile = slice(c, c + 128)
                probs = jnp.exp(dot(own_q[tile], keys, 1, 1) - logs[tile, h : h + 1])
                product = dot(own_d[tile], values, 1, 1) * probs
                level = levels[h][tile].astype(full)
                gated = product * level
                rest = jnp.sum(gated, -1, keepdims=True)
                sloped.append((gated - probs * rest).astype(low))
                weighted.append((probs * level).astype(low))
                produced.append(product)
            slopes, weights = jnp.concatenate(sloped, 0), jnp.concatenate(weighted, 0)
            product = jnp.concatenate(produced, 0)
            masks[h] = product if masks[h] is None else masks[h] + product
            new = (dot(slopes, own_k), dot(own_q, slopes, 0, 0).T, dot(own_d, weights, 0, 0).T)
            totals = new if totals is None else tuple(a + b for a, b in zip(totals, new))
        grad_q, grad_k, grad_v = (
            (totals[0] * scale).astype(low),
            totals[1].astype(low),
            totals[2].astype(low),
        )
        for n, grad in enumerate((grad_q, grad_k, grad_v)):
            at = pl.ds(pl.multiple_of(n * group + hp * width, width), width)
            if n == 0:
                for r in range(4):
                    rows = quarter_rows(place, length, s, r)
                    grads_ref[rows, at] = grad[r * part : (r + 1) * part]
            else:
                grads_ref[here, at] = grad
        sums_q += jnp.sum(grad_q.astype(full), 0, keepdims=True)
        sums_v += jnp.sum(grad_v.astype(full), 0, keepdims=True)
    for h in range(2):
        mask = masks[h].astype(low)
        keep_ref[h] = mask[: 2 * part]
        send_ref[h] = mask[2 * part :]
    sums_ref[...] = jnp.concatenate([sums_q, sums_v, jnp.zeros((6, width), full)], 0)
    half = tokens_ref.shape[1] // 2
    for n in range(3):
        at = pl.ds(pl.multiple_of(n * group + hp * width, width), width)
        grad = grads_ref[:, at]
        for r, ref in enumerate((keep_w, send_w)):
            rows = tokens_ref[:, pl.ds(pl.multiple_of((place[2] ^ r) * half, half), half)]
            ref[:, n * width : (n + 1) * width] = dot(rows, grad, 0, 0).astype(low)


def attend_back(
    flow, place, queries, keys, values, grad_context, logsum, tokens, gate, side, length,
    scale, begin, masks, at, heads_held, weights,
):
    rows, width = queries.shape
    heads, part, lanes = gate.shape[0], length // 4, 128
    pairs = heads // 2
    column = head_columns(rows, lanes, side, pairs, begin)
    group = lanes
    mask = pl.BlockSpec((2, length // 2, length), lambda hp, place: (at, 0, 0))
    anywhere = [pl.BlockSpec(memory_space=pl.ANY)]
    held = [*weights, *masks]
    aliases = {11: 3, 12: 4}
    if masks:
        aliases.update({13: 1, 14: 2})
    return flow.call(
        functools.partial(
            attend_back_kernel, length=length, scale=scale, lane=0 if side else 2 * begin
        ),
        "attend_back",
        (1,),
        [place],
        [queries, keys, values, grad_context, logsum, tokens] + [gate] * 4 + held,
        [column] * 4
        + [pl.BlockSpec(logsum.shape, lambda hp, place: (0, 0))]
        + [pl.BlockSpec(tokens.shape, lambda hp, place: (0, 0))]
        + gate_specs(side == 0, part, length, begin)
        + anywhere * len(held),
        [shape((rows, 3 * group), low)]
        + [shape((heads_held, length // 2, length), low)] * 2
        + [shape(weights[0].shape, low)] * 2
        + [shape((8, group), full)],
        [pl.BlockSpec((rows, 3 * group), lambda hp, place: (0, 0))]
        + [mask] * 2
        + [pl.BlockSpec((width // 2, 3 * lanes), lambda hp, place: (0, begin))] * 2
        + [pl.BlockSpec((8, lanes), lambda hp, place: (0, hp))],
        aliases=aliases,
        spaces="hhh-h-" + "h" * 4 + "-" * len(held),
        out_spaces="h-----",
        us=8.8,
    )


def norm_forward(hidden, gain, shift):
    centre = hidden - jnp.mean(hidden, -1, keepdims=True)
    spread = jnp.mean(centre * centre, -1, keepdims=True)
    inverse = lax.rsqrt(spread + epsilon)
    normed = centre * inverse
    return normed * gain + shift, normed, inverse


def norm_backward(incoming, normed, inverse, gain):
    scaled = incoming * gain
    return inverse * (
        scaled
        - jnp.mean(scaled, -1, keepdims=True)
        - normed * jnp.mean(scaled * normed, -1, keepdims=True)
    )


def add_rows(ref, rows):
    packed = jnp.concatenate(
        [jnp.sum(row, 0, keepdims=True) for row in rows]
        + [jnp.zeros((8 - len(rows), ref.shape[1]), full)],
        0,
    )

    @pl.when(pl.program_id(0) == 0)
    def _():
        ref[...] = packed

    @pl.when(pl.program_id(0) > 0)
    def _():
        ref[...] += packed


def first_norm_kernel(
    slots_ref, context_ref, tokens_ref, weight_ref, bias_ref, gain_ref, shift_ref,
    order_ref, picked_ref, compact_ref, low_ref, kept_ref, normed_ref, inverse_ref,
):
    length, slots = tokens_ref.shape[0], slots_ref.shape[-1]
    position = lax.broadcasted_iota(jnp.int32, (length, slots), 0)
    hit = (position == slots_ref[pl.ds(pl.program_id(0), 1), :]).astype(full)
    chosen = jnp.max(hit, -1, keepdims=True)
    row = lax.broadcasted_iota(jnp.int32, (length, length), 0)
    column = lax.broadcasted_iota(jnp.int32, (length, length), 1)
    lower = (column <= row).astype(full).astype(low)
    upto = dot(lower, jnp.broadcast_to(chosen, (length, 128)).astype(low))[:, :1]
    count = jnp.sum(chosen, 0, keepdims=True)
    at = lax.broadcasted_iota(jnp.int32, (length, 1), 0).astype(full)
    target = jnp.where(chosen > 0, upto - 1.0, count + at - upto)
    order = (column.astype(full) == target).astype(full)
    picked_ref[...] = (order * chosen)[:, :slots].astype(low)
    order = order.astype(low)
    order_ref[...] = order
    context = dot(order, context_ref[...], 0, 0).astype(low)
    tokens = dot(order, tokens_ref[...], 0, 0)
    compact_ref[...] = context[:slots]
    attention = dot(context, weight_ref[...]) + bias_ref[...]
    out, normed, inverse = norm_forward(tokens + attention, gain_ref[...], shift_ref[...])
    out = out.astype(low)
    low_ref[...] = out
    kept_ref[...] = out[:slots]
    normed_ref[...] = normed
    inverse_ref[...] = jnp.broadcast_to(inverse[:slots], (slots, 128))


def by_seq(n, w):
    return pl.BlockSpec((n, w), lambda s: (s, 0))


def whole_of(a):
    return pl.BlockSpec(a.shape, lambda *_: (0,) * a.ndim)


def first_norm(flow, positions, context, tokens, weight, bias, gain, shift, length):
    rows, width = tokens.shape
    seqs, slots = positions.shape
    vectors = [weight, bias, gain, shift]
    return flow.call(
        first_norm_kernel,
        "first_norm",
        (seqs,),
        [],
        [positions, context, tokens, *vectors],
        [
            whole_of(positions),
            by_seq(length, width),
            by_seq(length, width),
        ]
        + [whole_of(v) for v in vectors],
        [
            shape((rows, length), low),
            shape((rows, slots), low),
            shape((seqs * slots, width), low),
            shape((rows, width), low),
            shape((seqs * slots, width), low),
            shape((rows, width), full),
            shape((seqs * slots, 128), full),
        ],
        [
            by_seq(length, length),
            by_seq(length, slots),
            by_seq(slots, width),
            by_seq(length, width),
            by_seq(slots, width),
            by_seq(length, width),
            by_seq(slots, 128),
        ],
        spaces="-h-----",
        out_spaces="hhh-hhh",
        us=9,
    )


def gelu_parts(hidden):
    size = jnp.abs(hidden)
    t = 1.0 / (1.0 + (0.3275911 * 0.7071067811865476) * size)
    poly = 1.061405429 * t - 1.453152027
    poly = poly * t + 1.421413741
    poly = poly * t - 0.284496736
    poly = poly * t + 0.254829592
    bell = jnp.exp(hidden * hidden * -0.5)
    tail = 0.5 * poly * t * bell
    below = jnp.where(hidden > 0, 1.0 - tail, tail)
    return below, bell


def far_pieces(place, pieces, held, sems, order):
    i = pl.program_id(0)
    part = pieces[0][0].shape[1]
    along = place[1] & 1

    def copies(n):
        for x in range(2):
            up, down = pieces[2 * order[n] + x]
            at = pl.ds(pl.multiple_of((along ^ x) * part, part), part)
            yield pltpu.make_async_copy(up, held[0].at[n, :, at], sems.at[n, 2 * x])
            yield pltpu.make_async_copy(down, held[1].at[n, at, :], sems.at[n, 2 * x + 1])

    @pl.when(i == 0)
    def _():
        for n in range(2):
            for copy in copies(n):
                copy.start()

    for n in range(2):

        @pl.when(i == n)
        def _(n=n):
            for copy in copies(n):
                copy.wait()

    return held[0][i], held[1][i]


def forward_kernel(place, x_ref, *refs, own, length, slots):
    if own:
        (up_ref, down_ref, bias_ref, total_ref, active_ref, slope_ref) = refs
        up, down = up_ref[...], down_ref[...]
    else:
        pieces, refs = refs[:8], refs[8:]
        bias_ref, start_ref, total_ref, active_ref, slope_ref, *held, sems = refs
        pieces = [pieces[2 * r : 2 * r + 2] for r in range(4)]
        up, down = far_pieces(place, pieces, held, sems, (0, 1))

    @pl.when(pl.program_id(0) == 0)
    def _():
        total_ref[...] = jnp.zeros_like(total_ref) if own else start_ref[...]

    bias = bias_ref[...]
    step = 256
    for block in range(x_ref.shape[0] // slots):
        rows = slice(block * slots, (block + 1) * slots)
        s, part = divmod(block, length // slots)
        kept = slice(s * slots, (s + 1) * slots)
        x = x_ref[rows, :]
        parts = []
        for c in range(0, up.shape[1], step):
            hidden = dot(x, up[:, c : c + step]) + bias[:, c : c + step]
            below, bell = gelu_parts(hidden)
            active = (hidden * below).astype(low)
            parts.append(active)
            if part == 0:
                active_ref[kept, c : c + step] = active
                slope_ref[kept, c : c + step] = below + hidden * bell * 0.3989422804014327
        total_ref[rows, :] += dot(jnp.concatenate(parts, 1), down)


def own_specs(width, half, first):
    return [
        pl.BlockSpec((width, half), lambda i, place: (0, place[2] ^ i ^ first)),
        pl.BlockSpec((half, width), lambda i, place: (place[2] ^ i ^ first, 0)),
    ]


def far_scratch(width, half):
    return [
        pltpu.VMEM((2, width, half), low),
        pltpu.VMEM((2, half, width), low),
        pltpu.SemaphoreType.DMA((2, 4)),
    ]


def forward(flow, place, x, weights, bias, start, length, slots):
    rows, width = x.shape
    own = start is None
    half = bias.shape[1] // 2
    kept = rows // length * slots
    whole = pl.BlockSpec((rows, width), lambda i, place: (0, 0))
    wide = pl.BlockSpec((kept, half), lambda i, place: (0, i))
    anywhere = pl.BlockSpec(memory_space=pl.ANY)
    return flow.call(
        functools.partial(forward_kernel, own=own, length=length, slots=slots),
        "forward",
        (2,),
        [place],
        [x, *weights, bias] + ([] if own else [start]),
        [whole]
        + (own_specs(width, half, 0) if own else [anywhere] * 8)
        + [pl.BlockSpec((1, half), lambda i, place: (0, place[2] ^ i))]
        + ([] if own else [whole]),
        [shape((rows, width), full), shape((kept, 2 * half), low), shape((kept, 2 * half), full)],
        [whole, wide, wide],
        scratch=[] if own else far_scratch(width, half),
        spaces="----" if own else "-" * 11,
        out_spaces="-hh",
        us=14.5,
    )


def second_norm_kernel(
    total_ref, normed_ref, cotangent_ref, order_ref, picked_ref,
    offset_ref, gain1_ref, shift1_ref, gain2_ref, shift2_ref,
    out_ref, grad_ref, low_ref, sums_ref,
):
    slots = picked_ref.shape[1]
    first_out = normed_ref[...] * gain1_ref[...] + shift1_ref[...]
    gain = gain2_ref[...]
    out, normed, inverse = norm_forward(
        first_out + (total_ref[...] + offset_ref[...]), gain, shift2_ref[...]
    )
    out_ref[...] = dot(order_ref[...], out.astype(low)).astype(low)
    grad_out = dot(picked_ref[...], cotangent_ref[...], 0, 0)
    normed, inverse = normed[:slots], inverse[:slots]
    grad = norm_backward(grad_out, normed, inverse, gain)
    grad_ref[...] = grad
    low_ref[...] = grad.astype(low)
    add_rows(sums_ref, (grad_out * normed, grad_out, grad))


def second_norm(flow, total, normed, cotangent, order, picked, vectors):
    rows, width = total.shape
    length, slots = order.shape[1], picked.shape[1]
    seqs = rows // length
    return flow.call(
        second_norm_kernel,
        "second_norm",
        (seqs,),
        [],
        [total, normed, cotangent, order, picked, *vectors],
        [by_seq(length, width)] * 3
        + [by_seq(length, length), by_seq(length, slots)]
        + [whole_of(v) for v in vectors],
        [
            shape((rows, width), low),
            shape((seqs * slots, width), full),
            shape((seqs * slots, width), low),
            shape((8, width), full),
        ],
        [
            by_seq(length, width),
            by_seq(slots, width),
            by_seq(slots, width),
            pl.BlockSpec((8, width), lambda s: (0, 0)),
        ],
        spaces="-" * (5 + len(vectors)),
        out_spaces="----",
        us=6,
    )


def backward_kernel(place, grad_ref, x_ref, *refs, own):
    if own:
        (up_ref, down_ref, active_ref, slope_ref, start_ref), refs = refs[:5], refs[5:]
        up, down = up_ref[...], down_ref[...]
    else:
        pieces, (active_ref, slope_ref), refs = refs[:8], refs[8:10], refs[10:]
        refs, (*held, sems) = refs[:6], refs[6:]
        pieces = [pieces[2 * r : 2 * r + 2] for r in range(4)]
        up, down = far_pieces(place, pieces, held, sems, (1, 0))
    total_ref, down_send, down_keep, up_send, up_keep, sums_ref = refs
    i = pl.program_id(0)

    @pl.when(i == 0)
    def _():
        total_ref[...] = start_ref[...] if own else jnp.zeros_like(total_ref)

    grad = grad_ref[...]
    step = 256
    parts = []
    for c in range(0, up.shape[1], step):
        grad_active = dot(grad, down[c : c + step, :], 1, 1)
        grad_hidden = (grad_active * slope_ref[:, c : c + step]).astype(low)
        parts.append(grad_hidden)
        sums = jnp.sum(grad_hidden.astype(full), 0, keepdims=True)
        sums_ref[:, c : c + step] = jnp.broadcast_to(sums, (sums_ref.shape[0], step))
    grad_hidden = jnp.concatenate(parts, 1)
    total_ref[...] += dot(grad_hidden, up, 1, 1)
    down_grad = dot(active_ref[...], grad, 0, 0).astype(low)
    up_grad = dot(x_ref[...], grad_hidden, 0, 0).astype(low)

    @pl.when(i == 0)
    def _():
        down_send[...] = down_grad
        up_send[...] = up_grad

    @pl.when(i == 1)
    def _():
        down_keep[...] = down_grad
        up_keep[...] = up_grad


def backward(flow, place, grad, x, weights, active, slope, start):
    rows, width = grad.shape
    own = start is not None
    half = active.shape[1] // 2
    whole = pl.BlockSpec((rows, width), lambda i, place: (0, 0))
    wide = pl.BlockSpec((rows, half), lambda i, place: (0, i ^ 1))
    anywhere = pl.BlockSpec(memory_space=pl.ANY)
    down_part = pl.BlockSpec((half, width), lambda i, place: (0, 0))
    up_part = pl.BlockSpec((width, half), lambda i, place: (0, 0))
    return flow.call(
        functools.partial(backward_kernel, own=own),
        "backward",
        (2,),
        [place],
        [grad, x, *weights, active, slope] + ([start] if own else []),
        [whole, whole]
        + (own_specs(width, half, 1) if own else [anywhere] * 8)
        + [wide, wide]
        + ([whole] if own else []),
        [shape((rows, width), full)]
        + [shape((half, width), low)] * 2
        + [shape((width, half), low)] * 2
        + [shape((8, 2 * half), full)],
        [whole, down_part, down_part, up_part, up_part]
        + [pl.BlockSpec((8, half), lambda i, place: (0, i ^ 1))],
        scratch=[] if own else far_scratch(width, half),
        spaces="----hh-" if own else "-" * 10 + "hh",
        out_spaces="------",
        us=12,
    )


def first_back_kernel(
    place, total_ref, second_ref, normed_ref, inverse_ref, gain_ref, weight_ref, picked_ref,
    rows_ref, resid_ref, context_ref, sums_ref, *refs,
):
    s = pl.program_id(0)
    grad_refs, total_grads = refs[:4], refs[4:]
    grad_first = second_ref[...] + total_ref[...]
    normed = normed_ref[...]
    resid = norm_backward(grad_first, normed, inverse_ref[:, :1], gain_ref[...])
    upper = resid.astype(low)
    lower = (resid - upper.astype(full)).astype(low)
    picked = picked_ref[...]
    resid_ref[...] = dot(picked, upper) + dot(picked, lower)
    grad_context = dot(upper, weight_ref[...], 1, 1).astype(low)
    context_ref[...] = dot(picked, grad_context).astype(low)
    add_rows(sums_ref, (grad_first * normed, grad_first, resid))
    weight_grad = dot(rows_ref[...], upper, 0, 0)

    @pl.when(s == 0)
    def _():
        total_grads[0][...] = weight_grad

    @pl.when(s > 0)
    def _():
        total_grads[0][...] += weight_grad

    @pl.when(s == pl.num_programs(0) - 1)
    def _():
        half = weight_ref.shape[0] // 2
        for side in range(2):
            for r in range(2):
                down = pl.ds(pl.multiple_of((place[2] ^ r) * half, half), half)
                along = pl.ds(pl.multiple_of((place[0] ^ side) * half, half), half)
                grad_refs[2 * side + r][...] = total_grads[0][down, along].astype(low)


def first_back(flow, place, total, second, normed, inverse, gain, weight, picked, rows_c, length):
    rows, width = normed.shape
    slots = picked.shape[1]
    seqs, per_seq = rows // length, length // slots
    half = width // 2
    seq = lambda n, w: pl.BlockSpec((n, w), lambda s, place: (s, 0))
    fixed = lambda n, w: pl.BlockSpec((n, w), lambda s, place: (0, 0))
    return flow.call(
        first_back_kernel,
        "first_back",
        (seqs,),
        [place],
        [total, second, normed, inverse, gain, weight, picked, rows_c],
        [
            seq(slots, width),
            seq(slots, width),
            pl.BlockSpec((slots, width), lambda s, place: (s * per_seq, 0)),
            seq(slots, 128),
            whole_of(gain),
            whole_of(weight),
            seq(length, slots),
            seq(slots, width),
        ],
        [shape((rows, width), full), shape((rows, width), low), shape((8, width), full)]
        + [shape((half, 4 * half), low)] * 4,
        [seq(length, width), seq(length, width), fixed(8, width)]
        + [pl.BlockSpec((half, half), lambda s, place: (0, 3))] * 4,
        scratch=[pltpu.VMEM((width, width), full)],
        spaces="--------",
        out_spaces="h------",
        us=10,
    )


def project_kernel(tokens_ref, *refs, scale):
    weights, (bias_q, bias_v), outs = refs[:3], refs[3:5], refs[5:]
    tokens = tokens_ref[...]
    queries = (dot(tokens, weights[0][...]) + bias_q[...]).astype(low)
    outs[0][...] = (queries.astype(full) * scale).astype(low)
    outs[1][...] = dot(tokens, weights[1][...]).astype(low)
    outs[2][...] = (dot(tokens, weights[2][...]) + bias_v[...]).astype(low)


def project(flow, tokens, weights, biases, scale):
    rows, width = tokens.shape
    block = pl.BlockSpec((256, width), lambda i: (i, 0))
    return flow.call(
        functools.partial(project_kernel, scale=scale),
        "project",
        (rows // 256,),
        [],
        [tokens, *weights, *biases],
        [block] + [whole_of(v) for v in (*weights, *biases)],
        [shape((rows, width), low)] * 3,
        [block] * 3,
        spaces="-" * 6,
        out_spaces="hhh",
        us=8.5,
    )


def input_kernel(place, resid_ref, *refs, blocks):
    grads, weights, out_ref = refs[: len(blocks)], refs[len(blocks) : -1], refs[-1]
    total = resid_ref[...]
    for ref, (side, start, group) in zip(grads, blocks):
        for n in range(3):
            weight = weights[3 * side + n][:, start : start + group]
            total += dot(ref[:, n * group : (n + 1) * group], weight, 1, 1)
    out_ref[...] = total.astype(low)


def input_grad(flow, place, resid, parts, weights):
    rows, width = resid.shape
    half = width // 2
    block = pl.BlockSpec((256, width), lambda i, place: (i, 0))
    grads = [part[2] for part in parts]
    specs = [
        pl.BlockSpec((width, half), lambda i, place, side=side: (0, place[0] ^ side))
        for side in range(2)
        for n in range(3)
    ]
    return flow.call(
        functools.partial(
            input_kernel, blocks=[(side, start, g.shape[1] // 3) for side, start, g in parts]
        ),
        "input_grad",
        (rows // 256,),
        [place],
        [resid, *grads, *weights, *weights],
        [block]
        + [pl.BlockSpec((256, g.shape[1]), lambda i, place: (i, 0)) for g in grads]
        + specs,
        [shape((rows, width), low)],
        [block],
        spaces="h" * (1 + len(parts)) + "-" * 6,
        out_spaces="h",
        polled=False,
        us=12.3,
    )[0]


def gate_kernel(place, scores_ref, noise_ref, gate_ref, *parts):
    gate = jax.nn.sigmoid((scores_ref[...].astype(full) + noise_ref[...].astype(full)) / heat)
    gate_ref[...] = gate.astype(low)
    part = gate_ref.shape[1] // 4
    mine = pl.ds(pl.multiple_of(place[1] * part, part), part)
    for p, ref in enumerate(parts):

        @pl.when(pl.program_id(0) == p)
        def _(ref=ref):
            ref[...] = gate_ref[:, mine, :]


def gates(flow, place, scores, noise):
    heads, length, _ = scores.shape
    pairs, part = heads // 2, length // 4
    block = pl.BlockSpec((2, length, length), lambda i, place: (i, 0, 0))
    return flow.call(
        gate_kernel,
        "gates",
        (pairs,),
        [place],
        [scores, noise],
        [block, block],
        [shape(scores.shape, low)] + [shape((2, part, length), low)] * pairs,
        [block] + [pl.BlockSpec((2, part, length), lambda i, place: (0, 0, 0))] * pairs,
        spaces="hh",
        out_spaces="h" + "-" * pairs,
        us=5.5,
    )


def mask_kernel(place, scores_ref, noise_ref, mine_ref, got_ref, *refs):
    out_ref = refs[-1]
    half = mine_ref.shape[1]
    for side, ref in enumerate((mine_ref, got_ref)):
        core = place[2] ^ side
        rows = pl.ds(pl.multiple_of(core * half, half), half)
        gate = jax.nn.sigmoid(
            (scores_ref[:, rows, :].astype(full) + noise_ref[:, rows, :].astype(full)) / heat
        )
        out_ref[:, rows, :] = ref[...].astype(full) * (gate * (1.0 - gate) / heat)


def mask_grad(flow, place, scores, noise, mine, got, begin, earlier):
    heads, length, _ = scores.shape
    block = pl.BlockSpec((1, length, length), lambda i, place: (begin + i, 0, 0))
    half = pl.BlockSpec((1, length // 2, length), lambda i, place: (i, 0, 0))
    return flow.call(
        mask_kernel,
        "mask_grad",
        (mine.shape[0],),
        [place],
        [scores, noise, mine, got, *earlier],
        [block, block, half, half] + [pl.BlockSpec(memory_space=pl.ANY)] * len(earlier),
        [shape(scores.shape, full)],
        [block],
        aliases={5: 0} if earlier else {},
        spaces="hh--" + "h" * len(earlier),
        out_spaces="h",
        polled=False,
        us=mine.shape[0],
    )


def make_local(n_dp):
    bits = n_dp.bit_length() - 1

    def added(a, b):
        return (a.astype(full) + b.astype(full)).astype(low)

    def in_order(mine, other, bit, axis):
        return jnp.concatenate(
            [jnp.where(bit == 0, mine, other), jnp.where(bit == 0, other, mine)], axis
        )

    def local(
        tokens,
        masked_positions,
        cotangent,
        query_weight,
        query_bias,
        key_weight,
        value_weight,
        value_bias,
        output_weight,
        output_bias,
        first_gain,
        first_shift,
        up_weight,
        up_bias,
        down_weight,
        lowering_offset,
        second_gain,
        second_shift,
        channel_filter_scores,
        mask_noise,
    ):
        rows, width = tokens.shape
        seqs, slots = masked_positions.shape
        length = rows // seqs
        own_heads = channel_filter_scores.shape[0]
        depth = width // (2 * own_heads)
        scale = depth ** (-0.5)
        pairs = own_heads * depth // 128
        dp, tp = lax.axis_index("dp"), lax.axis_index("tp")
        bit = [(dp >> b) & 1 for b in range(bits)]
        quarter = 2 * bit[0] + bit[1]

        place = jnp.stack([tp, quarter, bit[0]]).astype(jnp.int32)

        def halves(a, axis, which):
            n = a.shape[axis] // 2
            return lax.dynamic_slice_in_dim(a, which * n, n, axis)

        def quarter_of(a, axis):
            n = a.shape[axis] // 4
            return lax.dynamic_slice_in_dim(a, quarter * n, n, axis)

        flow = Flow(n_dp)
        swap = flow.swap
        row = lambda v: v[None, :]
        projections = (query_weight, key_weight, value_weight)

        gate, *gate_parts = gates(flow, place, channel_filter_scores, mask_noise)
        far_gates = {}

        def gather_gate(p):
            near = gate_parts[p]
            got, due = swap(near, "tp")
            (near,) = yield [got], due, [near]
            (beside, due), (over, _) = swap(near, 1), swap(near, 0)
            beside, over = yield [beside, over], due, []
            corner, due = swap(beside, 0)
            (corner,) = yield [corner], due, []
            far_gates[p] = near, beside, over, corner

        far_weights = {}

        def gather_weight(n, mine):
            near, due = swap(mine, "tp")
            (near,) = yield [near], due + (4.0, 10.0)[n], [mine]
            (beside, due), (over, _) = swap(near, 1), swap(near, 0)
            extra = [lax.ppermute(up_bias, "tp", [(0, 1), (1, 0)])] if n == 0 else []
            beside, over, *extra = yield [beside, over, *extra], due, []
            if extra:
                far_weights["bias"] = extra[0]
            corner, due = swap(beside, 0)
            (corner,) = yield [corner], due, []
            far_weights[n] = near, beside, over, corner

        for p in range(pairs):
            flow.start(gather_gate(p))
        flow.start(gather_weight(0, quarter_of(up_weight, 1)))
        flow.start(gather_weight(1, quarter_of(down_weight, 0)))

        queries, keys, values = project(
            flow, tokens, projections, (query_bias, value_bias), scale
        )
        context, logsum = attend_own(flow, place, queries, keys, values, gate, length)
        earlier, logsums = [context], [[], logsum]
        for p in range(pairs):
            flow.wait(lambda: p in far_gates)
            context, part, far_gate = attend_far(
                flow, place, queries, keys, values, far_gates[p], p, pairs, earlier, length
            )
            logsums[0].append(part)
            earlier = [context, far_gate]

        order, picked, context_c, x, x_c, normed, inverse = first_norm(
            flow,
            masked_positions,
            context,
            tokens,
            output_weight,
            output_bias,
            first_gain,
            first_shift,
            length,
        )
        own_weights, own_bias = (up_weight, down_weight), row(up_bias)
        total, own_active, own_slope = forward(
            flow, place, x, own_weights, own_bias, None, length, slots
        )
        flow.wait(lambda: len(far_weights) == 3)
        bias_far = row(far_weights["bias"])
        far = [far_weights[n][r] for r in range(4) for n in range(2)]
        total, far_active, far_slope = forward(
            flow, place, x, far, bias_far, total, length, slots
        )
        vectors = [lowering_offset, first_gain, first_shift, second_gain, second_shift]
        layer_output, grad_second, grad_forward, sums_second = second_norm(
            flow, total, normed, cotangent, order, picked, vectors
        )

        def first_half(a, axis):
            return lax.slice_in_dim(a, 0, a.shape[axis] // 2, axis=axis)

        def last_half(a, axis):
            return lax.slice_in_dim(a, a.shape[axis] // 2, a.shape[axis], axis=axis)

        done = flow.done
        first_ways = tuple(range(1, bits))

        def split(a, way, axis, relative_axis):
            if way == 1 and relative_axis is not None:
                return first_half(a, relative_axis), last_half(a, relative_axis)
            return halves(a, axis, bit[way]), halves(a, axis, 1 - bit[way])

        def summed(mine, ways, axis, relative_axis):
            for way in ways:
                keep, send = split(mine, way, axis, relative_axis)
                got, due = swap(send, way)
                (got,) = yield [got], due, [send]
                mine = added(keep, got)
            return mine

        def core_sum(keep, send):
            got, due = swap(send, 0)
            (got,) = yield [got], due, [send]
            return keep, got

        def reduce_far(parts, keep, send):
            keep, got = yield from core_sum(keep, send)
            for name, pick, axis, relative_axis, before in parts:
                piece = added(pick(keep), pick(got))
                flow.start(send_far(name, piece, axis, relative_axis, before))

        def send_far(name, mine, axis, relative_axis, before):
            mine = yield from summed(mine, before, axis, relative_axis)
            got, due = swap(mine, "tp")
            (got,) = yield [got], due, [mine]
            done[name] = got

        def reduce_own(parts, keep, send):
            keep, got = yield from core_sum(keep, send)
            for name, pick, axis, relative_axis, before in parts:
                piece = added(pick(keep), pick(got))
                flow.start(rest_own(name, piece, axis, relative_axis, before))

        def rest_own(name, mine, axis, relative_axis, before):
            mine = yield from summed(mine, before, axis, relative_axis)
            (mine,) = yield [mine], name, []
            mine = added(mine, done[name])
            after = tuple(way for way in first_ways if way not in before)
            mine = yield from summed(mine, after[:-1], axis, relative_axis)
            got, due = swap(mine, after[-1])
            (got,) = yield [got], due, [mine]
            mine = added(mine, got)
            for way in reversed(before + after[:-1]):
                got, due = swap(mine, way)
                (got,) = yield [got], due, [mine]
                along = relative_axis if way == 1 and relative_axis is not None else axis
                mine = in_order(mine, got, bit[way], along)
            got, due = swap(mine, 0)
            (got,) = yield [got], due, [mine]
            done[name + " whole"] = (mine, got)

        def spread(name, axis):
            return in_order(*done[name + " whole"], bit[0], axis).astype(full)

        def whole(a):
            return a

        def add_vectors(name, mine):
            for way in ("tp",) + tuple(range(bits)):
                got, due = swap(mine, way)
                (got,) = yield [got], due + 5.0, [mine]
                mine = mine + got
            done[name] = mine

        def both(mine, theirs):
            return in_order(mine, theirs, tp, 0)

        def hidden_half(sums):
            return in_order(*jnp.split(sums[0], 2), bit[0], 0)

        parts_down = [("down", whole, 0, None, orders["down"])]
        parts_up = [("up", whole, 0, None, orders["up"])]
        parts_qkv = [("qkv", whole, 0, None, orders["qkv"])]
        mask_pairs = [(0, pairs - 1), (pairs - 1, 1)]
        parts_mask = [
            ("mask" + str(n), whole, 2, 1, orders["mask" + str(n)]) for n in range(len(mask_pairs))
        ]

        back, down_send, down_keep, up_send, up_keep, far_sums = backward(
            flow, place, grad_forward, x_c, far, far_active, far_slope, None
        )
        flow.start(reduce_far(parts_down, down_keep, down_send))
        flow.start(reduce_far(parts_up, up_keep, up_send))
        back, down_send, down_keep, up_send, up_keep, own_sums = backward(
            flow, place, grad_forward, x_c, own_weights, own_active, own_slope, back
        )
        flow.start(reduce_own(parts_down, down_keep, down_send))
        flow.start(reduce_own(parts_up, up_keep, up_send))

        resid, grad_context, sums_first, own_keep, own_send, far_keep, far_send = first_back(
            flow,
            place,
            back,
            grad_second,
            normed,
            inverse,
            first_gain,
            output_weight,
            picked,
            context_c,
            length,
        )
        early = [both(hidden_half(own_sums), hidden_half(far_sums))]
        early += [sums_first[i] for i in range(3)] + [sums_second[i] for i in range(3)]
        def back_part(side, gate, p, masks, at, held, weights):
            logsum = logsums[0][p] if side else logsums[1]
            return attend_back(
                flow, place, queries, keys, values, grad_context, logsum, tokens, gate, side,
                length, scale, p, masks, at, held, weights,
            )

        sums_parts, grads = [[], []], []
        for side in (1, 0):
            begin = (reduce_own, reduce_far)[side]
            weights = ((own_keep, own_send), (far_keep, far_send))[side]
            masks = ()
            for p in range(pairs):
                first, many = [part for part in mask_pairs if part[0] <= p < sum(part)][0]
                grad, *masks, w_keep, w_send, part = back_part(
                    side, (gate, far_gate)[side], p, masks, p - first, 2 * many, weights
                )
                weights = (w_keep, w_send)
                grads.append((side, p * 128, grad))
                sums_parts[side].append(part)
                if p == first + many - 1:
                    number = mask_pairs.index((first, many))
                    flow.start(begin(parts_mask[number : number + 1], *masks))
                    masks = ()
            flow.start(begin(parts_qkv, *weights))
        sums_own, sums_far = (jnp.concatenate(part, 1) for part in sums_parts)
        vectors = early + [both(sums_own[i], sums_far[i]) for i in range(2)]
        flow.start(add_vectors("vectors", jnp.concatenate(vectors).reshape(-1, 128)))
        results = {}

        def tokens_part():
            results["tokens"] = input_grad(flow, place, resid, grads, projections)

        flow.fillers.append((7.0, tokens_part))
        masks = []

        def mask_part(p, mine, got):
            for name, axis in (("down", 0), ("up", 1)):
                if name + " whole" in done and name not in results:
                    results[name] = spread(name, axis)
                    flow.sends.append(results[name])
            masks[:] = mask_grad(
                flow, place, channel_filter_scores, mask_noise, mine, got, 2 * mask_pairs[p][0],
                list(masks),
            )

        def watch():
            for p, (name, *_) in enumerate(parts_mask):
                pair = done.pop(name + " whole", None)
                if pair is not None:
                    flow.fillers.insert(0, (4.0, functools.partial(mask_part, p, *pair)))
            return not flow.tasks

        flow.wait(watch)
        for _, filler in flow.fillers:
            filler()
        for name, axis in (("down", 0), ("up", 1)):
            if name not in results:
                results[name] = spread(name, axis)
        down_grad, up_grad, qkv_grad = results["down"], results["up"], spread("qkv", 0)
        hidden_all = 2 * up_weight.shape[1]
        vectors = done["vectors"].reshape(-1)
        up_bias_grad = halves(vectors[:hidden_all], 0, tp)
        vectors = halves(vectors[hidden_all:].reshape(-1, width), 1, tp)
        fg, fs, ob, sg, ss, db, query_bias_grad, value_bias_grad = [vectors[i] for i in range(8)]

        group = own_heads * depth
        output_grad = qkv_grad[:, 3 * group :]
        by_pair = [jnp.split(part, 3, 1) for part in jnp.split(qkv_grad[:, : 3 * group], pairs, 1)]
        qkv_grads = [jnp.concatenate([part[n] for part in by_pair], 1) for n in range(3)]
        return (
            layer_output,
            results["tokens"],
            qkv_grads[0],
            query_bias_grad,
            qkv_grads[1],
            qkv_grads[2],
            value_bias_grad,
            output_grad,
            ob,
            fg,
            fs,
            up_grad,
            up_bias_grad,
            down_grad,
            db,
            sg,
            ss,
            masks[0],
        )

    return local


def solution(mesh):
    in_specs = (
        P(("dp", "tp"), None),
        P(("dp", "tp"), None),
        P(("dp", "tp"), None),
        P(),
        P(),
        P(),
        P(),
        P(),
        P(),
        P(),
        P(),
        P(),
        P(None, "tp"),
        P("tp"),
        P("tp", None),
        P(),
        P(),
        P(),
        P("tp", None, None),
        P("tp", None, None),
    )
    out_specs = (
        P(("dp", "tp"), None),
        P(("dp", "tp"), None),
        P(None, "tp"),
        P("tp"),
        P(None, "tp"),
        P(None, "tp"),
        P("tp"),
        P(None, "tp"),
        P("tp"),
        P("tp"),
        P("tp"),
        P(None, "tp"),
        P("tp"),
        P("tp", None),
        P("tp"),
        P("tp"),
        P("tp"),
        P("tp", None, None),
    )
    local = make_local(mesh.shape["dp"])
    return jax.shard_map(local, mesh=mesh, in_specs=in_specs, out_specs=out_specs, check_vma=False)
```
